128 devices in a mesh: depth: 16 (over z, x_hi, core), res: 8 (over x_lo, y).
Axes of the slice: x: 4 (x_hi: 2, x_lo: 2; x = x_hi * 2 + x_lo), y: 4, z: 4, core: 2. Of those that a mesh axis runs over, the one named last changes fastest.
Arguments:
- alignment_state: bfloat16 [256, 256, 64], P('depth', 'res'), may hold values from -8 to 8
- pairwise_state: bfloat16 [256, 256, 128], P('res', 'depth'), may hold values from -6 to 6
- alignment_mask: int32 [256, 256], P('depth', 'res'), may hold values 0 or 1
- residue_entry_mask: int32 [256], P('res'), may hold values 0 or 1
- sequence_live_count: int32 [16], P('depth'), may hold values from 5 to 16, as said below
- horizontal_intake_coefs: bfloat16 [64, 256], replicated, may hold values from -0.75 to 0.75
- pairwise_bias_weights: bfloat16 [128, 8], replicated, may hold values from -0.5 to 0.5
- horizontal_readout_coefs: bfloat16 [64, 64], replicated, may hold values from -0.75 to 0.75
- column_input_weights: bfloat16 [64, 144], replicated, may hold values from -0.75 to 0.75
- vertical_readout_coefs: bfloat16 [64, 64], replicated, may hold values from -0.75 to 0.75
- tensor_factor_coefs: bfloat16 [64, 64], replicated, may hold values from -0.75 to 0.75
- outer_output_weights: bfloat16 [1024, 128], replicated, may hold values from -0.1875 to 0.1875
- adjoint_of_result_track: bfloat16 [256, 256, 64], P('depth', 'res'), may hold values from -6 to 6
- pairwise_cotangent: bfloat16 [256, 256, 128], P('res', 'depth'), may hold values from -3 to 3
Outputs:
- alignment_gradient: float32 [256, 256, 64], P('depth', 'res')
- pair_grad: float32 [256, 256, 128], P('res', 'depth')
The draws below stay inside these ranges and needn't reach their ends.
Inputs may be any that keep to these rules, and one draw needn't show every extreme that they name: `sequence_live_count`: the last block holds 16 live sequences.
All inputs are finite; a program needn't handle non-finite values. No bound on the sum of `alignment_mask` or of `residue_entry_mask` on one device may be relied on, other than what follows from the above.
Results may differ from the reference program's by a relative error of at most 0.0015.
Values may be sent and summed in bfloat16 or wider, within the bound.
No kernel may reach another device: no remote copies, remote signals or barrier semaphores. Data moves between devices by JAX's collectives and lax.ppermute only.
A program may use at most 448 MiB of HBM per device.

```python
import jax
import jax.numpy as jnp
from jax import lax

FEATURE_DEPTH = 64
CZ = 128
ATTN_LANES = 8
ATTN_FEATURES = 8
FACTOR_BREADTH = 32
DEPTH_SHARE = 16
ADDED_ALIGNED = 256
WINDOW_LENGTH = 256
DSH = 16


def draw_alignment_state(key, part):
    key = jax.random.fold_in(key, 11)
    perturbation_seed = jax.random.fold_in(key, 0)
    payload_lanes = jax.random.normal(perturbation_seed, (ADDED_ALIGNED, WINDOW_LENGTH, FEATURE_DEPTH), dtype=jnp.float32)
    return jnp.clip(payload_lanes, -6.0, 6.0).astype(jnp.bfloat16)


def draw_column_input_weights(key, part):
    key = jax.random.fold_in(key, 13)
    breadth_extent = 2 * ATTN_LANES * ATTN_FEATURES + 2 * ATTN_FEATURES
    magnitude_factor = FEATURE_DEPTH ** (-0.5)
    payload_lanes = magnitude_factor * jax.random.normal(key, (FEATURE_DEPTH, breadth_extent), dtype=jnp.float32)
    return jnp.clip(payload_lanes, -0.75, 0.75).astype(jnp.bfloat16)


def draw_sequence_live_count(key, part):
    key = jax.random.fold_in(key, 7)
    shard_index = jnp.arange(DSH, dtype=jnp.int32)
    floor_value = DEPTH_SHARE // 3
    spread = DEPTH_SHARE - floor_value
    rising = floor_value + shard_index * spread // max(DSH - 1, 1)
    jitter = jax.random.randint(key, (DSH,), 0, max(DEPTH_SHARE // 8, 1) + 1, dtype=jnp.int32)
    counts = jnp.minimum(rising + jitter * (shard_index > 0), DEPTH_SHARE)
    counts = jnp.where(shard_index == DSH - 1, DEPTH_SHARE, counts)
    return counts.astype(jnp.int32)


def touch_ends(values, key, least, top_value):
    dims = values.shape
    place = [jax.random.randint(jax.random.fold_in(key, axis), (), 0, dims[axis]) for axis in range(len(dims))]
    values = values.at[tuple(place)].set(least)
    longest = dims.index(max(dims))
    place[longest] = (place[longest] + 1) % dims[longest]
    return values.at[tuple(place)].set(top_value)


def block_levels(stream_key, shape, cuts, low, top_value):
    loudness, own = 1.0, jax.random.fold_in(stream_key, 6)
    for dim, blocks in cuts:
        steps = jnp.exp(jax.random.uniform(jax.random.fold_in(own, dim), (blocks,), jnp.float32, low / len(cuts), top_value / len(cuts)))
        loudness = loudness * jnp.repeat(steps, shape[dim] // blocks).reshape([-1 if axis == dim else 1 for axis in range(len(shape))])
    return loudness


def normal_values(key, dims, scale, reach, cuts=(), kind=jnp.bfloat16):
    drawn = jax.random.normal(key, dims, jnp.float32) * scale
    if len(cuts) > 0:
        drawn = block_levels(key, dims, cuts, -0.22, 0.18) * drawn
    return jnp.clip(drawn, min=-reach, max=reach).astype(kind)


def setup_inputs(seed: int = 0) -> dict:
    streams_of = jax.random.split(jax.random.key(seed), 15)
    return {
        "alignment_state": draw_alignment_state(jax.random.fold_in(streams_of[14], 71), 0),
        "pairwise_state": normal_values(streams_of[1], (WINDOW_LENGTH, WINDOW_LENGTH, CZ), 1.0, 6.0, ((0, 8), (1, 16))),
        "alignment_mask": touch_ends((jax.random.randint(streams_of[2], (ADDED_ALIGNED, WINDOW_LENGTH), 0, 4) < 3).astype(jnp.int32), jax.random.fold_in(streams_of[2], 1), 0, 1),
        "residue_entry_mask": touch_ends((jax.random.randint(streams_of[3], (WINDOW_LENGTH,), 0, 8) < 7).astype(jnp.int32), jax.random.fold_in(streams_of[3], 1), 0, 1),
        "sequence_live_count": draw_sequence_live_count(jax.random.fold_in(streams_of[14], 71), 0),
        "horizontal_intake_coefs": normal_values(streams_of[5], (FEATURE_DEPTH, 4 * ATTN_LANES * ATTN_FEATURES), FEATURE_DEPTH ** -0.5, 0.75),
        "pairwise_bias_weights": normal_values(streams_of[6], (CZ, ATTN_LANES), CZ ** -0.5, 0.5),
        "horizontal_readout_coefs": normal_values(streams_of[7], (ATTN_LANES * ATTN_FEATURES, FEATURE_DEPTH), (ATTN_LANES * ATTN_FEATURES) ** -0.5, 0.75),
        "column_input_weights": draw_column_input_weights(jax.random.fold_in(streams_of[14], 71), 0),
        "vertical_readout_coefs": normal_values(streams_of[9], (ATTN_LANES * ATTN_FEATURES, FEATURE_DEPTH), (ATTN_LANES * ATTN_FEATURES) ** -0.5, 0.75),
        "tensor_factor_coefs": normal_values(streams_of[10], (FEATURE_DEPTH, 2 * FACTOR_BREADTH), FEATURE_DEPTH ** -0.5, 0.75),
        "outer_output_weights": normal_values(streams_of[11], (FACTOR_BREADTH * FACTOR_BREADTH, CZ), (FACTOR_BREADTH * FACTOR_BREADTH) ** -0.5, 0.1875),
        "adjoint_of_result_track": normal_values(streams_of[12], (ADDED_ALIGNED, WINDOW_LENGTH, FEATURE_DEPTH), 1.0, 6.0, ((0, 16), (1, 8))),
        "pairwise_cotangent": normal_values(streams_of[13], (WINDOW_LENGTH, WINDOW_LENGTH, CZ), 0.5, 3.0, ((0, 8), (1, 16))),
    }


highest_precision = lax.Precision.HIGHEST

def layer_normalize(payload_lanes):
    center = payload_lanes - lax.optimization_barrier(jnp.mean(payload_lanes, -1, keepdims=True))
    spread = lax.optimization_barrier(jnp.mean(center * center, -1, keepdims=True))
    return center * lax.rsqrt(spread + 1e-05)

def complete_mask(alignment_mask, residue_entry_mask, sequence_live_count):
    seq_index = jnp.arange(ADDED_ALIGNED, dtype=jnp.int32)
    shard_count = sequence_live_count[seq_index // DEPTH_SHARE]
    sequence_active = (seq_index % DEPTH_SHARE < shard_count).astype(jnp.float32)
    return alignment_mask.astype(jnp.float32) * residue_entry_mask.astype(jnp.float32)[None, :] * sequence_active[:, None]

def pair_bias(pairwise_single, pairwise_bias_weights):
    return jnp.einsum('ijc,ch->ijh', layer_normalize(pairwise_single), pairwise_bias_weights.astype(jnp.float32), precision=highest_precision)

def attend(queries, gating, key_value, bias_complete, key_entry_mask):
    sequence_row_group, row_len = (queries.shape[0], queries.shape[1])
    col_len = key_value.shape[1]
    head_number = bias_complete.shape[2]
    inner_channel_width = queries.shape[2]
    head_dim = inner_channel_width // head_number
    query_heads = queries.reshape(sequence_row_group, row_len, head_number, head_dim)
    key_rows = key_value[..., :inner_channel_width].reshape(sequence_row_group, col_len, head_number, head_dim)
    value_rows = key_value[..., inner_channel_width:].reshape(sequence_row_group, col_len, head_number, head_dim)
    logits = jnp.einsum('sihd,sjhd->shij', query_heads, key_rows, precision=highest_precision) * head_dim ** (-0.5)
    logits = logits + jnp.transpose(bias_complete, (2, 0, 1))[None]
    logits = jnp.where(key_entry_mask[:, None, None, :] > 0, logits, -1000000000.0)
    weights = jax.nn.softmax(logits, axis=-1)
    attended_output = jnp.einsum('shij,sjhd->sihd', weights, value_rows, precision=highest_precision)
    return jax.nn.sigmoid(gating) * attended_output.reshape(sequence_row_group, row_len, inner_channel_width)

def row_block(block_rows, bias_complete, block_mask, horizontal_intake_coefs, horizontal_readout_coefs):
    inner_channel_width = horizontal_readout_coefs.shape[0]
    normalized_input = layer_normalize(block_rows)
    projected_input = jnp.einsum('nze,eb->nzb', normalized_input, horizontal_intake_coefs.astype(jnp.float32), precision=highest_precision)
    attended_output = attend(projected_input[..., :inner_channel_width], projected_input[..., 3 * inner_channel_width:], projected_input[..., inner_channel_width:3 * inner_channel_width], bias_complete, block_mask)
    return block_rows + jnp.einsum('iwu,ux->iwx', attended_output, horizontal_readout_coefs.astype(jnp.float32), precision=highest_precision)

def row_delta(solo_aligned_track, bias_complete, active_mask, horizontal_intake_coefs, horizontal_readout_coefs):
    partition_sets = solo_aligned_track.reshape(ADDED_ALIGNED // DEPTH_SHARE, DEPTH_SHARE, WINDOW_LENGTH, FEATURE_DEPTH)
    mask_blocks = active_mask.reshape(ADDED_ALIGNED // DEPTH_SHARE, DEPTH_SHARE, WINDOW_LENGTH)

    def one_block(pieces):
        return row_block(pieces[0], bias_complete, pieces[1], horizontal_intake_coefs, horizontal_readout_coefs)
    returned_tuple = lax.map(jax.checkpoint(one_block), (partition_sets, mask_blocks))
    return returned_tuple.reshape(ADDED_ALIGNED, WINDOW_LENGTH, FEATURE_DEPTH)

def column_delta(alignment_after_rows, active_mask, column_input_weights, vertical_readout_coefs):
    inner_channel_width = vertical_readout_coefs.shape[0]
    head_number = ATTN_LANES
    head_dim = inner_channel_width // head_number
    column_weight_matrix = column_input_weights.astype(jnp.float32)
    normalized_input = layer_normalize(alignment_after_rows)
    query_grand_total = jnp.einsum('yo,yob->ob', active_mask, normalized_input, precision=highest_precision)
    sequence_grand_total = lax.optimization_barrier(jnp.sum(active_mask, 0))
    query_mean = query_grand_total / jnp.maximum(sequence_grand_total, 1.0)[:, None]
    col_query = (jnp.dot(query_mean, column_weight_matrix[:, :inner_channel_width], precision=highest_precision) * head_dim ** (-0.5)).reshape(-1, head_number, head_dim)
    col_proj = jnp.einsum('sic,cf->sif', normalized_input, column_weight_matrix[:, inner_channel_width:], precision=highest_precision)
    col_key = col_proj[..., :head_dim]
    col_value = col_proj[..., head_dim:2 * head_dim]
    col_gate = col_proj[..., 2 * head_dim:]
    logits = jnp.einsum('ihd,sid->sih', col_query, col_key, precision=highest_precision)
    logits = jnp.where(active_mask[..., None] > 0, logits, -1000000000.0)
    weights = jax.nn.softmax(logits, axis=0)
    attended_output = jnp.einsum('sih,sid->ihd', weights, col_value, precision=highest_precision)
    mixed_heads = (jax.nn.sigmoid(col_gate).reshape(ADDED_ALIGNED, WINDOW_LENGTH, head_number, head_dim) * attended_output[None]).reshape(ADDED_ALIGNED, WINDOW_LENGTH, inner_channel_width)
    return alignment_after_rows + jnp.einsum('dvn,na->dva', mixed_heads, vertical_readout_coefs.astype(jnp.float32), precision=highest_precision)

def outer_product_inputs(alignment_after_columns, active_mask, tensor_factor_coefs):
    projected_input = jnp.einsum('nze,eb->nzb', layer_normalize(alignment_after_columns), tensor_factor_coefs.astype(jnp.float32), precision=highest_precision)
    left_proj = active_mask[..., None] * projected_input[..., :FACTOR_BREADTH]
    right_proj = active_mask[..., None] * projected_input[..., FACTOR_BREADTH:]
    return (left_proj, right_proj)

def reference(alignment_state, pairwise_state, alignment_mask, residue_entry_mask, sequence_live_count, horizontal_intake_coefs, pairwise_bias_weights, horizontal_readout_coefs, column_input_weights, vertical_readout_coefs, tensor_factor_coefs, outer_output_weights, adjoint_of_result_track, pairwise_cotangent):
    active_mask = complete_mask(alignment_mask, residue_entry_mask, sequence_live_count)

    def forward_pass(solo_aligned_track, pairwise_single):
        bias_complete = pair_bias(pairwise_single, pairwise_bias_weights)
        alignment_after_rows = row_delta(solo_aligned_track, bias_complete, active_mask, horizontal_intake_coefs, horizontal_readout_coefs)
        return column_delta(alignment_after_rows, active_mask, column_input_weights, vertical_readout_coefs)
    alignment_after_columns, backprop_primary = jax.vjp(forward_pass, alignment_state.astype(jnp.float32), pairwise_state.astype(jnp.float32))
    outer_factors, backprop_outer_product = jax.vjp(lambda payload_lanes: outer_product_inputs(payload_lanes, active_mask, tensor_factor_coefs), alignment_after_columns)
    left_proj, right_proj = outer_factors
    pair_norm = jnp.einsum('si,sj->ij', active_mask, active_mask, precision=highest_precision)
    inverse = 1.0 / jnp.maximum(pair_norm, 1.0)
    pairwise_single_cotangent = pairwise_cotangent.astype(jnp.float32)
    pair_back = jnp.einsum('ijk,fk->ijf', pairwise_single_cotangent, outer_output_weights.astype(jnp.float32), precision=highest_precision)
    pair_back = (pair_back * inverse[..., None]).reshape(WINDOW_LENGTH, WINDOW_LENGTH, FACTOR_BREADTH, FACTOR_BREADTH)
    left_grad = jnp.einsum('ijab,sjb->sia', pair_back, right_proj, precision=highest_precision)
    right_grad = jnp.einsum('ijab,sia->sjb', pair_back, left_proj, precision=highest_precision)
    second_gradient, = backprop_outer_product((left_grad, right_grad))
    second_gradient = second_gradient + adjoint_of_result_track.astype(jnp.float32)
    alignment_gradient, pairwise_portion = backprop_primary(second_gradient)
    return (alignment_gradient, pairwise_portion + pairwise_single_cotangent)
```

```python
import jax
import jax.numpy as jnp
from jax import lax
from jax.experimental import pallas as pl
from jax.experimental.pallas import tpu as pltpu
from jax.sharding import PartitionSpec as P

f32 = jnp.float32
bf16 = jnp.bfloat16
EPS = 1e-05
NEG = -1000000000.0
SCALE = 8 ** (-0.5)
NN = (((1,), (0,)), ((), ()))
NT = (((1,), (1,)), ((), ()))
TN = (((0,), (0,)), ((), ()))
VMEM = pltpu.CompilerParams(vmem_limit_bytes=50 * 1024 * 1024)


def mm(a, b, dims=NN):
    return lax.dot_general(a, b, dims, preferred_element_type=f32)


def split(x):
    hi = x.astype(bf16)
    lo = (x - hi.astype(f32)).astype(bf16)
    return hi, lo


def split3(x):
    hi = x.astype(bf16)
    rest = x - hi.astype(f32)
    mid = rest.astype(bf16)
    lo = (rest - mid.astype(f32)).astype(bf16)
    return hi, mid, lo


def cat(parts, axis):
    return jnp.concatenate(parts, axis=axis)


def mm2(x, w, dims=NN):
    hi, lo = split(x)
    return mm(hi, w, dims) + mm(lo, w, dims)


def mm3(x, w):
    hi, mid, lo = split3(x)
    return mm(hi, w) + mm(mid, w) + mm(lo, w)


def norm_rows(x):
    center = x - jnp.mean(x, -1, keepdims=True)
    rstd = lax.rsqrt(jnp.mean(center * center, -1, keepdims=True) + EPS)
    return center * rstd, rstd


def norm_back(normed, rstd, grad):
    return rstd * (
        grad
        - jnp.mean(grad, -1, keepdims=True)
        - normed * jnp.mean(grad * normed, -1, keepdims=True)
    )


def pair2(x):
    hi, lo = split(x)
    return cat([hi, lo], 1)


def head_mask(rows, cols, row_div, col_div):
    a = lax.broadcasted_iota(jnp.int32, (rows, cols), 0) // row_div
    b = lax.broadcasted_iota(jnp.int32, (rows, cols), 1) // col_div
    return (a == b).astype(f32)


def bias_kernel(pair_ref, wb_ref, out_ref, scr):
    xn, _ = norm_rows(pair_ref[...].astype(f32).reshape(512, 128))
    scr[...] = xn.reshape(32, 16, 128)
    wbt = wb_ref[...].astype(f32).T
    w2 = cat([wbt, wbt], 1).astype(bf16)
    own = head_mask(8, 256, 1, 32)
    rows = []
    for j in range(16):
        x2 = pair2(scr[:, j, :])
        tiled = cat([x2] * 8, 0)
        full = mm(w2, tiled, NT)
        rows.append(jnp.sum(full * own, 0, keepdims=True))
    block = cat(rows, 0)
    for k in range(16):
        out_ref[k] = block


def row_fwd_kernel(
    g_ref, own_ref, bias_ref, win_ref, wo_ref,
    p_ref, o_ref, x2_ref, x2o_ref, m1_ref, any_ref, c1_ref,
    wqg, wvt2, wkk, wo2,
):
    s = pl.program_id(0)

    @pl.when(s == 0)
    def _():
        w = win_ref[...].astype(f32)
        wt = w.T
        qg = cat([wt[0:64], wt[192:256]], 0)
        wqg[...] = cat([qg, qg], 1).astype(bf16)
        wvt = wt[128:192]
        wvt2[...] = cat([wvt, wvt], 1).astype(bf16)
        wk = w[:, 64:128]
        row = cat([wk, wk], 1)
        wkk[...] = cat([row, row], 0).astype(bf16)
        wo = wo_ref[...].astype(f32)
        wo2[...] = cat([wo, wo], 0).astype(bf16)

    g = g_ref[...].reshape(256, 128).astype(f32)
    live = g[:, 64:65]
    xn, _ = norm_rows(g[:, :64])
    x2 = pair2(xn)
    x2_ref[0] = x2
    kk = mm(x2, wkk[...])
    khi = kk.astype(bf16)
    lane = lax.broadcasted_iota(jnp.int32, (256, 128), 1)
    k2 = jnp.where(lane < 64, kk, kk - khi.astype(f32)).astype(bf16)
    vt = mm(wvt2[...], x2, NT)

    own = own_ref[0].astype(f32)
    xo = own[:, :64]
    xon, _ = norm_rows(xo)
    x2o = pair2(xon)
    x2o_ref[0] = x2o
    qg = mm(wqg[...], cat([x2o] * 8, 0), NT)
    heads = head_mask(64, 256, 8, 32)
    q = qg[:64] * (heads * SCALE)
    gate = jax.nn.sigmoid(qg[64:])
    qhi, qlo = split(q)
    logits = mm(k2, cat([qhi, qhi], 0)) + mm(khi[:, :64], qlo)
    logits = logits + bias_ref[...].reshape(256, 256)
    logits = jnp.where(live > 0, logits, NEG)
    e = jnp.exp(logits - jnp.max(logits, 0, keepdims=True))
    p = e * (1.0 / jnp.sum(e, 0, keepdims=True))
    p_ref[0] = p
    any_ref[0] = jnp.broadcast_to(jnp.max(live, 0, keepdims=True), (8, 256))
    phi, plo = split(p)
    vhi, vlo = split(vt)
    first = mm(cat([vhi, vlo], 0), phi)
    o = (first[:64] + first[64:] + mm(vhi, plo)) * heads
    o_ref[0] = o
    ahi, alo = split(o * gate)
    y = mm(cat([ahi, alo], 0), wo2[...], TN)
    m1 = xo + jnp.sum(y.reshape(8, 32, 64), 0)
    m1_ref[0] = m1
    c1_ref[:, 0, s, :] = cat([m1[:16], m1[16:]], 1)
    lv = own[:, 64:]
    c1_ref[:, 1, s, :] = cat([lv[:16], lv[16:]], 1)


def diag2(w):
    z = jnp.zeros_like(w)
    return cat([cat([w, z], 1), cat([z, w], 1)], 0)


def col_kernel(c1_ref, cw_ref, out_ref):
    x = c1_ref[:, 0].reshape(256, 128)
    live = c1_ref[:, 1].reshape(256, 128)
    halves = (head_mask(128, 128, 64, 64) * (1.0 / 64)).astype(bf16)
    center = x - mm3(x, halves)
    xn = center * lax.rsqrt(mm3(center * center, halves) + EPS)
    cw = cw_ref[...].astype(f32)
    wq = diag2(cw[:, 0:64]).astype(bf16)
    wk = diag2(cw[:, 64:128]).astype(bf16)
    wv = diag2(cw[:, 128:192]).astype(bf16)
    total = jnp.sum(live * xn, 0, keepdims=True)
    count = jnp.sum(live, 0, keepdims=True)
    mean = total / jnp.maximum(count, 1.0)
    colq = mm3(jnp.broadcast_to(mean, (8, 128)), wq)[0:1] * SCALE
    kt = mm2(xn, wk)
    vt = mm2(xn, wv)
    groups = head_mask(128, 128, 8, 8).astype(bf16)
    logits = jnp.where(live > 0, mm3(kt * colq, groups), NEG)
    peak = jnp.max(logits, 0, keepdims=True)
    e = jnp.exp(logits - peak)
    den = jnp.sum(e, 0, keepdims=True)
    w = e / den
    wv_ = w * vt
    attended = jnp.sum(wv_, 0, keepdims=True)
    khi, klo = split(kt)

    def by_key(z):
        zhi, zlo = split(z)
        full = mm(khi, zhi, TN) + mm(klo, zhi, TN) + mm(khi, zlo, TN)
        lane = lax.broadcasted_iota(jnp.int32, (8, 128), 1)
        return jnp.where(lane < 64, full[0:8], full[64:72])

    lt = live.T
    rows = [
        by_key(wv_), by_key(w), attended, peak, den, colq, count, count, count, count,
        lt[0:1, :128], lt[0:1, 128:], lt[64:65, :128], lt[64:65, 128:],
        count, count, count, count,
    ]
    block = cat(rows, 0)
    for k in range(16):
        out_ref[k] = block


def unpair(x):
    return cat([x[:, 0:64], x[:, 64:128]], 0)


def spread(v):
    return jnp.broadcast_to(v[None], (16, 32, 64)).reshape(512, 64)


def factor_kernel(m1_ref, c2_ref, own_ref, cw_ref, wv_ref, wt_ref, m2_ref, d_ref):
    m1 = m1_ref[...].reshape(512, 64)
    live = own_ref[...].reshape(512, 128)[:, 64:].astype(f32)
    attended = unpair(c2_ref[:, 16, :])
    xn, _ = norm_rows(m1)
    gate = jax.nn.sigmoid(mm2(xn, cw_ref[:, 192:256]))
    m2 = m1 + mm2(gate * spread(attended), wv_ref[...])
    m2_ref[...] = m2.reshape(16, 32, 64)
    xn2, _ = norm_rows(m2)
    lr = live * mm2(xn2, wt_ref[...])
    lt = cat(
        [cat([c2_ref[:, 24, :], c2_ref[:, 25, :]], 1), cat([c2_ref[:, 26, :], c2_ref[:, 27, :]], 1)],
        0,
    )
    pad = jnp.zeros((12, 32, 64), f32)
    planes = [lt[None, :, 64 * k:64 * k + 64] for k in range(4)]
    right = cat(planes + [pad], 0).reshape(512, 64)
    block = cat([lr, right], 1).astype(bf16).reshape(16, 32, 128)
    for k in range(8):
        d_ref[k] = block


def outer_kernel(
    da_ref, own_ref, cta_ref, ctb_ref, w_ref, m2_ref, c2_ref, m1_ref, adj_ref, cw_ref, wv_ref,
    wt_ref, g2_ref, dcg_ref, e1_ref,
    inv, turned, stage, res, lrs,
):
    step = pl.program_id(0)
    steps = 8
    per = 4

    @pl.when(step == 0)
    def _():
        norm = jnp.zeros((256, 32), f32)
        for k in range(4):
            allk = da_ref[:, k, :, 64:].reshape(256, 64)
            ownk = own_ref[0, k, :, 64:]
            norm = norm + mm(allk, ownk, NT)
        value = 1.0 / jnp.maximum(norm, 1.0)
        for k in range(32):
            inv[k] = jnp.broadcast_to(value[:, k:k + 1], (256, 128))
        for s in range(16):
            piece = da_ref[:, s].reshape(256, 128).astype(f32).T
            for half in range(2):
                cols = piece[:, 128 * half:128 * half + 128]
                lrs[half, pl.ds(s, 32, stride=16), :] = cols[0:32]
                lrs[half, pl.ds(512 + s, 32, stride=16), :] = cols[32:64]
        for half in range(2):
            turned[0, :, 128 * half:128 * half + 128] = lrs[half, 512:1024].astype(bf16)
            turned[1, :, 128 * half:128 * half + 128] = lrs[half, 0:512].astype(bf16)

    for side in range(2):
        for k in range(per):
            one = step * per + k
            if side == 0:
                ct = cta_ref[:, 0, k].reshape(256, 128)
            else:
                ct = ctb_ref[:, 0, 0, k].reshape(256, 128)
            hi, lo = split(ct.astype(f32) * inv[one])
            both = mm(turned[side], cat([hi, lo], 1))
            u = both[:, :128] + both[:, 128:]
            uhi, ulo = split(u)
            stage[side, :, pl.ds(pl.multiple_of(one * 16, 16), 16), 0:128] = uhi.reshape(32, 16, 128)
            stage[side, :, pl.ds(pl.multiple_of(one * 16, 16), 16), 128:256] = ulo.reshape(32, 16, 128)

    @pl.when(step == steps - 1)
    def _():
        grads = []
        for side in range(2):
            def body(b, acc):
                return acc + mm(stage[side, b], w_ref[side, b], NT)

            acc = lax.fori_loop(0, 32, body, jnp.zeros((512, 32), f32))
            res[:, 0:32] = acc
            grads.append(cat([res[pl.ds(s, 32, stride=16), :] for s in range(16)], 0)[:, 0:32])
        live = own_ref[...].reshape(512, 128)
        lv = adj_ref[...].reshape(512, 128)[:, 64:].astype(f32)
        dlr = cat(grads, 1) * lv
        m2 = m2_ref[...].reshape(512, 64)
        xn2, rstd2 = norm_rows(m2)
        adj = adj_ref[...].reshape(512, 128)[:, :64].astype(f32)
        g2 = adj + norm_back(xn2, rstd2, mm2(dlr, wt_ref[...], NT))
        g2_ref[...] = g2.reshape(16, 32, 64)
        xn, _ = norm_rows(m1_ref[...].reshape(512, 64))
        gate = jax.nn.sigmoid(mm2(xn, cw_ref[:, 192:256]))
        dmix = mm2(g2, wv_ref[...], NT)
        attended = spread(unpair(c2_ref[:, 16, :]))
        dcg_ref[...] = (dmix * attended * gate * (1.0 - gate)).reshape(16, 32, 64)
        da = jnp.sum((gate * dmix).reshape(16, 32, 64), 0)
        packed = cat([da[:16], da[16:]], 1)
        for k in range(16):
            e1_ref[k] = packed


def row_bwd_kernel(
    e1_ref, c2_ref, m1_ref, own_ref, g2_ref, dcg_ref, cw_ref,
    p_ref, o_ref, x2_ref, x2o_ref, any_ref, win_ref, wo_ref,
    g1_ref, dxo_ref, f_ref, bias_ref,
    g1s, wqg, wkt2, wvv, wo2, wback, wown,
):
    s = pl.program_id(0)

    @pl.when(s == 0)
    def _():
        w = win_ref[...].astype(f32)
        wt = w.T
        qg = cat([wt[0:64], wt[192:256]], 0)
        wqg[...] = cat([qg, qg], 1).astype(bf16)
        wkt2[...] = cat([wt[64:128], wt[64:128]], 1).astype(bf16)
        wv = w[:, 128:192]
        row = cat([wv, wv], 1)
        wvv[...] = cat([row, row], 0).astype(bf16)
        wo = wo_ref[...].astype(f32)
        wo2[...] = cat([wo, wo], 1).astype(bf16)
        wback[...] = cat([wt[64:128], wt[64:128], wt[128:192], wt[128:192]], 0).astype(bf16)
        wown[...] = cat([qg, qg], 0).astype(bf16)

        cw = cw_ref[...]
        groups = head_mask(64, 64, 8, 8).astype(bf16)
        da = jnp.sum(e1_ref[...], 0)
        da = unpair(da)
        attended = unpair(c2_ref[:, 16, :])
        peak = unpair(c2_ref[:, 17, :])
        den = unpair(c2_ref[:, 18, :])
        colq = unpair(c2_ref[:, 19, :])
        count = unpair(c2_ref[:, 20, :])
        delta = mm3(da * attended, groups)
        feature = lax.broadcasted_iota(jnp.int32, (32, 64), 1) % 8
        dq = jnp.zeros((32, 64), f32)
        for k in range(8):
            z = mm3(da * unpair(c2_ref[:, k, :]), groups) - delta * unpair(c2_ref[:, 8 + k, :])
            dq = dq + jnp.where(feature == k, z, 0.0)
        dtotal = mm2(dq * SCALE, cw[:, 0:64], NT) / jnp.maximum(count, 1.0)
        live = own_ref[...].reshape(512, 128)[:, 64:].astype(f32)
        xn, rstd = norm_rows(m1_ref[...].reshape(512, 64))
        kt = mm2(xn, cw[:, 64:128])
        vt = mm2(xn, cw[:, 128:192])
        qs = spread(colq)
        logits = jnp.where(live > 0, mm3(kt * qs, groups), NEG)
        weights = jnp.exp(logits - spread(peak)) / spread(den)
        das = spread(da)
        dl = weights * (mm2(vt * das, groups) - spread(delta)) * live
        dxn = (
            mm2(dcg_ref[...].reshape(512, 64), cw[:, 192:256], NT)
            + mm2(dl * qs, cw[:, 64:128], NT)
            + mm2(weights * das, cw[:, 128:192], NT)
            + live * spread(dtotal)
        )
        g1 = g2_ref[...].reshape(512, 64) + norm_back(xn, rstd, dxn)
        g1s[...] = g1.reshape(16, 32, 64)
        bias_ref[...] = jnp.zeros_like(bias_ref)

    dm = g1s[s]
    g1_ref[0] = dm
    heads = head_mask(64, 256, 8, 32)
    p = p_ref[0]
    o = o_ref[0]
    x2 = x2_ref[0]
    x2o = x2o_ref[0]
    vv = mm(x2, wvv[...])
    vhi = vv.astype(bf16)
    lane = lax.broadcasted_iota(jnp.int32, (256, 128), 1)
    v2 = jnp.where(lane < 64, vv, vv - vhi.astype(f32)).astype(bf16)
    khi, klo = split(mm(wkt2[...], x2, NT))
    qg = mm(wqg[...], cat([x2o] * 8, 0), NT)
    q = qg[:64] * (heads * SCALE)
    gate = jax.nn.sigmoid(qg[64:])
    dout = mm(wo2[...], cat([pair2(dm)] * 8, 0), NT)
    dgate = dout * o * gate * (1.0 - gate)
    do = dout * gate * heads
    do_live = do * any_ref[0, 0:1, :]
    delta = jnp.sum(do_live * o, 0, keepdims=True)
    lhi, llo = split(do_live)
    dp = mm(v2, cat([lhi, lhi], 0)) + mm(vhi[:, :64], llo)
    ds = p * (dp - delta)
    bias_ref[...] += ds.reshape(16, 16, 256)
    shi, slo = split(ds)
    first = mm(cat([khi, klo], 0), shi)
    dq = (first[:64] + first[64:] + mm(khi, slo)) * (heads * SCALE)
    qhi, qlo = split(q)
    zero = jnp.zeros((64, 256), bf16)
    dk = mm(shi, cat([qhi, qlo], 0), NT) + mm(slo, cat([qhi, zero], 0), NT)
    phi, plo = split(p)
    dhi, dlo = split(do)
    dv = mm(phi, cat([dhi, dlo], 0), NT) + mm(plo, cat([dhi, zero], 0), NT)
    kv = cat([dk, dv], 1)
    dx = mm2(kv, wback[...]).reshape(8, 32, 64)
    f_ref[:, 0] = cat([dx[:, :16], dx[:, 16:]], 2)
    qhi2, qlo2 = split(cat([dq, dgate], 0))
    dxo = mm(cat([qhi2, qlo2], 0), wown[...], TN)
    dxo_ref[0] = jnp.sum(dxo.reshape(8, 32, 64), 0)


def final_rows_kernel(f_ref, dxo_ref, g1_ref, own_ref, out_ref):
    total = jnp.sum(f_ref[...], 0)
    total = cat([total[:, :, :64], total[:, :, 64:]], 1).reshape(512, 64)
    total = total + dxo_ref[...].reshape(512, 64)
    xn, rstd = norm_rows(own_ref[...].reshape(512, 128)[:, :64].astype(f32))
    out = g1_ref[...].reshape(512, 64) + norm_back(xn, rstd, total)
    out_ref[...] = out.reshape(16, 32, 64)


def final_pair_kernel(b_ref, pair_ref, wb_ref, ct_ref, out_ref, scr):
    total = jnp.sum(b_ref[...], 0)
    wbt = wb_ref[...].astype(f32).T
    w2 = cat([wbt, wbt], 0).astype(bf16)
    own = head_mask(8, 256, 1, 32)
    for j in range(16):
        wide = jnp.broadcast_to(total[j:j + 1, :], (8, 256)) * own
        hi, lo = split(wide)
        y = mm(cat([hi, lo], 0), w2, TN)
        scr[:, j, :] = jnp.sum(y.reshape(8, 32, 128), 0)
    xn, rstd = norm_rows(pair_ref[...].reshape(512, 128).astype(f32))
    out = norm_back(xn, rstd, scr[...].reshape(512, 128)) + ct_ref[...].reshape(512, 128).astype(f32)
    out_ref[...] = out.reshape(32, 16, 128)


def sds(shape, dtype=f32):
    return jax.ShapeDtypeStruct(shape, dtype)


def full(shape):
    zeros = (0,) * len(shape)
    return pl.BlockSpec(shape, lambda s: zeros)


def row(shape):
    rest = (0,) * (len(shape) - 1)
    return pl.BlockSpec((1,) + shape[1:], lambda s: (s,) + rest)


def whole_call(kernel, out_shape, *args, scratch=()):
    return pl.pallas_call(
        kernel, out_shape=out_shape, scratch_shapes=list(scratch), compiler_params=VMEM
    )(*args)


def body(
    alignment_state,
    pairwise_state,
    alignment_mask,
    residue_entry_mask,
    sequence_live_count,
    horizontal_intake_coefs,
    pairwise_bias_weights,
    horizontal_readout_coefs,
    column_input_weights,
    vertical_readout_coefs,
    tensor_factor_coefs,
    outer_output_weights,
    adjoint_of_result_track,
    pairwise_cotangent,
):
    seq = jnp.arange(16, dtype=jnp.int32)
    live = (
        alignment_mask
        * residue_entry_mask[None, :]
        * (seq < sequence_live_count[0]).astype(jnp.int32)[:, None]
    ).astype(bf16)
    live_lanes = jnp.broadcast_to(live[:, :, None], (16, 32, 64))
    own = cat([alignment_state, live_lanes], 2)
    adj = cat([adjoint_of_result_track, live_lanes], 2)
    cw = cat(
        [
            column_input_weights[:, :64],
            jnp.tile(column_input_weights[:, 64:72], (1, 8)),
            jnp.tile(column_input_weights[:, 72:80], (1, 8)),
            column_input_weights[:, 80:],
        ],
        1,
    )
    w3 = outer_output_weights.reshape(32, 32, 128)
    wouter = jnp.stack([w3.transpose(1, 0, 2), w3], 0)
    wouter = cat([wouter, wouter], 3)

    turned = pairwise_cotangent.transpose(1, 0, 2)
    perm = [(d * 8 + r, (2 * r + d % 2) * 8 + d // 2) for d in range(16) for r in range(8)]
    turned = lax.ppermute(turned, ("depth", "res"), perm)
    both = cat([pairwise_cotangent.reshape(512, 128), turned.reshape(512, 128)], 0)
    ct = lax.all_gather(both, "depth", axis=0, tiled=False)

    rows = lax.all_to_all(jnp.broadcast_to(own[None], (8, 16, 32, 128)), "res", 0, 0)
    bias_block = whole_call(
        bias_kernel, sds((16, 16, 256)), pairwise_state, pairwise_bias_weights,
        scratch=[pltpu.VMEM((32, 16, 128), f32)],
    )
    bias = lax.all_to_all(bias_block, "depth", 0, 0)

    grow = pl.BlockSpec((8, 1, 32, 128), lambda s: (0, s, 0, 0))
    p, o, x2, x2o, m1, any_live, c1 = pl.pallas_call(
        row_fwd_kernel,
        grid=(16,),
        in_specs=[grow, row((16, 32, 128)), full((16, 16, 256)), full((64, 256)), full((64, 64))],
        out_specs=[
            row((16, 256, 256)), row((16, 64, 256)), row((16, 256, 128)), row((16, 32, 128)),
            row((16, 32, 64)), row((16, 8, 256)), full((16, 2, 16, 128)),
        ],
        out_shape=[
            sds((16, 256, 256)), sds((16, 64, 256)), sds((16, 256, 128), bf16),
            sds((16, 32, 128), bf16), sds((16, 32, 64)), sds((16, 8, 256)), sds((16, 2, 16, 128)),
        ],
        scratch_shapes=[
            pltpu.VMEM((128, 128), bf16), pltpu.VMEM((64, 128), bf16),
            pltpu.VMEM((128, 128), bf16), pltpu.VMEM((128, 64), bf16),
        ],
        compiler_params=VMEM,
    )(rows, own, bias, horizontal_intake_coefs, horizontal_readout_coefs)

    c1 = lax.all_to_all(c1, "depth", 0, 0)
    c2 = whole_call(col_kernel, sds((16, 32, 128)), c1, cw)
    c2 = lax.all_to_all(c2, "depth", 0, 0)
    m2, dblock = whole_call(
        factor_kernel, [sds((16, 32, 64)), sds((8, 16, 32, 128), bf16)],
        m1, c2, own, cw, vertical_readout_coefs, tensor_factor_coefs,
    )
    factors = lax.all_to_all(dblock, "res", 0, 0)

    cta = ct.reshape(16, 2, 32, 16, 128)
    ctb = ct.reshape(8, 2, 2, 16, 32, 128)
    g2, dcg, e1 = pl.pallas_call(
        outer_kernel,
        grid=(8,),
        in_specs=[
            full((8, 16, 32, 128)),
            pl.BlockSpec((1, 16, 32, 128), lambda s: (0, 0, 0, 0)),
            pl.BlockSpec((16, 1, 4, 16, 128), lambda s: (0, 0, s, 0, 0)),
            pl.BlockSpec((8, 1, 1, 4, 32, 128), lambda s: (0, s // 4, 1, s % 4, 0, 0)),
            full((2, 32, 32, 256)),
            full((16, 32, 64)), full((16, 32, 128)), full((16, 32, 64)), full((16, 32, 128)),
            full((64, 256)), full((64, 64)), full((64, 64)),
        ],
        out_specs=[full((16, 32, 64)), full((16, 32, 64)), full((16, 16, 128))],
        out_shape=[sds((16, 32, 64)), sds((16, 32, 64)), sds((16, 16, 128))],
        scratch_shapes=[
            pltpu.VMEM((32, 256, 128), f32),
            pltpu.VMEM((2, 512, 256), bf16),
            pltpu.VMEM((2, 32, 512, 256), bf16),
            pltpu.VMEM((512, 128), f32),
            pltpu.VMEM((2, 1024, 128), f32),
        ],
        compiler_params=VMEM,
    )(
        factors, dblock, cta, ctb, wouter, m2, c2, m1, adj, cw, vertical_readout_coefs,
        tensor_factor_coefs,
    )
    e1 = lax.all_to_all(e1, "depth", 0, 0)

    g1, dxo, fblock, bblock = pl.pallas_call(
        row_bwd_kernel,
        grid=(16,),
        in_specs=[
            full((16, 16, 128)), full((16, 32, 128)), full((16, 32, 64)), full((16, 32, 128)),
            full((16, 32, 64)), full((16, 32, 64)), full((64, 256)),
            row((16, 256, 256)), row((16, 64, 256)), row((16, 256, 128)), row((16, 32, 128)),
            row((16, 8, 256)), full((64, 256)), full((64, 64)),
        ],
        out_specs=[
            row((16, 32, 64)), row((16, 32, 64)),
            pl.BlockSpec((8, 1, 16, 128), lambda s: (0, s, 0, 0)), full((16, 16, 256)),
        ],
        out_shape=[sds((16, 32, 64)), sds((16, 32, 64)), sds((8, 16, 16, 128)), sds((16, 16, 256))],
        scratch_shapes=[
            pltpu.VMEM((16, 32, 64), f32),
            pltpu.VMEM((128, 128), bf16), pltpu.VMEM((64, 128), bf16), pltpu.VMEM((128, 128), bf16),
            pltpu.VMEM((64, 128), bf16), pltpu.VMEM((256, 64), bf16), pltpu.VMEM((256, 64), bf16),
        ],
        compiler_params=VMEM,
    )(
        e1, c2, m1, own, g2, dcg, cw, p, o, x2, x2o, any_live,
        horizontal_intake_coefs, horizontal_readout_coefs,
    )
    fsum = lax.all_to_all(fblock, "res", 0, 0)
    bsum = lax.all_to_all(bblock, "depth", 0, 0)
    alignment_gradient = whole_call(final_rows_kernel, sds((16, 32, 64)), fsum, dxo, g1, own)
    pair_grad = whole_call(
        final_pair_kernel, sds((32, 16, 128)), bsum, pairwise_state, pairwise_bias_weights,
        pairwise_cotangent, scratch=[pltpu.VMEM((32, 16, 128), f32)],
    )
    return alignment_gradient, pair_grad


def solution(mesh):
    in_specs = (
        P("depth", "res", None),
        P("res", "depth", None),
        P("depth", "res"),
        P("res"),
        P("depth"),
        P(),
        P(),
        P(),
        P(),
        P(),
        P(),
        P(),
        P("depth", "res", None),
        P("res", "depth", None),
    )
    out_specs = (P("depth", "res", None), P("res", "depth", None))
    return jax.shard_map(body, mesh=mesh, in_specs=in_specs, out_specs=out_specs, check_vma=False)
```

```python
import jax
import jax.numpy as jnp
from jax import lax
from jax.experimental import pallas as pl
from jax.experimental.pallas import tpu as pltpu
from jax.sharding import PartitionSpec as P

f32 = jnp.float32
bf16 = jnp.bfloat16
EPS = 1e-05
NEG = -1000000000.0
SCALE = 8 ** (-0.5)
NN = (((1,), (0,)), ((), ()))
NT = (((1,), (1,)), ((), ()))
TN = (((0,), (0,)), ((), ()))
GROUP = 4
OWN_STEP = 8
VMEM = pltpu.CompilerParams(vmem_limit_bytes=50 * 1024 * 1024)


def mm(a, b, dims=NN):
    return lax.dot_general(a, b, dims, preferred_element_type=f32)


def split(x):
    hi = x.astype(bf16)
    lo = (x - hi.astype(f32)).astype(bf16)
    return hi, lo


def split3(x):
    hi = x.astype(bf16)
    rest = x - hi.astype(f32)
    mid = rest.astype(bf16)
    lo = (rest - mid.astype(f32)).astype(bf16)
    return hi, mid, lo


def cat(parts, axis):
    return jnp.concatenate(parts, axis=axis)


def mm2(x, w, dims=NN):
    hi, lo = split(x)
    return mm(hi, w, dims) + mm(lo, w, dims)


def mm3(x, w):
    hi, mid, lo = split3(x)
    return mm(hi, w) + mm(mid, w) + mm(lo, w)


def norm_rows(x):
    center = x - jnp.mean(x, -1, keepdims=True)
    rstd = lax.rsqrt(jnp.mean(center * center, -1, keepdims=True) + EPS)
    return center * rstd, rstd


def norm_back(normed, rstd, grad):
    return rstd * (
        grad
        - jnp.mean(grad, -1, keepdims=True)
        - normed * jnp.mean(grad * normed, -1, keepdims=True)
    )


def pair2(x):
    hi, lo = split(x)
    return cat([hi, lo], 1)


def head_mask(rows, cols, row_div, col_div):
    a = lax.broadcasted_iota(jnp.int32, (rows, cols), 0) // row_div
    b = lax.broadcasted_iota(jnp.int32, (rows, cols), 1) // col_div
    return (a == b).astype(f32)


def bias_kernel(pair_ref, wb_ref, out_ref, scr):
    xn, _ = norm_rows(pair_ref[...].astype(f32).reshape(512, 128))
    scr[...] = xn.reshape(32, 16, 128)
    wbt = wb_ref[...].astype(f32).T
    w2 = cat([wbt, wbt], 1).astype(bf16)
    own = head_mask(8, 256, 1, 32)
    rows = []
    for j in range(16):
        x2 = pair2(scr[:, j, :])
        tiled = cat([x2] * 8, 0)
        full = mm(w2, tiled, NT)
        rows.append(jnp.sum(full * own, 0, keepdims=True))
    block = cat(rows, 0)
    for k in range(16):
        out_ref[k] = block


def row_fwd_kernel(
    g_ref, own_ref, bias_ref, win_ref, wo_ref,
    p_ref, o_ref, x2_ref, x2o_ref, m1_ref, any_ref, c1_ref,
    wqg, wvt2, wkk, wo2,
):
    s = pl.program_id(0)

    @pl.when(s == 0)
    def _():
        w = win_ref[...].astype(f32)
        wt = w.T
        qg = cat([wt[0:64], wt[192:256]], 0)
        wqg[...] = cat([qg, qg], 1).astype(bf16)
        wvt = wt[128:192]
        wvt2[...] = cat([wvt, wvt], 1).astype(bf16)
        wk = w[:, 64:128]
        row = cat([wk, wk], 1)
        wkk[...] = cat([row, row], 0).astype(bf16)
        wo = wo_ref[...].astype(f32)
        wo2[...] = cat([wo, wo], 0).astype(bf16)

    for u in range(GROUP):
        g = g_ref[:, u].reshape(256, 128).astype(f32)
        live = g[:, 64:65]
        xn, _ = norm_rows(g[:, :64])
        x2 = pair2(xn)
        x2_ref[u] = x2
        kk = mm(x2, wkk[...])
        khi = kk.astype(bf16)
        lane = lax.broadcasted_iota(jnp.int32, (256, 128), 1)
        k2 = jnp.where(lane < 64, kk, kk - khi.astype(f32)).astype(bf16)
        vt = mm(wvt2[...], x2, NT)

        own = own_ref[u].astype(f32)
        xo = own[:, :64]
        xon, _ = norm_rows(xo)
        x2o = pair2(xon)
        x2o_ref[u] = x2o
        qg = mm(wqg[...], cat([x2o] * 8, 0), NT)
        heads = head_mask(64, 256, 8, 32)
        q = qg[:64] * (heads * SCALE)
        gate = jax.nn.sigmoid(qg[64:])
        qhi, qlo = split(q)
        logits = mm(k2, cat([qhi, qhi], 0)) + mm(khi[:, :64], qlo)
        logits = logits + bias_ref[...].reshape(256, 256)
        logits = jnp.where(live > 0, logits, NEG)
        e = jnp.exp(logits - jnp.max(logits, 0, keepdims=True))
        p = e * (1.0 / jnp.sum(e, 0, keepdims=True))
        p_ref[u] = p
        any_ref[u] = jnp.broadcast_to(jnp.max(live, 0, keepdims=True), (8, 256))
        phi, plo = split(p)
        vhi, vlo = split(vt)
        first = mm(cat([vhi, vlo], 0), phi)
        o = (first[:64] + first[64:] + mm(vhi, plo)) * heads
        o_ref[u] = o
        ahi, alo = split(o * gate)
        y = mm(cat([ahi, alo], 0), wo2[...], TN)
        m1 = xo + jnp.sum(y.reshape(8, 32, 64), 0)
        m1_ref[u] = m1
        c1_ref[:, 0, s * GROUP + u, :] = cat([m1[:16], m1[16:]], 1)
        lv = own[:, 64:]
        c1_ref[:, 1, s * GROUP + u, :] = cat([lv[:16], lv[16:]], 1)


def diag2(w):
    z = jnp.zeros_like(w)
    return cat([cat([w, z], 1), cat([z, w], 1)], 0)


def col_kernel(c1_ref, cw_ref, out_ref):
    x = c1_ref[:, 0].reshape(256, 128)
    live = c1_ref[:, 1].reshape(256, 128)
    halves = (head_mask(128, 128, 64, 64) * (1.0 / 64)).astype(bf16)
    center = x - mm3(x, halves)
    xn = center * lax.rsqrt(mm3(center * center, halves) + EPS)
    cw = cw_ref[...].astype(f32)
    wq = diag2(cw[:, 0:64]).astype(bf16)
    wk = diag2(cw[:, 64:128]).astype(bf16)
    wv = diag2(cw[:, 128:192]).astype(bf16)
    total = jnp.sum(live * xn, 0, keepdims=True)
    count = jnp.sum(live, 0, keepdims=True)
    mean = total / jnp.maximum(count, 1.0)
    colq = mm3(jnp.broadcast_to(mean, (8, 128)), wq)[0:1] * SCALE
    kt = mm2(xn, wk)
    vt = mm2(xn, wv)
    groups = head_mask(128, 128, 8, 8).astype(bf16)
    logits = jnp.where(live > 0, mm3(kt * colq, groups), NEG)
    peak = jnp.max(logits, 0, keepdims=True)
    e = jnp.exp(logits - peak)
    den = jnp.sum(e, 0, keepdims=True)
    w = e / den
    wv_ = w * vt
    attended = jnp.sum(wv_, 0, keepdims=True)
    khi, klo = split(kt)

    def by_key(z):
        zhi, zlo = split(z)
        full = mm(khi, zhi, TN) + mm(klo, zhi, TN) + mm(khi, zlo, TN)
        lane = lax.broadcasted_iota(jnp.int32, (8, 128), 1)
        return jnp.where(lane < 64, full[0:8], full[64:72])

    lt = live.T
    rows = [
        by_key(wv_), by_key(w), attended, peak, den, colq, count, count, count, count,
        lt[0:1, :128], lt[0:1, 128:], lt[64:65, :128], lt[64:65, 128:],
        count, count, count, count,
    ]
    block = cat(rows, 0)
    for k in range(16):
        out_ref[k] = block


def unpair(x):
    return cat([x[:, 0:64], x[:, 64:128]], 0)


def spread(v):
    return jnp.broadcast_to(v[None], (16, 32, 64)).reshape(512, 64)


def factor_kernel(m1_ref, c2_ref, own_ref, cw_ref, wv_ref, wt_ref, m2_ref, d_ref):
    m1 = m1_ref[...].reshape(512, 64)
    live = own_ref[...].reshape(512, 128)[:, 64:].astype(f32)
    attended = unpair(c2_ref[:, 16, :])
    xn, _ = norm_rows(m1)
    gate = jax.nn.sigmoid(mm2(xn, cw_ref[:, 192:256]))
    m2 = m1 + mm2(gate * spread(attended), wv_ref[...])
    m2_ref[...] = m2.reshape(16, 32, 64)
    xn2, _ = norm_rows(m2)
    lr = live * mm2(xn2, wt_ref[...])
    lt = cat(
        [cat([c2_ref[:, 24, :], c2_ref[:, 25, :]], 1), cat([c2_ref[:, 26, :], c2_ref[:, 27, :]], 1)],
        0,
    )
    pad = jnp.zeros((12, 32, 64), f32)
    planes = [lt[None, :, 64 * k:64 * k + 64] for k in range(4)]
    right = cat(planes + [pad], 0).reshape(512, 64)
    block = cat([lr, right], 1).astype(bf16).reshape(16, 32, 128)
    for k in range(8):
        d_ref[k] = block


def outer_kernel(
    da_ref, own_ref, cta_ref, ctb_ref, w_ref, m2_ref, c2_ref, m1_ref, adj_ref, cw_ref, wv_ref,
    wt_ref, g2_ref, dcg_ref, e1_ref,
    inv, turned, stage, res, lrs,
):
    step = pl.program_id(0)

    @pl.when(step == 0)
    def _():
        norm = jnp.zeros((256, 32), f32)
        for k in range(4):
            allk = da_ref[:, k, :, 64:].reshape(256, 64)
            ownk = own_ref[0, k, :, 64:]
            norm = norm + mm(allk, ownk, NT)
        value = 1.0 / jnp.maximum(norm, 1.0)
        for k in range(32):
            inv[k] = jnp.broadcast_to(value[:, k:k + 1], (256, 128))
        for s in range(16):
            piece = da_ref[:, s].reshape(256, 128).astype(f32).T
            for half in range(2):
                cols = piece[:, 128 * half:128 * half + 128]
                lrs[half, pl.ds(s, 32, stride=16), :] = cols[0:32]
                lrs[half, pl.ds(512 + s, 32, stride=16), :] = cols[32:64]
        for half in range(2):
            turned[0, :, 128 * half:128 * half + 128] = lrs[half, 512:1024].astype(bf16)
            turned[1, :, 128 * half:128 * half + 128] = lrs[half, 0:512].astype(bf16)

    for side in range(2):
        for k in range(OWN_STEP):
            one = step * OWN_STEP + k
            if side == 0:
                ct = cta_ref[:, 0, k].reshape(256, 128)
            else:
                ct = ctb_ref[:, 0, 0, k].reshape(256, 128)
            hi, lo = split(ct.astype(f32) * inv[one])
            both = mm(turned[side], cat([hi, lo], 1))
            uhi, ulo = split(both[:, :128] + both[:, 128:])
            at = pl.ds(pl.multiple_of(one * 16, 16), 16)
            for b in range(32):
                stage[side, at, 256 * b:256 * b + 128] = uhi[16 * b:16 * b + 16]
                stage[side, at, 256 * b + 128:256 * b + 256] = ulo[16 * b:16 * b + 16]

    @pl.when(step == 32 // OWN_STEP - 1)
    def _():
        grads = []
        for side in range(2):
            res[:, 0:32] = mm(stage[side], w_ref[side], NT)
            grads.append(cat([res[pl.ds(s, 32, stride=16), :] for s in range(16)], 0)[:, 0:32])
        lv = adj_ref[...].reshape(512, 128)[:, 64:].astype(f32)
        dlr = cat(grads, 1) * lv
        m2 = m2_ref[...].reshape(512, 64)
        xn2, rstd2 = norm_rows(m2)
        adj = adj_ref[...].reshape(512, 128)[:, :64].astype(f32)
        g2 = adj + norm_back(xn2, rstd2, mm2(dlr, wt_ref[...], NT))
        g2_ref[...] = g2.reshape(16, 32, 64)
        xn, _ = norm_rows(m1_ref[...].reshape(512, 64))
        gate = jax.nn.sigmoid(mm2(xn, cw_ref[:, 192:256]))
        dmix = mm2(g2, wv_ref[...], NT)
        attended = spread(unpair(c2_ref[:, 16, :]))
        dcg_ref[...] = (dmix * attended * gate * (1.0 - gate)).reshape(16, 32, 64)
        da = jnp.sum((gate * dmix).reshape(16, 32, 64), 0)
        packed = cat([da[:16], da[16:]], 1)
        for k in range(16):
            e1_ref[k] = packed


def row_bwd_kernel(
    e1_ref, c2_ref, m1_ref, own_ref, g2_ref, dcg_ref, cw_ref,
    p_ref, o_ref, x2_ref, x2o_ref, any_ref, win_ref, wo_ref,
    g1_ref, dxo_ref, f_ref, bias_ref,
    g1s, wqg, wkt2, wvv, wo2, wback, wown,
):
    s = pl.program_id(0)

    @pl.when(s == 0)
    def _():
        w = win_ref[...].astype(f32)
        wt = w.T
        qg = cat([wt[0:64], wt[192:256]], 0)
        wqg[...] = cat([qg, qg], 1).astype(bf16)
        wkt2[...] = cat([wt[64:128], wt[64:128]], 1).astype(bf16)
        wv = w[:, 128:192]
        row = cat([wv, wv], 1)
        wvv[...] = cat([row, row], 0).astype(bf16)
        wo = wo_ref[...].astype(f32)
        wo2[...] = cat([wo, wo], 1).astype(bf16)
        wback[...] = cat([wt[64:128], wt[64:128], wt[128:192], wt[128:192]], 0).astype(bf16)
        wown[...] = cat([qg, qg], 0).astype(bf16)

        cw = cw_ref[...]
        groups = head_mask(64, 64, 8, 8).astype(bf16)
        da = jnp.sum(e1_ref[...], 0)
        da = unpair(da)
        attended = unpair(c2_ref[:, 16, :])
        peak = unpair(c2_ref[:, 17, :])
        den = unpair(c2_ref[:, 18, :])
        colq = unpair(c2_ref[:, 19, :])
        count = unpair(c2_ref[:, 20, :])
        delta = mm3(da * attended, groups)
        feature = lax.broadcasted_iota(jnp.int32, (32, 64), 1) % 8
        dq = jnp.zeros((32, 64), f32)
        for k in range(8):
            z = mm3(da * unpair(c2_ref[:, k, :]), groups) - delta * unpair(c2_ref[:, 8 + k, :])
            dq = dq + jnp.where(feature == k, z, 0.0)
        dtotal = mm2(dq * SCALE, cw[:, 0:64], NT) / jnp.maximum(count, 1.0)
        live = own_ref[...].reshape(512, 128)[:, 64:].astype(f32)
        xn, rstd = norm_rows(m1_ref[...].reshape(512, 64))
        kt = mm2(xn, cw[:, 64:128])
        vt = mm2(xn, cw[:, 128:192])
        qs = spread(colq)
        logits = jnp.where(live > 0, mm3(kt * qs, groups), NEG)
        weights = jnp.exp(logits - spread(peak)) / spread(den)
        das = spread(da)
        dl = weights * (mm2(vt * das, groups) - spread(delta)) * live
        dxn = (
            mm2(dcg_ref[...].reshape(512, 64), cw[:, 192:256], NT)
            + mm2(dl * qs, cw[:, 64:128], NT)
            + mm2(weights * das, cw[:, 128:192], NT)
            + live * spread(dtotal)
        )
        g1 = g2_ref[...].reshape(512, 64) + norm_back(xn, rstd, dxn)
        g1s[...] = g1.reshape(16, 32, 64)
        bias_ref[...] = jnp.zeros_like(bias_ref)

    for u in range(GROUP):
        dm = g1s[s * GROUP + u]
        g1_ref[u] = dm
        heads = head_mask(64, 256, 8, 32)
        p = p_ref[u]
        o = o_ref[u]
        x2 = x2_ref[u]
        x2o = x2o_ref[u]
        vv = mm(x2, wvv[...])
        vhi = vv.astype(bf16)
        lane = lax.broadcasted_iota(jnp.int32, (256, 128), 1)
        v2 = jnp.where(lane < 64, vv, vv - vhi.astype(f32)).astype(bf16)
        khi, klo = split(mm(wkt2[...], x2, NT))
        qg = mm(wqg[...], cat([x2o] * 8, 0), NT)
        q = qg[:64] * (heads * SCALE)
        gate = jax.nn.sigmoid(qg[64:])
        dout = mm(wo2[...], cat([pair2(dm)] * 8, 0), NT)
        dgate = dout * o * gate * (1.0 - gate)
        do = dout * gate * heads
        do_live = do * any_ref[u, 0:1, :]
        delta = jnp.sum(do_live * o, 0, keepdims=True)
        lhi, llo = split(do_live)
        dp = mm(v2, cat([lhi, lhi], 0)) + mm(vhi[:, :64], llo)
        ds = p * (dp - delta)
        bias_ref[...] += ds.reshape(16, 16, 256)
        shi, slo = split(ds)
        first = mm(cat([khi, klo], 0), shi)
        dq = (first[:64] + first[64:] + mm(khi, slo)) * (heads * SCALE)
        qhi, qlo = split(q)
        zero = jnp.zeros((64, 256), bf16)
        dk = mm(shi, cat([qhi, qlo], 0), NT) + mm(slo, cat([qhi, zero], 0), NT)
        phi, plo = split(p)
        dhi, dlo = split(do)
        dv = mm(phi, cat([dhi, dlo], 0), NT) + mm(plo, cat([dhi, zero], 0), NT)
        kv = cat([dk, dv], 1)
        dx = mm2(kv, wback[...]).reshape(8, 32, 64)
        f_ref[:, u] = cat([dx[:, :16], dx[:, 16:]], 2)
        qhi2, qlo2 = split(cat([dq, dgate], 0))
        dxo = mm(cat([qhi2, qlo2], 0), wown[...], TN)
        dxo_ref[u] = jnp.sum(dxo.reshape(8, 32, 64), 0)


def final_rows_kernel(f_ref, dxo_ref, g1_ref, own_ref, out_ref):
    total = jnp.sum(f_ref[...], 0)
    total = cat([total[:, :, :64], total[:, :, 64:]], 1).reshape(512, 64)
    total = total + dxo_ref[...].reshape(512, 64)
    xn, rstd = norm_rows(own_ref[...].reshape(512, 128)[:, :64].astype(f32))
    out = g1_ref[...].reshape(512, 64) + norm_back(xn, rstd, total)
    out_ref[...] = out.reshape(16, 32, 64)


def final_pair_kernel(b_ref, pair_ref, wb_ref, ct_ref, out_ref, scr):
    total = jnp.sum(b_ref[...], 0)
    wbt = wb_ref[...].astype(f32).T
    w2 = cat([wbt, wbt], 0).astype(bf16)
    own = head_mask(8, 256, 1, 32)
    for j in range(16):
        wide = jnp.broadcast_to(total[j:j + 1, :], (8, 256)) * own
        hi, lo = split(wide)
        y = mm(cat([hi, lo], 0), w2, TN)
        scr[:, j, :] = jnp.sum(y.reshape(8, 32, 128), 0)
    xn, rstd = norm_rows(pair_ref[...].reshape(512, 128).astype(f32))
    out = norm_back(xn, rstd, scr[...].reshape(512, 128)) + ct_ref[...].reshape(512, 128).astype(f32)
    out_ref[...] = out.reshape(32, 16, 128)


def sds(shape, dtype=f32):
    return jax.ShapeDtypeStruct(shape, dtype)


def full(shape):
    zeros = (0,) * len(shape)
    return pl.BlockSpec(shape, lambda s: zeros)


def row(shape):
    rest = (0,) * (len(shape) - 1)
    return pl.BlockSpec((GROUP,) + shape[1:], lambda s: (s,) + rest)


def whole_call(kernel, out_shape, *args, scratch=()):
    return pl.pallas_call(
        kernel, out_shape=out_shape, scratch_shapes=list(scratch), compiler_params=VMEM
    )(*args)


def row_forward(rows, own, bias, win, wo):
    grow = pl.BlockSpec((8, GROUP, 32, 128), lambda s: (0, s, 0, 0))
    return pl.pallas_call(
        row_fwd_kernel,
        grid=(16 // GROUP,),
        in_specs=[grow, row((16, 32, 128)), full((16, 16, 256)), full((64, 256)), full((64, 64))],
        out_specs=[
            row((16, 256, 256)), row((16, 64, 256)), row((16, 256, 128)), row((16, 32, 128)),
            row((16, 32, 64)), row((16, 8, 256)), full((16, 2, 16, 128)),
        ],
        out_shape=[
            sds((16, 256, 256)), sds((16, 64, 256)), sds((16, 256, 128), bf16),
            sds((16, 32, 128), bf16), sds((16, 32, 64)), sds((16, 8, 256)), sds((16, 2, 16, 128)),
        ],
        scratch_shapes=[
            pltpu.VMEM((128, 128), bf16), pltpu.VMEM((64, 128), bf16),
            pltpu.VMEM((128, 128), bf16), pltpu.VMEM((128, 64), bf16),
        ],
        compiler_params=VMEM,
    )(rows, own, bias, win, wo)


def outer_product(ct, factors, dblock, wouter, m2, c2, m1, adj, cw, wvo, wtf):
    cta = ct.reshape(16, 2, 32, 16, 128)
    ctb = ct.reshape(8, 2, 2, 16, 32, 128)
    return pl.pallas_call(
        outer_kernel,
        grid=(32 // OWN_STEP,),
        in_specs=[
            full((8, 16, 32, 128)),
            pl.BlockSpec((1, 16, 32, 128), lambda s: (0, 0, 0, 0)),
            pl.BlockSpec((16, 1, OWN_STEP, 16, 128), lambda s: (0, 0, s, 0, 0)),
            pl.BlockSpec(
                (8, 1, 1, OWN_STEP, 32, 128),
                lambda s: (0, s // (16 // OWN_STEP), 1, s % (16 // OWN_STEP), 0, 0),
            ),
            full((2, 32, 8192)),
            full((16, 32, 64)), full((16, 32, 128)), full((16, 32, 64)), full((16, 32, 128)),
            full((64, 256)), full((64, 64)), full((64, 64)),
        ],
        out_specs=[full((16, 32, 64)), full((16, 32, 64)), full((16, 16, 128))],
        out_shape=[sds((16, 32, 64)), sds((16, 32, 64)), sds((16, 16, 128))],
        scratch_shapes=[
            pltpu.VMEM((32, 256, 128), f32),
            pltpu.VMEM((2, 512, 256), bf16),
            pltpu.VMEM((2, 512, 8192), bf16),
            pltpu.VMEM((512, 128), f32),
            pltpu.VMEM((2, 1024, 128), f32),
        ],
        compiler_params=VMEM,
    )(
        factors, dblock, cta, ctb, wouter, m2, c2, m1, adj, cw, wvo, wtf,
    )


def row_backward(e1, c2, m1, own, g2, dcg, cw, p, o, x2, x2o, any_live, win, wo):
    return pl.pallas_call(
        row_bwd_kernel,
        grid=(16 // GROUP,),
        in_specs=[
            full((16, 16, 128)), full((16, 32, 128)), full((16, 32, 64)), full((16, 32, 128)),
            full((16, 32, 64)), full((16, 32, 64)), full((64, 256)),
            row((16, 256, 256)), row((16, 64, 256)), row((16, 256, 128)), row((16, 32, 128)),
            row((16, 8, 256)), full((64, 256)), full((64, 64)),
        ],
        out_specs=[
            row((16, 32, 64)), row((16, 32, 64)),
            pl.BlockSpec((8, GROUP, 16, 128), lambda s: (0, s, 0, 0)), full((16, 16, 256)),
        ],
        out_shape=[sds((16, 32, 64)), sds((16, 32, 64)), sds((8, 16, 16, 128)), sds((16, 16, 256))],
        scratch_shapes=[
            pltpu.VMEM((16, 32, 64), f32),
            pltpu.VMEM((128, 128), bf16), pltpu.VMEM((64, 128), bf16), pltpu.VMEM((128, 128), bf16),
            pltpu.VMEM((64, 128), bf16), pltpu.VMEM((256, 64), bf16), pltpu.VMEM((256, 64), bf16),
        ],
        compiler_params=VMEM,
    )(
        e1, c2, m1, own, g2, dcg, cw, p, o, x2, x2o, any_live,
        win, wo,
    )


def body(
    alignment_state,
    pairwise_state,
    alignment_mask,
    residue_entry_mask,
    sequence_live_count,
    horizontal_intake_coefs,
    pairwise_bias_weights,
    horizontal_readout_coefs,
    column_input_weights,
    vertical_readout_coefs,
    tensor_factor_coefs,
    outer_output_weights,
    adjoint_of_result_track,
    pairwise_cotangent,
):
    seq = jnp.arange(16, dtype=jnp.int32)
    live = (
        alignment_mask
        * residue_entry_mask[None, :]
        * (seq < sequence_live_count[0]).astype(jnp.int32)[:, None]
    ).astype(bf16)
    live_lanes = jnp.broadcast_to(live[:, :, None], (16, 32, 64))
    own = cat([alignment_state, live_lanes], 2)
    adj = cat([adjoint_of_result_track, live_lanes], 2)
    cw = cat(
        [
            column_input_weights[:, :64],
            jnp.tile(column_input_weights[:, 64:72], (1, 8)),
            jnp.tile(column_input_weights[:, 72:80], (1, 8)),
            column_input_weights[:, 80:],
        ],
        1,
    )
    w3 = outer_output_weights.reshape(32, 32, 128)
    wouter = jnp.stack([w3, w3.transpose(1, 0, 2)], 0)
    wouter = cat([wouter, wouter], 3).reshape(2, 32, 8192)

    turned = pairwise_cotangent.transpose(1, 0, 2)
    perm = [(d * 8 + r, (2 * r + d % 2) * 8 + d // 2) for d in range(16) for r in range(8)]
    turned = lax.ppermute(turned, ("depth", "res"), perm)
    both = cat([pairwise_cotangent.reshape(512, 128), turned.reshape(512, 128)], 0)

    rows = lax.all_to_all(jnp.broadcast_to(own[None], (8, 16, 32, 128)), "res", 0, 0)
    bias_block = whole_call(
        bias_kernel, sds((16, 16, 256)), pairwise_state, pairwise_bias_weights,
        scratch=[pltpu.VMEM((32, 16, 128), f32)],
    )
    bias_block, rows, both = lax.optimization_barrier((bias_block, rows, both))
    ct = lax.all_gather(both, "depth", axis=0, tiled=False)
    bias = lax.all_to_all(bias_block, "depth", 0, 0)

    p, o, x2, x2o, m1, any_live, c1 = row_forward(
        rows, own, bias, horizontal_intake_coefs, horizontal_readout_coefs
    )

    c1 = lax.all_to_all(c1, "depth", 0, 0)
    c2 = whole_call(col_kernel, sds((16, 32, 128)), c1, cw)
    c2 = lax.all_to_all(c2, "depth", 0, 0)
    m2, dblock = whole_call(
        factor_kernel, [sds((16, 32, 64)), sds((8, 16, 32, 128), bf16)],
        m1, c2, own, cw, vertical_readout_coefs, tensor_factor_coefs,
    )
    factors = lax.all_to_all(dblock, "res", 0, 0)

    g2, dcg, e1 = outer_product(
        ct, factors, dblock, wouter, m2, c2, m1, adj, cw, vertical_readout_coefs,
        tensor_factor_coefs,
    )
    e1 = lax.all_to_all(e1, "depth", 0, 0)

    g1, dxo, fblock, bblock = row_backward(
        e1, c2, m1, own, g2, dcg, cw, p, o, x2, x2o, any_live,
        horizontal_intake_coefs, horizontal_readout_coefs,
    )
    fsum = lax.all_to_all(fblock, "res", 0, 0)
    bsum = lax.all_to_all(bblock, "depth", 0, 0)
    alignment_gradient = whole_call(final_rows_kernel, sds((16, 32, 64)), fsum, dxo, g1, own)
    pair_grad = whole_call(
        final_pair_kernel, sds((32, 16, 128)), bsum, pairwise_state, pairwise_bias_weights,
        pairwise_cotangent, scratch=[pltpu.VMEM((32, 16, 128), f32)],
    )
    return alignment_gradient, pair_grad


def solution(mesh):
    in_specs = (
        P("depth", "res", None),
        P("res", "depth", None),
        P("depth", "res"),
        P("res"),
        P("depth"),
        P(),
        P(),
        P(),
        P(),
        P(),
        P(),
        P(),
        P("depth", "res", None),
        P("res", "depth", None),
    )
    out_specs = (P("depth", "res", None), P("res", "depth", None))
    return jax.shard_map(body, mesh=mesh, in_specs=in_specs, out_specs=out_specs, check_vma=False)
```

```python
import jax
import jax.numpy as jnp
from jax import lax
from jax.experimental import pallas as pl
from jax.experimental.pallas import tpu as pltpu
from jax.sharding import PartitionSpec as P

f32 = jnp.float32
bf16 = jnp.bfloat16
EPS = 1e-05
NEG = -1000000000.0
SCALE = 8 ** (-0.5)
NN = (((1,), (0,)), ((), ()))
NT = (((1,), (1,)), ((), ()))
TN = (((0,), (0,)), ((), ()))
GROUP = 4
OWN_STEP = 8
VMEM = pltpu.CompilerParams(vmem_limit_bytes=50 * 1024 * 1024)


def mm(a, b, dims=NN):
    return lax.dot_general(a, b, dims, preferred_element_type=f32)


def split(x):
    hi = x.astype(bf16)
    lo = (x - hi.astype(f32)).astype(bf16)
    return hi, lo


def split3(x):
    hi = x.astype(bf16)
    rest = x - hi.astype(f32)
    mid = rest.astype(bf16)
    lo = (rest - mid.astype(f32)).astype(bf16)
    return hi, mid, lo


def cat(parts, axis):
    return jnp.concatenate(parts, axis=axis)


def mm2(x, w, dims=NN):
    hi, lo = split(x)
    return mm(hi, w, dims) + mm(lo, w, dims)


def mm3(x, w):
    hi, mid, lo = split3(x)
    return mm(hi, w) + mm(mid, w) + mm(lo, w)


def norm_rows(x):
    center = x - jnp.mean(x, -1, keepdims=True)
    rstd = lax.rsqrt(jnp.mean(center * center, -1, keepdims=True) + EPS)
    return center * rstd, rstd


def norm_back(normed, rstd, grad):
    return rstd * (
        grad
        - jnp.mean(grad, -1, keepdims=True)
        - normed * jnp.mean(grad * normed, -1, keepdims=True)
    )


def pair2(x):
    hi, lo = split(x)
    return cat([hi, lo], 1)


def head_mask(rows, cols, row_div, col_div):
    a = lax.broadcasted_iota(jnp.int32, (rows, cols), 0) // row_div
    b = lax.broadcasted_iota(jnp.int32, (rows, cols), 1) // col_div
    return (a == b).astype(f32)


def bias_kernel(pair_ref, wb_ref, out_ref, scr):
    xn, _ = norm_rows(pair_ref[...].astype(f32).reshape(512, 128))
    scr[...] = xn.reshape(32, 16, 128)
    wbt = wb_ref[...].astype(f32).T
    w2 = cat([wbt, wbt], 1).astype(bf16)
    own = head_mask(8, 256, 1, 32)
    rows = []
    for j in range(16):
        x2 = pair2(scr[:, j, :])
        tiled = cat([x2] * 8, 0)
        full = mm(w2, tiled, NT)
        rows.append(jnp.sum(full * own, 0, keepdims=True))
    block = cat(rows, 0)
    for k in range(16):
        out_ref[k] = block


def pack_kernel(x_ref, mask_ref, res_ref, count_ref, rows_ref, own_ref):
    seq = lax.broadcasted_iota(jnp.int32, (16, 32), 0)
    alive = (seq < count_ref[0]).astype(f32)
    live = mask_ref[...].astype(f32) * res_ref[...].astype(f32) * alive
    x = x_ref[...]
    diag = head_mask(32, 32, 1, 1)
    cols = [
        jnp.broadcast_to(jnp.sum(diag * live[k:k + 1, :], 1, keepdims=True), (32, 64))[None]
        for k in range(16)
    ]
    own_ref[...] = cat([x.astype(f32), cat(cols, 0)], 2).astype(bf16)
    dense = cat([x[:, :16], x[:, 16:]], 2)
    plane = cat([live, jnp.zeros((16, 96), f32)], 1).astype(bf16)
    for k in range(8):
        rows_ref[k, 0:16] = dense
        rows_ref[k, 16] = plane


def unpack(p):
    return cat([p[:, :, :64], p[:, :, 64:]], 1).reshape(256, 64)


def proj_kernel(
    g_ref, plane_ref, own_ref, win_ref,
    k2_ref, v2_ref, kt_ref, vt_ref, q_ref, gate_ref, live_ref,
    wqg, wkvt, wkk, wvv,
):
    s = pl.program_id(0)

    @pl.when(s == 0)
    def _():
        w = win_ref[...].astype(f32)
        wt = w.T
        qg = cat([wt[0:64], wt[192:256]], 0)
        wqg[...] = cat([qg, qg], 1).astype(bf16)
        kv = wt[64:192]
        wkvt[...] = cat([kv, kv], 1).astype(bf16)
        for at, ref in ((64, wkk), (128, wvv)):
            one = w[:, at:at + 64]
            row = cat([one, one], 1)
            ref[...] = cat([row, row], 0).astype(bf16)
        live_ref[...] = cat([plane_ref[k, 0, :, 0:32] for k in range(8)], 1)

    lane = lax.broadcasted_iota(jnp.int32, (256, 128), 1)
    heads = head_mask(64, 256, 8, 32) * SCALE

    def two(x):
        hi = x.astype(bf16).astype(f32)
        return jnp.where(lane < 64, hi, x - hi).astype(bf16)

    for u in range(GROUP):
        xn, _ = norm_rows(unpack(g_ref[:, u].astype(f32)))
        x2 = pair2(xn)
        k2_ref[u] = two(mm(x2, wkk[...]))
        v2_ref[u] = two(mm(x2, wvv[...]))
        hi, lo = split(mm(wkvt[...], x2, NT))
        kt_ref[u] = cat([hi[:64], lo[:64]], 0)
        vt_ref[u] = cat([hi[64:], lo[64:]], 0)
        xon, _ = norm_rows(own_ref[u].astype(f32)[:, :64])
        qg = mm(wqg[...], cat([pair2(xon)] * 8, 0), NT)
        qhi, qlo = split(qg[:64] * heads)
        q_ref[u] = cat([qhi, qlo], 0)
        gate_ref[u] = jax.nn.sigmoid(qg[64:])


def row_fwd_kernel(
    k2_ref, vt_ref, q_ref, gate_ref, live_ref, own_ref, bias_ref, wo_ref,
    p_ref, o_ref, m1_ref, any_ref, c1_ref,
):
    s = pl.program_id(0)
    heads = head_mask(64, 256, 8, 32)
    wo = wo_ref[...]
    wo2 = cat([wo, wo], 0)
    seq = lax.broadcasted_iota(jnp.int32, (16, 128), 0)
    for u in range(GROUP):
        pick = (seq == s * GROUP + u).astype(bf16)
        live = mm(live_ref[...], pick, TN)
        k2 = k2_ref[u]
        qhi, qlo = q_ref[u, 0:64], q_ref[u, 64:128]
        logits = mm(k2, cat([qhi, qhi], 0)) + mm(k2[:, :64], qlo)
        logits = logits + bias_ref[...].reshape(256, 256)
        logits = jnp.where(cat([live, live], 1) > 0, logits, NEG)
        e = jnp.exp(logits - jnp.max(logits, 0, keepdims=True))
        p = e * (1.0 / jnp.sum(e, 0, keepdims=True))
        p_ref[u] = p
        some = jnp.max(live, 0, keepdims=True)
        any_ref[u] = jnp.broadcast_to(cat([some, some], 1), (8, 256))
        phi, plo = split(p)
        vt = vt_ref[u]
        first = mm(vt, phi)
        o = (first[:64] + first[64:] + mm(vt[:64], plo)) * heads
        o_ref[u] = o
        ahi, alo = split(o * gate_ref[u])
        y = mm(cat([ahi, alo], 0), wo2, TN)
        own = own_ref[u].astype(f32)
        m1 = own[:, :64] + jnp.sum(y.reshape(8, 32, 64), 0)
        m1_ref[u] = m1
        c1_ref[:, 0, s * GROUP + u, :] = cat([m1[:16], m1[16:]], 1)
        lv = own[:, 64:]
        c1_ref[:, 1, s * GROUP + u, :] = cat([lv[:16], lv[16:]], 1)


def diag2(w):
    z = jnp.zeros_like(w)
    return cat([cat([w, z], 1), cat([z, w], 1)], 0)


def col_kernel(c1_ref, cw_ref, out_ref):
    x = c1_ref[:, 0].reshape(256, 128)
    live = c1_ref[:, 1].reshape(256, 128)
    halves = (head_mask(128, 128, 64, 64) * (1.0 / 64)).astype(bf16)
    center = x - mm3(x, halves)
    xn = center * lax.rsqrt(mm3(center * center, halves) + EPS)
    cw = cw_ref[...].astype(f32)
    wq = diag2(cw[:, 0:64]).astype(bf16)
    wk = diag2(cw[:, 64:128]).astype(bf16)
    wv = diag2(cw[:, 128:192]).astype(bf16)
    total = jnp.sum(live * xn, 0, keepdims=True)
    count = jnp.sum(live, 0, keepdims=True)
    mean = total / jnp.maximum(count, 1.0)
    colq = mm3(jnp.broadcast_to(mean, (8, 128)), wq)[0:1] * SCALE
    kt = mm2(xn, wk)
    vt = mm2(xn, wv)
    groups = head_mask(128, 128, 8, 8).astype(bf16)
    logits = jnp.where(live > 0, mm3(kt * colq, groups), NEG)
    peak = jnp.max(logits, 0, keepdims=True)
    e = jnp.exp(logits - peak)
    den = jnp.sum(e, 0, keepdims=True)
    w = e / den
    wv_ = w * vt
    attended = jnp.sum(wv_, 0, keepdims=True)
    khi, klo = split(kt)

    def by_key(z):
        zhi, zlo = split(z)
        full = mm(khi, zhi, TN) + mm(klo, zhi, TN) + mm(khi, zlo, TN)
        lane = lax.broadcasted_iota(jnp.int32, (8, 128), 1)
        return jnp.where(lane < 64, full[0:8], full[64:72])

    lt = live.T
    rows = [
        by_key(wv_), by_key(w), attended, peak, den, colq, count, count, count, count,
        lt[0:1, :128], lt[0:1, 128:], lt[64:65, :128], lt[64:65, 128:],
        count, count, count, count,
    ]
    block = cat(rows, 0)
    for k in range(16):
        out_ref[k] = block


def unpair(x):
    return cat([x[:, 0:64], x[:, 64:128]], 0)


def spread(v):
    return jnp.broadcast_to(v[None], (16, 32, 64)).reshape(512, 64)


def factor_kernel(m1_ref, c2_ref, own_ref, cw_ref, wv_ref, wt_ref, m2_ref, d_ref):
    m1 = m1_ref[...].reshape(512, 64)
    live = own_ref[...].reshape(512, 128)[:, 64:].astype(f32)
    attended = unpair(c2_ref[:, 16, :])
    xn, _ = norm_rows(m1)
    gate = jax.nn.sigmoid(mm2(xn, cw_ref[:, 192:256]))
    m2 = m1 + mm2(gate * spread(attended), wv_ref[...])
    m2_ref[...] = m2.reshape(16, 32, 64)
    xn2, _ = norm_rows(m2)
    lr = live * mm2(xn2, wt_ref[...])
    lr = lr.reshape(16, 32, 64)
    lr = cat([lr[:, :16], lr[:, 16:]], 2).astype(bf16)
    lt = [c2_ref[:, 24 + k, :].astype(bf16) for k in range(4)]
    for k in range(8):
        d_ref[k, 0:16] = lr
        for q in range(4):
            d_ref[k, 16 + q] = lt[q]


def masks_by_row(p):
    low = cat([p[:, 0], p[:, 1]], 2)
    high = cat([p[:, 2], p[:, 3]], 2)
    return cat([low, high], 1)


def outer_kernel(
    core_ref, da_ref, own_ref, cta_ref, ctb_ref, cta2_ref, ctb2_ref, w_ref, m2_ref, c2_ref, m1_ref,
    ownx_ref, adj_ref, cw_ref, wv_ref, wt_ref, g2_ref, dcg_ref, e1_ref,
    inv, turned, stage, res, lrs, wide, wf,
):
    step = pl.program_id(0)
    core = core_ref[0]

    @pl.when(step == 0)
    def _():
        every = masks_by_row(da_ref[:, 16:20]).reshape(256, 256)
        mine = masks_by_row(own_ref[:, 16:20]).reshape(32, 256)
        value = 1.0 / jnp.maximum(mm(every, mine, NT), 1.0)
        for k in range(32):
            inv[k] = jnp.broadcast_to(value[:, k:k + 1], (256, 128))
        for s in range(16):
            piece = unpack(da_ref[:, s].astype(f32)).T
            for half in range(2):
                cols = piece[:, 128 * half:128 * half + 128]
                lrs[half, pl.ds(s, 32, stride=16), :] = cols[0:32]
                lrs[half, pl.ds(512 + s, 32, stride=16), :] = cols[32:64]
        for half in range(2):
            turned[0, :, 128 * half:128 * half + 128] = lrs[half, 512:1024].astype(bf16)
            turned[1, :, 128 * half:128 * half + 128] = lrs[half, 0:512].astype(bf16)
        wf[...] = w_ref[...].astype(f32)
        for k in range(32):
            first = wf[pl.ds(k, 32, stride=32), :].astype(bf16)
            second = w_ref[32 * k:32 * k + 32]
            for part in range(2):
                wide[0, :, 256 * k + 128 * part:256 * k + 128 * part + 128] = first
                wide[1, :, 256 * k + 128 * part:256 * k + 128 * part + 128] = second

    for side in range(2):
        for k in range(OWN_STEP):
            if side == 0:
                one = step * OWN_STEP + k
                x = cta_ref[:, 0, k].astype(f32)
                y = cta2_ref[:, 0, k].astype(f32)
                ct = cat([jnp.where(core == 0, x, y), jnp.where(core == 0, y, x)], 1)
            else:
                slot, at = k // (OWN_STEP // 2), k % (OWN_STEP // 2)
                one = (slot + core) % 2 * 16 + step * (OWN_STEP // 2) + at
                ct = (ctb_ref if slot == 0 else ctb2_ref)[:, 0, at].astype(f32)
            hi, lo = split(ct.reshape(256, 128) * inv[one])
            both = mm(turned[side], cat([hi, lo], 1))
            uhi, ulo = split(both[:, :128] + both[:, 128:])
            rows = pl.ds(pl.multiple_of(one * 16, 16), 16)
            for b in range(32):
                stage[side, rows, 256 * b:256 * b + 128] = uhi[16 * b:16 * b + 16]
                stage[side, rows, 256 * b + 128:256 * b + 256] = ulo[16 * b:16 * b + 16]

    @pl.when(step == 32 // OWN_STEP - 1)
    def _():
        grads = []
        for side in range(2):
            res[:, 0:32] = mm(stage[side], wide[side], NT)
            grads.append(cat([res[pl.ds(s, 32, stride=16), :] for s in range(16)], 0)[:, 0:32])
        lv = ownx_ref[...].reshape(512, 128)[:, 64:].astype(f32)
        dlr = cat(grads, 1) * lv
        m2 = m2_ref[...].reshape(512, 64)
        xn2, rstd2 = norm_rows(m2)
        adj = adj_ref[...].reshape(512, 64).astype(f32)
        g2 = adj + norm_back(xn2, rstd2, mm2(dlr, wt_ref[...], NT))
        g2_ref[...] = g2.reshape(16, 32, 64)
        xn, _ = norm_rows(m1_ref[...].reshape(512, 64))
        gate = jax.nn.sigmoid(mm2(xn, cw_ref[:, 192:256]))
        dmix = mm2(g2, wv_ref[...], NT)
        attended = spread(unpair(c2_ref[:, 16, :]))
        dcg_ref[...] = (dmix * attended * gate * (1.0 - gate)).reshape(16, 32, 64)
        da = jnp.sum((gate * dmix).reshape(16, 32, 64), 0)
        packed = cat([da[:16], da[16:]], 1)
        for k in range(16):
            e1_ref[k] = packed


def row_bwd_kernel(
    e1_ref, c2_ref, m1_ref, own_ref, g2_ref, dcg_ref, cw_ref,
    p_ref, o_ref, v2_ref, gate_ref, any_ref, wo_ref,
    g1_ref, ds_ref, do_ref, dg_ref, bias_ref,
    g1s,
):
    s = pl.program_id(0)

    @pl.when(s == 0)
    def _():
        cw = cw_ref[...]
        groups = head_mask(64, 64, 8, 8).astype(bf16)
        da = jnp.sum(e1_ref[...], 0)
        da = unpair(da)
        attended = unpair(c2_ref[:, 16, :])
        peak = unpair(c2_ref[:, 17, :])
        den = unpair(c2_ref[:, 18, :])
        colq = unpair(c2_ref[:, 19, :])
        count = unpair(c2_ref[:, 20, :])
        delta = mm3(da * attended, groups)
        feature = lax.broadcasted_iota(jnp.int32, (32, 64), 1) % 8
        dq = jnp.zeros((32, 64), f32)
        for k in range(8):
            z = mm3(da * unpair(c2_ref[:, k, :]), groups) - delta * unpair(c2_ref[:, 8 + k, :])
            dq = dq + jnp.where(feature == k, z, 0.0)
        dtotal = mm2(dq * SCALE, cw[:, 0:64], NT) / jnp.maximum(count, 1.0)
        live = own_ref[...].reshape(512, 128)[:, 64:].astype(f32)
        xn, rstd = norm_rows(m1_ref[...].reshape(512, 64))
        kt = mm2(xn, cw[:, 64:128])
        vt = mm2(xn, cw[:, 128:192])
        qs = spread(colq)
        logits = jnp.where(live > 0, mm3(kt * qs, groups), NEG)
        weights = jnp.exp(logits - spread(peak)) / spread(den)
        das = spread(da)
        dl = weights * (mm2(vt * das, groups) - spread(delta)) * live
        dxn = (
            mm2(dcg_ref[...].reshape(512, 64), cw[:, 192:256], NT)
            + mm2(dl * qs, cw[:, 64:128], NT)
            + mm2(weights * das, cw[:, 128:192], NT)
            + live * spread(dtotal)
        )
        g1 = g2_ref[...].reshape(512, 64) + norm_back(xn, rstd, dxn)
        g1s[...] = g1.reshape(16, 32, 64)
        bias_ref[...] = jnp.zeros_like(bias_ref)

    heads = head_mask(64, 256, 8, 32)
    wo = wo_ref[...]
    wo2 = cat([wo, wo], 1)
    for u in range(GROUP):
        dm = g1s[s * GROUP + u]
        g1_ref[u] = dm
        o = o_ref[u]
        v2 = v2_ref[u]
        gate = gate_ref[u]
        dout = mm(wo2, cat([pair2(dm)] * 8, 0), NT)
        hi, lo = split(dout * o * gate * (1.0 - gate))
        dg_ref[u] = cat([hi, lo], 0)
        do = dout * gate * heads
        hi, lo = split(do)
        do_ref[u] = cat([hi, lo], 0)
        do_live = do * any_ref[u, 0:1, :]
        delta = jnp.sum(do_live * o, 0, keepdims=True)
        lhi, llo = split(do_live)
        dp = mm(v2, cat([lhi, lhi], 0)) + mm(v2[:, :64], llo)
        ds = p_ref[u] * (dp - delta)
        bias_ref[...] += ds.reshape(16, 16, 256)
        shi, slo = split(ds)
        ds_ref[u, :, 0:256] = shi
        ds_ref[u, :, 256:512] = slo


def row_inputs_kernel(
    p_ref, ds_ref, do_ref, dg_ref, q_ref, kt_ref, win_ref, dxo_ref, f_ref, wback, wown
):
    @pl.when(pl.program_id(0) == 0)
    def _():
        wt = win_ref[...].astype(f32).T
        qg = cat([wt[0:64], wt[192:256]], 0)
        wback[...] = cat([wt[64:128], wt[64:128], wt[128:192], wt[128:192]], 0).astype(bf16)
        wown[...] = cat([qg, qg], 0).astype(bf16)

    heads = head_mask(64, 256, 8, 32) * SCALE
    zero = jnp.zeros((64, 256), bf16)
    for u in range(GROUP):
        shi, slo = ds_ref[u, :, 0:256], ds_ref[u, :, 256:512]
        kt = kt_ref[u]
        q = q_ref[u]
        do = do_ref[u]
        dg = dg_ref[u]
        first = mm(kt, shi)
        dq = (first[:64] + first[64:] + mm(kt[:64], slo)) * heads
        dk = mm(shi, q, NT) + mm(slo, cat([q[:64], zero], 0), NT)
        phi, plo = split(p_ref[u])
        dv = mm(phi, do, NT) + mm(plo, cat([do[:64], zero], 0), NT)
        dx = mm2(cat([dk, dv], 1), wback[...]).reshape(8, 32, 64)
        f_ref[:, u] = cat([dx[:, :16], dx[:, 16:]], 2)
        qhi, qlo = split(dq)
        dxo = mm(cat([qhi, dg[:64], qlo, dg[64:]], 0), wown[...], TN)
        dxo_ref[u] = jnp.sum(dxo.reshape(8, 32, 64), 0)


def final_rows_kernel(f_ref, dxo_ref, g1_ref, own_ref, out_ref):
    total = jnp.sum(f_ref[...], 0)
    total = cat([total[:, :, :64], total[:, :, 64:]], 1).reshape(512, 64)
    total = total + dxo_ref[...].reshape(512, 64)
    xn, rstd = norm_rows(own_ref[...].reshape(512, 128)[:, :64].astype(f32))
    out = g1_ref[...].reshape(512, 64) + norm_back(xn, rstd, total)
    out_ref[...] = out.reshape(16, 32, 64)


def final_pair_kernel(b_ref, pair_ref, wb_ref, ct_ref, out_ref, scr):
    total = jnp.sum(b_ref[...], 0)
    wbt = wb_ref[...].astype(f32).T
    w2 = cat([wbt, wbt], 0).astype(bf16)
    own = head_mask(8, 256, 1, 32)
    for j in range(16):
        wide = jnp.broadcast_to(total[j:j + 1, :], (8, 256)) * own
        hi, lo = split(wide)
        y = mm(cat([hi, lo], 0), w2, TN)
        scr[:, j, :] = jnp.sum(y.reshape(8, 32, 128), 0)
    xn, rstd = norm_rows(pair_ref[...].reshape(512, 128).astype(f32))
    out = norm_back(xn, rstd, scr[...].reshape(512, 128)) + ct_ref[...].reshape(512, 128).astype(f32)
    out_ref[...] = out.reshape(32, 16, 128)


def sds(shape, dtype=f32):
    return jax.ShapeDtypeStruct(shape, dtype)


def full(shape):
    zeros = (0,) * len(shape)
    return pl.BlockSpec(shape, lambda s: zeros)


def row(shape):
    rest = (0,) * (len(shape) - 1)
    return pl.BlockSpec((GROUP,) + shape[1:], lambda s: (s,) + rest)


def whole_call(kernel, out_shape, *args, scratch=()):
    return pl.pallas_call(
        kernel, out_shape=out_shape, scratch_shapes=list(scratch), compiler_params=VMEM
    )(*args)


def project(rows, own, win):
    return pl.pallas_call(
        proj_kernel,
        grid=(16 // GROUP,),
        in_specs=[
            pl.BlockSpec((8, GROUP, 16, 128), lambda s: (0, s, 0, 0)),
            pl.BlockSpec((8, 1, 16, 128), lambda s: (0, 16, 0, 0)),
            row((16, 32, 128)), full((64, 256)),
        ],
        out_specs=[
            row((16, 256, 128)), row((16, 256, 128)), row((16, 128, 256)), row((16, 128, 256)),
            row((16, 128, 256)), row((16, 64, 256)), full((16, 256)),
        ],
        out_shape=[
            sds((16, 256, 128), bf16), sds((16, 256, 128), bf16), sds((16, 128, 256), bf16),
            sds((16, 128, 256), bf16), sds((16, 128, 256), bf16), sds((16, 64, 256)),
            sds((16, 256), bf16),
        ],
        scratch_shapes=[
            pltpu.VMEM((128, 128), bf16), pltpu.VMEM((128, 128), bf16),
            pltpu.VMEM((128, 128), bf16), pltpu.VMEM((128, 128), bf16),
        ],
        compiler_params=VMEM,
    )(rows, rows, own, win)


def row_forward(k2, vt, q, gate, live, own, bias, wo):
    return pl.pallas_call(
        row_fwd_kernel,
        grid=(16 // GROUP,),
        in_specs=[
            row((16, 256, 128)), row((16, 128, 256)), row((16, 128, 256)), row((16, 64, 256)),
            full((16, 256)), row((16, 32, 128)), full((16, 16, 256)), full((64, 64)),
        ],
        out_specs=[
            row((16, 256, 256)), row((16, 64, 256)), row((16, 32, 64)), row((16, 8, 256)),
            full((16, 2, 16, 128)),
        ],
        out_shape=[
            sds((16, 256, 256)), sds((16, 64, 256)), sds((16, 32, 64)), sds((16, 8, 256)),
            sds((16, 2, 16, 128)),
        ],
        compiler_params=VMEM,
    )(k2, vt, q, gate, live, own, bias, wo)


def outer_product(core, ct, ct2, factors, dblock, w, m2, c2, m1, own, adj, cw, wvo, wtf):
    half = OWN_STEP // 2
    one = pl.BlockSpec((8, 1, OWN_STEP, 16, 128), lambda s: (0, 0, s, 0, 0))
    two = pl.BlockSpec((8, 1, half, 32, 128), lambda s: (0, 1, s, 0, 0))
    return pl.pallas_call(
        outer_kernel,
        grid=(32 // OWN_STEP,),
        in_specs=[
            pl.BlockSpec(memory_space=pltpu.SMEM),
            full((8, 20, 16, 128)),
            pl.BlockSpec((1, 20, 16, 128), lambda s: (0, 0, 0, 0)),
            one, two, one, two,
            full((1024, 128)),
            full((16, 32, 64)), full((16, 32, 128)), full((16, 32, 64)), full((16, 32, 128)),
            full((16, 32, 64)), full((64, 256)), full((64, 64)), full((64, 64)),
        ],
        out_specs=[full((16, 32, 64)), full((16, 32, 64)), full((16, 16, 128))],
        out_shape=[sds((16, 32, 64)), sds((16, 32, 64)), sds((16, 16, 128))],
        scratch_shapes=[
            pltpu.VMEM((32, 256, 128), f32),
            pltpu.VMEM((2, 512, 256), bf16),
            pltpu.VMEM((2, 512, 8192), bf16),
            pltpu.VMEM((512, 128), f32),
            pltpu.VMEM((2, 1024, 128), f32),
            pltpu.VMEM((2, 32, 8192), bf16),
            pltpu.VMEM((1024, 128), f32),
        ],
        compiler_params=VMEM,
    )(
        core, factors, dblock, ct.reshape(8, 2, 32, 16, 128), ct.reshape(8, 2, 16, 32, 128),
        ct2.reshape(8, 2, 32, 16, 128), ct2.reshape(8, 2, 16, 32, 128), w, m2, c2, m1, own, adj,
        cw, wvo, wtf,
    )


def row_backward(e1, c2, m1, own, g2, dcg, cw, p, o, v2, gate, any_live, wo):
    return pl.pallas_call(
        row_bwd_kernel,
        grid=(16 // GROUP,),
        in_specs=[
            full((16, 16, 128)), full((16, 32, 128)), full((16, 32, 64)), full((16, 32, 128)),
            full((16, 32, 64)), full((16, 32, 64)), full((64, 256)),
            row((16, 256, 256)), row((16, 64, 256)), row((16, 256, 128)), row((16, 64, 256)),
            row((16, 8, 256)), full((64, 64)),
        ],
        out_specs=[
            row((16, 32, 64)), row((16, 256, 512)), row((16, 128, 256)), row((16, 128, 256)),
            full((16, 16, 256)),
        ],
        out_shape=[
            sds((16, 32, 64)), sds((16, 256, 512), bf16), sds((16, 128, 256), bf16),
            sds((16, 128, 256), bf16), sds((16, 16, 256)),
        ],
        scratch_shapes=[pltpu.VMEM((16, 32, 64), f32)],
        compiler_params=VMEM,
    )(e1, c2, m1, own, g2, dcg, cw, p, o, v2, gate, any_live, wo)


def row_inputs(p, ds, do, dg, q, kt, win):
    return pl.pallas_call(
        row_inputs_kernel,
        grid=(16 // GROUP,),
        in_specs=[
            row((16, 256, 256)), row((16, 256, 512)), row((16, 128, 256)), row((16, 128, 256)),
            row((16, 128, 256)), row((16, 128, 256)), full((64, 256)),
        ],
        out_specs=[row((16, 32, 64)), pl.BlockSpec((8, GROUP, 16, 128), lambda s: (0, s, 0, 0))],
        out_shape=[sds((16, 32, 64)), sds((8, 16, 16, 128))],
        scratch_shapes=[pltpu.VMEM((256, 64), bf16), pltpu.VMEM((256, 64), bf16)],
        compiler_params=VMEM,
    )(p, ds, do, dg, q, kt, win)


def body(
    alignment_state,
    pairwise_state,
    alignment_mask,
    residue_entry_mask,
    sequence_live_count,
    horizontal_intake_coefs,
    pairwise_bias_weights,
    horizontal_readout_coefs,
    column_input_weights,
    vertical_readout_coefs,
    tensor_factor_coefs,
    outer_output_weights,
    adjoint_of_result_track,
    pairwise_cotangent,
):
    smem = pl.BlockSpec(memory_space=pltpu.SMEM)
    vmem = pl.BlockSpec(memory_space=pltpu.VMEM)
    row_block, own = pl.pallas_call(
        pack_kernel,
        in_specs=[vmem, vmem, vmem, smem],
        out_shape=[sds((8, 17, 16, 128), bf16), sds((16, 32, 128), bf16)],
        compiler_params=VMEM,
    )(alignment_state, alignment_mask, residue_entry_mask.reshape(1, 32), sequence_live_count)
    rows = lax.all_to_all(row_block, "res", 0, 0)
    bias_block = whole_call(
        bias_kernel, sds((16, 16, 256)), pairwise_state, pairwise_bias_weights,
        scratch=[pltpu.VMEM((32, 16, 128), f32)],
    )
    cw = cat(
        [
            column_input_weights[:, :64],
            jnp.tile(column_input_weights[:, 64:72], (1, 8)),
            jnp.tile(column_input_weights[:, 72:80], (1, 8)),
            column_input_weights[:, 80:],
        ],
        1,
    )

    turned = pairwise_cotangent.transpose(1, 0, 2)
    perm = [(d * 8 + r, (2 * r + d % 2) * 8 + d // 2) for d in range(16) for r in range(8)]
    turned = lax.ppermute(turned, ("depth", "res"), perm)
    both = cat([pairwise_cotangent.reshape(512, 128), turned.reshape(512, 128)], 0)
    both = jnp.broadcast_to(both[None], (8, 1024, 128))

    bias_block, rows = lax.optimization_barrier((bias_block, rows))
    bias = lax.all_to_all(bias_block, "depth", 0, 0)
    k2, v2, kt, vt, q, gate, live = project(rows, own, horizontal_intake_coefs)
    bias, both = lax.optimization_barrier((bias, both))
    same_core = [[c + 2 * k for k in range(8)] for c in range(2)]
    ct = lax.all_to_all(both, "depth", 0, 0, axis_index_groups=same_core)
    p, o, m1, any_live, c1 = row_forward(
        k2, vt, q, gate, live, own, bias, horizontal_readout_coefs
    )
    c1, ct = lax.optimization_barrier((c1, ct))
    ct2 = lax.ppermute(ct, "depth", [(d, d ^ 1) for d in range(16)])
    c1 = lax.all_to_all(c1, "depth", 0, 0)
    c2 = whole_call(col_kernel, sds((16, 32, 128)), c1, cw)
    c2 = lax.all_to_all(c2, "depth", 0, 0)
    m2, dblock = whole_call(
        factor_kernel, [sds((16, 32, 64)), sds((8, 20, 16, 128), bf16)],
        m1, c2, own, cw, vertical_readout_coefs, tensor_factor_coefs,
    )
    factors = lax.all_to_all(dblock, "res", 0, 0)
    core = (lax.axis_index("depth") % 2).astype(jnp.int32).reshape(1)
    g2, dcg, e1 = outer_product(
        core, ct, ct2, factors, dblock, outer_output_weights, m2, c2, m1, own,
        adjoint_of_result_track, cw, vertical_readout_coefs, tensor_factor_coefs,
    )
    e1 = lax.all_to_all(e1, "depth", 0, 0)
    g1, ds, do, dg, bblock = row_backward(
        e1, c2, m1, own, g2, dcg, cw, p, o, v2, gate, any_live, horizontal_readout_coefs
    )
    bsum = lax.all_to_all(bblock, "depth", 0, 0)
    dxo, fblock = row_inputs(p, ds, do, dg, q, kt, horizontal_intake_coefs)
    fblock, bsum = lax.optimization_barrier((fblock, bsum))
    fsum = lax.all_to_all(fblock, "res", 0, 0)
    alignment_gradient = whole_call(final_rows_kernel, sds((16, 32, 64)), fsum, dxo, g1, own)
    pair_grad = whole_call(
        final_pair_kernel, sds((32, 16, 128)), bsum, pairwise_state, pairwise_bias_weights,
        pairwise_cotangent, scratch=[pltpu.VMEM((32, 16, 128), f32)],
    )
    return alignment_gradient, pair_grad


def solution(mesh):
    in_specs = (
        P("depth", "res", None),
        P("res", "depth", None),
        P("depth", "res"),
        P("res"),
        P("depth"),
        P(),
        P(),
        P(),
        P(),
        P(),
        P(),
        P(),
        P("depth", "res", None),
        P("res", "depth", None),
    )
    out_specs = (P("depth", "res", None), P("res", "depth", None))
    return jax.shard_map(body, mesh=mesh, in_specs=in_specs, out_specs=out_specs, check_vma=False)
```

```python
import jax
import jax.numpy as jnp
from jax import lax
from jax.experimental import pallas as pl
from jax.experimental.pallas import tpu as pltpu
from jax.sharding import PartitionSpec as P

f32 = jnp.float32
bf16 = jnp.bfloat16
EPS = 1e-05
NEG = -1000000000.0
SCALE = 8 ** (-0.5)
NN = (((1,), (0,)), ((), ()))
NT = (((1,), (1,)), ((), ()))
TN = (((0,), (0,)), ((), ()))
GROUP = 4
SMEM = pl.BlockSpec(memory_space=pltpu.SMEM)
OWN_STEP = 8
VMEM = pltpu.CompilerParams(vmem_limit_bytes=50 * 1024 * 1024)


def mm(a, b, dims=NN):
    return lax.dot_general(a, b, dims, preferred_element_type=f32)


def split(x):
    hi = x.astype(bf16)
    lo = (x - hi.astype(f32)).astype(bf16)
    return hi, lo


def split3(x):
    hi = x.astype(bf16)
    rest = x - hi.astype(f32)
    mid = rest.astype(bf16)
    lo = (rest - mid.astype(f32)).astype(bf16)
    return hi, mid, lo


def cat(parts, axis):
    return jnp.concatenate(parts, axis=axis)


def mm2(x, w, dims=NN):
    hi, lo = split(x)
    return mm(hi, w, dims) + mm(lo, w, dims)


def mm3(x, w):
    hi, mid, lo = split3(x)
    return mm(hi, w) + mm(mid, w) + mm(lo, w)


def norm_rows(x):
    center = x - jnp.mean(x, -1, keepdims=True)
    rstd = lax.rsqrt(jnp.mean(center * center, -1, keepdims=True) + EPS)
    return center * rstd, rstd


def norm_back(normed, rstd, grad):
    return rstd * (
        grad
        - jnp.mean(grad, -1, keepdims=True)
        - normed * jnp.mean(grad * normed, -1, keepdims=True)
    )


def pair2(x):
    hi, lo = split(x)
    return cat([hi, lo], 1)


def head_mask(rows, cols, row_div, col_div):
    a = lax.broadcasted_iota(jnp.int32, (rows, cols), 0) // row_div
    b = lax.broadcasted_iota(jnp.int32, (rows, cols), 1) // col_div
    return (a == b).astype(f32)


def bias_kernel(pair_ref, wb_ref, out_ref, scr):
    xn, _ = norm_rows(pair_ref[...].astype(f32).reshape(512, 128))
    scr[...] = xn.reshape(32, 16, 128)
    wbt = wb_ref[...].astype(f32).T
    w2 = cat([wbt, wbt], 1).astype(bf16)
    own = head_mask(8, 256, 1, 32)
    rows = []
    for j in range(16):
        x2 = pair2(scr[:, j, :])
        tiled = cat([x2] * 8, 0)
        full = mm(w2, tiled, NT)
        rows.append(jnp.sum(full * own, 0, keepdims=True))
    block = cat(rows, 0)
    for k in range(16):
        out_ref[k] = block


def res_order(place_ref):
    return [jnp.bitwise_xor(place_ref[1], k) for k in range(8)]


def pack_kernel(x_ref, mask_ref, res_ref, count_ref, rows_ref, own_ref):
    seq = lax.broadcasted_iota(jnp.int32, (16, 32), 0)
    alive = (seq < count_ref[0]).astype(f32)
    live = mask_ref[...].astype(f32) * res_ref[...].astype(f32) * alive
    x = x_ref[...]
    diag = head_mask(32, 32, 1, 1)
    cols = [
        jnp.broadcast_to(jnp.sum(diag * live[k:k + 1, :], 1, keepdims=True), (32, 64))[None]
        for k in range(16)
    ]
    own_ref[...] = cat([x.astype(f32), cat(cols, 0)], 2).astype(bf16)
    dense = cat([x[:, :16], x[:, 16:]], 2)
    plane = cat([live, jnp.zeros((16, 96), f32)], 1).astype(bf16)
    rows_ref[0:16] = dense
    rows_ref[16] = plane


def unpack(p):
    return cat([p[:, :, :64], p[:, :, 64:]], 1).reshape(256, 64)


def turn_kernel(ct_ref, turned_ref, out_ref):
    for k in range(8):
        out_ref[k, 0:512] = ct_ref[...].reshape(512, 128)
        out_ref[k, 512:1024] = turned_ref[...].reshape(512, 128)


def proj_kernel(*refs):
    g_refs, plane_refs = refs[0:8], refs[8:16]
    own_ref, win_ref, k2_ref, v2_ref, kt_ref, vt_ref, q_ref, gate_ref, live_ref = refs[16:25]
    wqg, wkvt, wkk, wvv = refs[25:]
    s = pl.program_id(0)

    @pl.when(s == 0)
    def _():
        w = win_ref[...].astype(f32)
        wt = w.T
        qg = cat([wt[0:64], wt[192:256]], 0)
        wqg[...] = cat([qg, qg], 1).astype(bf16)
        kv = wt[64:192]
        wkvt[...] = cat([kv, kv], 1).astype(bf16)
        for at, ref in ((64, wkk), (128, wvv)):
            one = w[:, at:at + 64]
            row = cat([one, one], 1)
            ref[...] = cat([row, row], 0).astype(bf16)
        live_ref[...] = cat([ref[0, :, 0:32] for ref in plane_refs], 1)

    lane = lax.broadcasted_iota(jnp.int32, (256, 128), 1)
    heads = head_mask(64, 256, 8, 32) * SCALE

    def two(x):
        hi = x.astype(bf16).astype(f32)
        return jnp.where(lane < 64, hi, x - hi).astype(bf16)

    for u in range(GROUP):
        xn, _ = norm_rows(unpack(cat([ref[u][None] for ref in g_refs], 0).astype(f32)))
        x2 = pair2(xn)
        k2_ref[u] = two(mm(x2, wkk[...]))
        v2_ref[u] = two(mm(x2, wvv[...]))
        hi, lo = split(mm(wkvt[...], x2, NT))
        kt_ref[u] = cat([hi[:64], lo[:64]], 0)
        vt_ref[u] = cat([hi[64:], lo[64:]], 0)
        xon, _ = norm_rows(own_ref[u].astype(f32)[:, :64])
        qg = mm(wqg[...], cat([pair2(xon)] * 8, 0), NT)
        qhi, qlo = split(qg[:64] * heads)
        q_ref[u] = cat([qhi, qlo], 0)
        gate_ref[u] = jax.nn.sigmoid(qg[64:])


def row_fwd_kernel(
    place_ref, k2_ref, vt_ref, q_ref, gate_ref, live_ref, own_ref, bias_ref, wo_ref,
    p_ref, o_ref, m1_ref, any_ref, c1_ref,
):
    s = pl.program_id(0)
    heads = head_mask(64, 256, 8, 32)
    wo = wo_ref[...]
    wo2 = cat([wo, wo], 0)
    seq = lax.broadcasted_iota(jnp.int32, (16, 128), 0)
    bias = cat([bias_ref[pl.ds(2 * at, 2)].reshape(32, 256) for at in res_order(place_ref)], 0)
    for u in range(GROUP):
        pick = (seq == s * GROUP + u).astype(bf16)
        live = mm(live_ref[...], pick, TN)
        k2 = k2_ref[u]
        qhi, qlo = q_ref[u, 0:64], q_ref[u, 64:128]
        logits = mm(k2, cat([qhi, qhi], 0)) + mm(k2[:, :64], qlo)
        logits = logits + bias
        logits = jnp.where(cat([live, live], 1) > 0, logits, NEG)
        e = jnp.exp(logits - jnp.max(logits, 0, keepdims=True))
        p = e * (1.0 / jnp.sum(e, 0, keepdims=True))
        p_ref[u] = p
        some = jnp.max(live, 0, keepdims=True)
        any_ref[u] = jnp.broadcast_to(cat([some, some], 1), (8, 256))
        phi, plo = split(p)
        vt = vt_ref[u]
        first = mm(vt, phi)
        o = (first[:64] + first[64:] + mm(vt[:64], plo)) * heads
        o_ref[u] = o
        ahi, alo = split(o * gate_ref[u])
        y = mm(cat([ahi, alo], 0), wo2, TN)
        own = own_ref[u].astype(f32)
        m1 = own[:, :64] + jnp.sum(y.reshape(8, 32, 64), 0)
        m1_ref[u] = m1
        c1_ref[:, 0, s * GROUP + u, :] = cat([m1[:16], m1[16:]], 1)
        lv = own[:, 64:]
        c1_ref[:, 1, s * GROUP + u, :] = cat([lv[:16], lv[16:]], 1)


def diag2(w):
    z = jnp.zeros_like(w)
    return cat([cat([w, z], 1), cat([z, w], 1)], 0)


def col_kernel(c1_ref, cw_ref, out_ref):
    x = c1_ref[:, 0].reshape(256, 128)
    live = c1_ref[:, 1].reshape(256, 128)
    halves = (head_mask(128, 128, 64, 64) * (1.0 / 64)).astype(bf16)
    center = x - mm3(x, halves)
    xn = center * lax.rsqrt(mm3(center * center, halves) + EPS)
    cw = cw_ref[...].astype(f32)
    wq = diag2(cw[:, 0:64]).astype(bf16)
    wk = diag2(cw[:, 64:128]).astype(bf16)
    wv = diag2(cw[:, 128:192]).astype(bf16)
    total = jnp.sum(live * xn, 0, keepdims=True)
    count = jnp.sum(live, 0, keepdims=True)
    mean = total / jnp.maximum(count, 1.0)
    colq = mm3(jnp.broadcast_to(mean, (8, 128)), wq)[0:1] * SCALE
    kt = mm2(xn, wk)
    vt = mm2(xn, wv)
    groups = head_mask(128, 128, 8, 8).astype(bf16)
    logits = jnp.where(live > 0, mm3(kt * colq, groups), NEG)
    peak = jnp.max(logits, 0, keepdims=True)
    e = jnp.exp(logits - peak)
    den = jnp.sum(e, 0, keepdims=True)
    w = e / den
    wv_ = w * vt
    attended = jnp.sum(wv_, 0, keepdims=True)
    khi, klo = split(kt)

    def by_key(z):
        zhi, zlo = split(z)
        full = mm(khi, zhi, TN) + mm(klo, zhi, TN) + mm(khi, zlo, TN)
        lane = lax.broadcasted_iota(jnp.int32, (8, 128), 1)
        return jnp.where(lane < 64, full[0:8], full[64:72])

    lt = live.T
    rows = [
        by_key(wv_), by_key(w), attended, peak, den, colq, count, count, count, count,
        lt[0:1, :128], lt[0:1, 128:], lt[64:65, :128], lt[64:65, 128:],
        count, count, count, count,
    ]
    block = cat(rows, 0)
    for k in range(16):
        out_ref[k] = block


def unpair(x):
    return cat([x[:, 0:64], x[:, 64:128]], 0)


def spread(v):
    return jnp.broadcast_to(v[None], (16, 32, 64)).reshape(512, 64)


def factor_kernel(m1_ref, c2_ref, own_ref, cw_ref, wv_ref, wt_ref, m2_ref, d_ref):
    m1 = m1_ref[...].reshape(512, 64)
    live = own_ref[...].reshape(512, 128)[:, 64:].astype(f32)
    attended = unpair(c2_ref[:, 16, :])
    xn, _ = norm_rows(m1)
    gate = jax.nn.sigmoid(mm2(xn, cw_ref[:, 192:256]))
    m2 = m1 + mm2(gate * spread(attended), wv_ref[...])
    m2_ref[...] = m2.reshape(16, 32, 64)
    xn2, _ = norm_rows(m2)
    lr = live * mm2(xn2, wt_ref[...])
    lr = lr.reshape(16, 32, 64)
    lr = cat([lr[:, :16], lr[:, 16:]], 2).astype(bf16)
    lt = [c2_ref[:, 24 + k, :].astype(bf16) for k in range(4)]
    for k in range(8):
        d_ref[k, 0:16] = lr
        for q in range(4):
            d_ref[k, 16 + q] = lt[q]


def masks_by_row(p):
    low = cat([p[:, 0], p[:, 1]], 2)
    high = cat([p[:, 2], p[:, 3]], 2)
    return cat([low, high], 1)


def outer_kernel(
    place_ref, da_ref, own_ref, cta_ref, ctb_ref, cta2_ref, ctb2_ref, w_ref, m2_ref, c2_ref, m1_ref,
    ownx_ref, adj_ref, cw_ref, wv_ref, wt_ref, g2_ref, dcg_ref, e1_ref,
    inv, turned, stage, res, lrs, wide, wf,
):
    step = pl.program_id(0)
    core = place_ref[0] % 2

    @pl.when(step == 0)
    def _():
        every = masks_by_row(da_ref[:, 16:20]).reshape(256, 256)
        mine = masks_by_row(own_ref[:, 16:20]).reshape(32, 256)
        value = 1.0 / jnp.maximum(mm(every, mine, NT), 1.0)
        for k in range(32):
            inv[k] = jnp.broadcast_to(value[:, k:k + 1], (256, 128))
        for s in range(16):
            piece = unpack(da_ref[:, s].astype(f32)).T
            for half in range(2):
                cols = piece[:, 128 * half:128 * half + 128]
                lrs[half, pl.ds(s, 32, stride=16), :] = cols[0:32]
                lrs[half, pl.ds(512 + s, 32, stride=16), :] = cols[32:64]
        for half in range(2):
            turned[0, :, 128 * half:128 * half + 128] = lrs[half, 512:1024].astype(bf16)
            turned[1, :, 128 * half:128 * half + 128] = lrs[half, 0:512].astype(bf16)
        wf[...] = w_ref[...].astype(f32)
        for k in range(32):
            first = wf[pl.ds(k, 32, stride=32), :].astype(bf16)
            second = w_ref[32 * k:32 * k + 32]
            for part in range(2):
                wide[0, :, 256 * k + 128 * part:256 * k + 128 * part + 128] = first
                wide[1, :, 256 * k + 128 * part:256 * k + 128 * part + 128] = second

    for side in range(2):
        for k in range(OWN_STEP):
            if side == 0:
                one = step * OWN_STEP + k
                x = cta_ref[:, 0, k].astype(f32)
                y = cta2_ref[:, 0, k].astype(f32)
                ct = cat([jnp.where(core == 0, x, y), jnp.where(core == 0, y, x)], 1)
            else:
                slot, at = k // (OWN_STEP // 2), k % (OWN_STEP // 2)
                one = (slot + core) % 2 * 16 + step * (OWN_STEP // 2) + at
                ct = (ctb_ref if slot == 0 else ctb2_ref)[:, 0, at].astype(f32)
            hi, lo = split(ct.reshape(256, 128) * inv[one])
            both = mm(turned[side], cat([hi, lo], 1))
            uhi, ulo = split(both[:, :128] + both[:, 128:])
            rows = pl.ds(pl.multiple_of(one * 16, 16), 16)
            for b in range(32):
                stage[side, rows, 256 * b:256 * b + 128] = uhi[16 * b:16 * b + 16]
                stage[side, rows, 256 * b + 128:256 * b + 256] = ulo[16 * b:16 * b + 16]

    @pl.when(step == 32 // OWN_STEP - 1)
    def _():
        grads = []
        for side in range(2):
            res[:, 0:32] = mm(stage[side], wide[side], NT)
            grads.append(cat([res[pl.ds(s, 32, stride=16), :] for s in range(16)], 0)[:, 0:32])
        lv = ownx_ref[...].reshape(512, 128)[:, 64:].astype(f32)
        dlr = cat(grads, 1) * lv
        m2 = m2_ref[...].reshape(512, 64)
        xn2, rstd2 = norm_rows(m2)
        adj = adj_ref[...].reshape(512, 64).astype(f32)
        g2 = adj + norm_back(xn2, rstd2, mm2(dlr, wt_ref[...], NT))
        g2_ref[...] = g2.reshape(16, 32, 64)
        xn, _ = norm_rows(m1_ref[...].reshape(512, 64))
        gate = jax.nn.sigmoid(mm2(xn, cw_ref[:, 192:256]))
        dmix = mm2(g2, wv_ref[...], NT)
        attended = spread(unpair(c2_ref[:, 16, :]))
        dcg_ref[...] = (dmix * attended * gate * (1.0 - gate)).reshape(16, 32, 64)
        da = jnp.sum((gate * dmix).reshape(16, 32, 64), 0)
        packed = cat([da[:16], da[16:]], 1)
        for k in range(16):
            e1_ref[k] = packed


def row_bwd_kernel(
    place_ref, e1_ref, c2_ref, m1_ref, own_ref, g2_ref, dcg_ref, cw_ref,
    p_ref, o_ref, v2_ref, gate_ref, any_ref, wo_ref,
    g1_ref, ds_ref, do_ref, dg_ref, bias_ref,
    g1s,
):
    s = pl.program_id(0)

    @pl.when(s == 0)
    def _():
        cw = cw_ref[...]
        groups = head_mask(64, 64, 8, 8).astype(bf16)
        da = jnp.sum(e1_ref[...], 0)
        da = unpair(da)
        attended = unpair(c2_ref[:, 16, :])
        peak = unpair(c2_ref[:, 17, :])
        den = unpair(c2_ref[:, 18, :])
        colq = unpair(c2_ref[:, 19, :])
        count = unpair(c2_ref[:, 20, :])
        delta = mm3(da * attended, groups)
        feature = lax.broadcasted_iota(jnp.int32, (32, 64), 1) % 8
        dq = jnp.zeros((32, 64), f32)
        for k in range(8):
            z = mm3(da * unpair(c2_ref[:, k, :]), groups) - delta * unpair(c2_ref[:, 8 + k, :])
            dq = dq + jnp.where(feature == k, z, 0.0)
        dtotal = mm2(dq * SCALE, cw[:, 0:64], NT) / jnp.maximum(count, 1.0)
        live = own_ref[...].reshape(512, 128)[:, 64:].astype(f32)
        xn, rstd = norm_rows(m1_ref[...].reshape(512, 64))
        kt = mm2(xn, cw[:, 64:128])
        vt = mm2(xn, cw[:, 128:192])
        qs = spread(colq)
        logits = jnp.where(live > 0, mm3(kt * qs, groups), NEG)
        weights = jnp.exp(logits - spread(peak)) / spread(den)
        das = spread(da)
        dl = weights * (mm2(vt * das, groups) - spread(delta)) * live
        dxn = (
            mm2(dcg_ref[...].reshape(512, 64), cw[:, 192:256], NT)
            + mm2(dl * qs, cw[:, 64:128], NT)
            + mm2(weights * das, cw[:, 128:192], NT)
            + live * spread(dtotal)
        )
        g1 = g2_ref[...].reshape(512, 64) + norm_back(xn, rstd, dxn)
        g1s[...] = g1.reshape(16, 32, 64)
        bias_ref[...] = jnp.zeros_like(bias_ref)

    heads = head_mask(64, 256, 8, 32)
    wo = wo_ref[...]
    wo2 = cat([wo, wo], 1)
    for u in range(GROUP):
        dm = g1s[s * GROUP + u]
        g1_ref[u] = dm
        o = o_ref[u]
        v2 = v2_ref[u]
        gate = gate_ref[u]
        dout = mm(wo2, cat([pair2(dm)] * 8, 0), NT)
        hi, lo = split(dout * o * gate * (1.0 - gate))
        dg_ref[u] = cat([hi, lo], 0)
        do = dout * gate * heads
        hi, lo = split(do)
        do_ref[u] = cat([hi, lo], 0)
        do_live = do * any_ref[u, 0:1, :]
        delta = jnp.sum(do_live * o, 0, keepdims=True)
        lhi, llo = split(do_live)
        dp = mm(v2, cat([lhi, lhi], 0)) + mm(v2[:, :64], llo)
        ds = p_ref[u] * (dp - delta)
        for k, at in enumerate(res_order(place_ref)):
            bias_ref[pl.ds(2 * at, 2)] += ds[32 * k:32 * k + 32].reshape(2, 16, 256)
        shi, slo = split(ds)
        ds_ref[u, :, 0:256] = shi
        ds_ref[u, :, 256:512] = slo


def row_inputs_kernel(
    place_ref, p_ref, ds_ref, do_ref, dg_ref, q_ref, kt_ref, win_ref, dxo_ref, f_ref, wback, wown
):
    @pl.when(pl.program_id(0) == 0)
    def _():
        wt = win_ref[...].astype(f32).T
        qg = cat([wt[0:64], wt[192:256]], 0)
        wback[...] = cat([wt[64:128], wt[64:128], wt[128:192], wt[128:192]], 0).astype(bf16)
        wown[...] = cat([qg, qg], 0).astype(bf16)

    heads = head_mask(64, 256, 8, 32) * SCALE
    zero = jnp.zeros((64, 256), bf16)
    for u in range(GROUP):
        shi, slo = ds_ref[u, :, 0:256], ds_ref[u, :, 256:512]
        kt = kt_ref[u]
        q = q_ref[u]
        do = do_ref[u]
        dg = dg_ref[u]
        first = mm(kt, shi)
        dq = (first[:64] + first[64:] + mm(kt[:64], slo)) * heads
        dk = mm(shi, q, NT) + mm(slo, cat([q[:64], zero], 0), NT)
        phi, plo = split(p_ref[u])
        dv = mm(phi, do, NT) + mm(plo, cat([do[:64], zero], 0), NT)
        dx = mm2(cat([dk, dv], 1), wback[...]).reshape(8, 32, 64)
        dense = cat([dx[:, :16], dx[:, 16:]], 2)
        for k, at in enumerate(res_order(place_ref)):
            f_ref[at, u] = dense[k]
        qhi, qlo = split(dq)
        dxo = mm(cat([qhi, dg[:64], qlo, dg[64:]], 0), wown[...], TN)
        dxo_ref[u] = jnp.sum(dxo.reshape(8, 32, 64), 0)


def final_rows_kernel(f_ref, dxo_ref, g1_ref, own_ref, out_ref):
    total = jnp.sum(f_ref[...], 0)
    total = cat([total[:, :, :64], total[:, :, 64:]], 1).reshape(512, 64)
    total = total + dxo_ref[...].reshape(512, 64)
    xn, rstd = norm_rows(own_ref[...].reshape(512, 128)[:, :64].astype(f32))
    out = g1_ref[...].reshape(512, 64) + norm_back(xn, rstd, total)
    out_ref[...] = out.reshape(16, 32, 64)


def final_pair_kernel(b_ref, pair_ref, wb_ref, ct_ref, out_ref, scr):
    total = jnp.sum(b_ref[...], 0)
    wbt = wb_ref[...].astype(f32).T
    w2 = cat([wbt, wbt], 0).astype(bf16)
    own = head_mask(8, 256, 1, 32)
    for j in range(16):
        wide = jnp.broadcast_to(total[j:j + 1, :], (8, 256)) * own
        hi, lo = split(wide)
        y = mm(cat([hi, lo], 0), w2, TN)
        scr[:, j, :] = jnp.sum(y.reshape(8, 32, 128), 0)
    xn, rstd = norm_rows(pair_ref[...].reshape(512, 128).astype(f32))
    out = norm_back(xn, rstd, scr[...].reshape(512, 128)) + ct_ref[...].reshape(512, 128).astype(f32)
    out_ref[...] = out.reshape(32, 16, 128)


def sds(shape, dtype=f32):
    return jax.ShapeDtypeStruct(shape, dtype)


def full(shape):
    zeros = (0,) * len(shape)
    return pl.BlockSpec(shape, lambda s: zeros)


def row(shape):
    rest = (0,) * (len(shape) - 1)
    return pl.BlockSpec((GROUP,) + shape[1:], lambda s: (s,) + rest)


def whole_call(kernel, out_shape, *args, scratch=()):
    return pl.pallas_call(
        kernel, out_shape=out_shape, scratch_shapes=list(scratch), compiler_params=VMEM
    )(*args)


def project(rows, own, win):
    return pl.pallas_call(
        proj_kernel,
        grid=(16 // GROUP,),
        in_specs=[
            *[row((17, 16, 128)) for _ in range(8)],
            *[pl.BlockSpec((1, 16, 128), lambda s: (16, 0, 0)) for _ in range(8)],
            row((16, 32, 128)), full((64, 256)),
        ],
        out_specs=[
            row((16, 256, 128)), row((16, 256, 128)), row((16, 128, 256)), row((16, 128, 256)),
            row((16, 128, 256)), row((16, 64, 256)), full((16, 256)),
        ],
        out_shape=[
            sds((16, 256, 128), bf16), sds((16, 256, 128), bf16), sds((16, 128, 256), bf16),
            sds((16, 128, 256), bf16), sds((16, 128, 256), bf16), sds((16, 64, 256)),
            sds((16, 256), bf16),
        ],
        scratch_shapes=[
            pltpu.VMEM((128, 128), bf16), pltpu.VMEM((128, 128), bf16),
            pltpu.VMEM((128, 128), bf16), pltpu.VMEM((128, 128), bf16),
        ],
        compiler_params=VMEM,
    )(*rows, *rows, own, win)


def row_forward(place, k2, vt, q, gate, live, own, bias, wo):
    return pl.pallas_call(
        row_fwd_kernel,
        grid=(16 // GROUP,),
        in_specs=[
            SMEM, row((16, 256, 128)), row((16, 128, 256)), row((16, 128, 256)), row((16, 64, 256)),
            full((16, 256)), row((16, 32, 128)), full((16, 16, 256)), full((64, 64)),
        ],
        out_specs=[
            row((16, 256, 256)), row((16, 64, 256)), row((16, 32, 64)), row((16, 8, 256)),
            full((16, 2, 16, 128)),
        ],
        out_shape=[
            sds((16, 256, 256)), sds((16, 64, 256)), sds((16, 32, 64)), sds((16, 8, 256)),
            sds((16, 2, 16, 128)),
        ],
        compiler_params=VMEM,
    )(place, k2, vt, q, gate, live, own, bias, wo)


def outer_product(place, ct, ct2, factors, dblock, w, m2, c2, m1, own, adj, cw, wvo, wtf):
    half = OWN_STEP // 2
    one = pl.BlockSpec((8, 1, OWN_STEP, 16, 128), lambda s: (0, 0, s, 0, 0))
    two = pl.BlockSpec((8, 1, half, 32, 128), lambda s: (0, 1, s, 0, 0))
    return pl.pallas_call(
        outer_kernel,
        grid=(32 // OWN_STEP,),
        in_specs=[
            SMEM,
            full((8, 20, 16, 128)),
            pl.BlockSpec((1, 20, 16, 128), lambda s: (0, 0, 0, 0)),
            one, two, one, two,
            full((1024, 128)),
            full((16, 32, 64)), full((16, 32, 128)), full((16, 32, 64)), full((16, 32, 128)),
            full((16, 32, 64)), full((64, 256)), full((64, 64)), full((64, 64)),
        ],
        out_specs=[full((16, 32, 64)), full((16, 32, 64)), full((16, 16, 128))],
        out_shape=[sds((16, 32, 64)), sds((16, 32, 64)), sds((16, 16, 128))],
        scratch_shapes=[
            pltpu.VMEM((32, 256, 128), f32),
            pltpu.VMEM((2, 512, 256), bf16),
            pltpu.VMEM((2, 512, 8192), bf16),
            pltpu.VMEM((512, 128), f32),
            pltpu.VMEM((2, 1024, 128), f32),
            pltpu.VMEM((2, 32, 8192), bf16),
            pltpu.VMEM((1024, 128), f32),
        ],
        compiler_params=VMEM,
    )(
        place, factors, dblock, ct.reshape(8, 2, 32, 16, 128), ct.reshape(8, 2, 16, 32, 128),
        ct2.reshape(8, 2, 32, 16, 128), ct2.reshape(8, 2, 16, 32, 128), w, m2, c2, m1, own, adj,
        cw, wvo, wtf,
    )


def row_backward(place, e1, c2, m1, own, g2, dcg, cw, p, o, v2, gate, any_live, wo):
    return pl.pallas_call(
        row_bwd_kernel,
        grid=(16 // GROUP,),
        in_specs=[
            SMEM, full((16, 16, 128)), full((16, 32, 128)), full((16, 32, 64)), full((16, 32, 128)),
            full((16, 32, 64)), full((16, 32, 64)), full((64, 256)),
            row((16, 256, 256)), row((16, 64, 256)), row((16, 256, 128)), row((16, 64, 256)),
            row((16, 8, 256)), full((64, 64)),
        ],
        out_specs=[
            row((16, 32, 64)), row((16, 256, 512)), row((16, 128, 256)), row((16, 128, 256)),
            full((16, 16, 256)),
        ],
        out_shape=[
            sds((16, 32, 64)), sds((16, 256, 512), bf16), sds((16, 128, 256), bf16),
            sds((16, 128, 256), bf16), sds((16, 16, 256)),
        ],
        scratch_shapes=[pltpu.VMEM((16, 32, 64), f32)],
        compiler_params=VMEM,
    )(place, e1, c2, m1, own, g2, dcg, cw, p, o, v2, gate, any_live, wo)


def row_inputs(place, p, ds, do, dg, q, kt, win):
    return pl.pallas_call(
        row_inputs_kernel,
        grid=(16 // GROUP,),
        in_specs=[
            SMEM, row((16, 256, 256)), row((16, 256, 512)), row((16, 128, 256)), row((16, 128, 256)),
            row((16, 128, 256)), row((16, 128, 256)), full((64, 256)),
        ],
        out_specs=[row((16, 32, 64)), pl.BlockSpec((8, GROUP, 16, 128), lambda s: (0, s, 0, 0))],
        out_shape=[sds((16, 32, 64)), sds((8, 16, 16, 128))],
        scratch_shapes=[pltpu.VMEM((256, 64), bf16), pltpu.VMEM((256, 64), bf16)],
        compiler_params=VMEM,
    )(place, p, ds, do, dg, q, kt, win)


def body(
    alignment_state,
    pairwise_state,
    alignment_mask,
    residue_entry_mask,
    sequence_live_count,
    horizontal_intake_coefs,
    pairwise_bias_weights,
    horizontal_readout_coefs,
    column_input_weights,
    vertical_readout_coefs,
    tensor_factor_coefs,
    outer_output_weights,
    adjoint_of_result_track,
    pairwise_cotangent,
):
    place = jnp.stack([lax.axis_index("depth"), lax.axis_index("res")]).astype(jnp.int32)
    vmem = pl.BlockSpec(memory_space=pltpu.VMEM)
    row_block, own = pl.pallas_call(
        pack_kernel,
        in_specs=[vmem, vmem, vmem, SMEM],
        out_shape=[sds((17, 16, 128), bf16), sds((16, 32, 128), bf16)],
        compiler_params=VMEM,
    )(alignment_state, alignment_mask, residue_entry_mask.reshape(1, 32), sequence_live_count)
    rows = [row_block] + [
        lax.ppermute(row_block, "res", [(r, r ^ k) for r in range(8)]) for k in range(1, 8)
    ]
    bias_block = whole_call(
        bias_kernel, sds((16, 16, 256)), pairwise_state, pairwise_bias_weights,
        scratch=[pltpu.VMEM((32, 16, 128), f32)],
    )
    cw = cat(
        [
            column_input_weights[:, :64],
            jnp.tile(column_input_weights[:, 64:72], (1, 8)),
            jnp.tile(column_input_weights[:, 72:80], (1, 8)),
            column_input_weights[:, 80:],
        ],
        1,
    )

    turned = pairwise_cotangent.transpose(1, 0, 2)
    perm = [(d * 8 + r, (2 * r + d % 2) * 8 + d // 2) for d in range(16) for r in range(8)]
    turned = lax.ppermute(turned, ("depth", "res"), perm)
    both = whole_call(turn_kernel, sds((8, 1024, 128), bf16), pairwise_cotangent, turned)

    bias = lax.all_to_all(bias_block, "depth", 0, 0)
    bias, both, *rows = lax.optimization_barrier((bias, both, *rows))
    k2, v2, kt, vt, q, gate, live = project(rows, own, horizontal_intake_coefs)
    same_core = [[c + 2 * k for k in range(8)] for c in range(2)]
    ct = lax.all_to_all(both, "depth", 0, 0, axis_index_groups=same_core)
    p, o, m1, any_live, c1 = row_forward(
        place, k2, vt, q, gate, live, own, bias, horizontal_readout_coefs
    )
    c1, ct = lax.optimization_barrier((c1, ct))
    ct2 = lax.ppermute(ct, "depth", [(d, d ^ 1) for d in range(16)])
    c1 = lax.all_to_all(c1, "depth", 0, 0)
    c2 = whole_call(col_kernel, sds((16, 32, 128)), c1, cw)
    c2 = lax.all_to_all(c2, "depth", 0, 0)
    m2, dblock = whole_call(
        factor_kernel, [sds((16, 32, 64)), sds((8, 20, 16, 128), bf16)],
        m1, c2, own, cw, vertical_readout_coefs, tensor_factor_coefs,
    )
    factors = lax.all_to_all(dblock, "res", 0, 0)
    g2, dcg, e1 = outer_product(
        place, ct, ct2, factors, dblock, outer_output_weights, m2, c2, m1, own,
        adjoint_of_result_track, cw, vertical_readout_coefs, tensor_factor_coefs,
    )
    e1 = lax.all_to_all(e1, "depth", 0, 0)
    g1, ds, do, dg, bblock = row_backward(
        place, e1, c2, m1, own, g2, dcg, cw, p, o, v2, gate, any_live, horizontal_readout_coefs
    )
    bsum = lax.all_to_all(bblock, "depth", 0, 0)
    dxo, fblock = row_inputs(place, p, ds, do, dg, q, kt, horizontal_intake_coefs)
    fblock, bsum = lax.optimization_barrier((fblock, bsum))
    fsum = lax.all_to_all(fblock, "res", 0, 0)
    alignment_gradient = whole_call(final_rows_kernel, sds((16, 32, 64)), fsum, dxo, g1, own)
    pair_grad = whole_call(
        final_pair_kernel, sds((32, 16, 128)), bsum, pairwise_state, pairwise_bias_weights,
        pairwise_cotangent, scratch=[pltpu.VMEM((32, 16, 128), f32)],
    )
    return alignment_gradient, pair_grad


def solution(mesh):
    in_specs = (
        P("depth", "res", None),
        P("res", "depth", None),
        P("depth", "res"),
        P("res"),
        P("depth"),
        P(),
        P(),
        P(),
        P(),
        P(),
        P(),
        P(),
        P("depth", "res", None),
        P("res", "depth", None),
    )
    out_specs = (P("depth", "res", None), P("res", "depth", None))
    return jax.shard_map(body, mesh=mesh, in_specs=in_specs, out_specs=out_specs, check_vma=False)
```

```python
import jax
import jax.numpy as jnp
from jax import lax
from jax.experimental import pallas as pl
from jax.experimental.pallas import tpu as pltpu
from jax.sharding import PartitionSpec as P

f32 = jnp.float32
bf16 = jnp.bfloat16
EPS = 1e-05
NEG = -1000000000.0
SCALE = 8 ** (-0.5)
NN = (((1,), (0,)), ((), ()))
NT = (((1,), (1,)), ((), ()))
TN = (((0,), (0,)), ((), ()))
GROUP = 8
SMEM = pl.BlockSpec(memory_space=pltpu.SMEM)
OWN_STEP = 8
def limit(mib):
    return pltpu.CompilerParams(vmem_limit_bytes=mib * 1024 * 1024)


VMEM = limit(50)
LARGE = limit(60)
SMALL = limit(50)


def mm(a, b, dims=NN):
    return lax.dot_general(a, b, dims, preferred_element_type=f32)


def split(x):
    hi = x.astype(bf16)
    lo = (x - hi.astype(f32)).astype(bf16)
    return hi, lo


def split3(x):
    hi = x.astype(bf16)
    rest = x - hi.astype(f32)
    mid = rest.astype(bf16)
    lo = (rest - mid.astype(f32)).astype(bf16)
    return hi, mid, lo


def cat(parts, axis):
    return jnp.concatenate(parts, axis=axis)


def mm2(x, w, dims=NN):
    hi, lo = split(x)
    return mm(hi, w, dims) + mm(lo, w, dims)


def mm3(x, w):
    hi, mid, lo = split3(x)
    return mm(hi, w) + mm(mid, w) + mm(lo, w)


def norm_rows(x):
    center = x - jnp.mean(x, -1, keepdims=True)
    rstd = lax.rsqrt(jnp.mean(center * center, -1, keepdims=True) + EPS)
    return center * rstd, rstd


def norm_back(normed, rstd, grad):
    return rstd * (
        grad
        - jnp.mean(grad, -1, keepdims=True)
        - normed * jnp.mean(grad * normed, -1, keepdims=True)
    )


def pair2(x):
    hi, lo = split(x)
    return cat([hi, lo], 1)


def head_mask(rows, cols, row_div, col_div):
    a = lax.broadcasted_iota(jnp.int32, (rows, cols), 0) // row_div
    b = lax.broadcasted_iota(jnp.int32, (rows, cols), 1) // col_div
    return (a == b).astype(f32)


def prepare_kernel(
    pair_hbm, wb_hbm, ct_hbm, x_hbm, mask_hbm, res_hbm, count_ref,
    bias_ref, rows_ref, own_ref, turned_ref,
    scr, pair_ref, wb_ref, ct_ref, x_ref, mask_ref, res_ref, sems,
):
    moves = [
        pltpu.make_async_copy(src, dst, sems.at[k])
        for k, (src, dst) in enumerate(
            (
                (x_hbm, x_ref), (mask_hbm, mask_ref), (res_hbm, res_ref), (ct_hbm, ct_ref),
                (pair_hbm, pair_ref), (wb_hbm, wb_ref),
            )
        )
    ]
    for move in moves:
        move.start()
    for move in moves:
        move.wait()
    seq = lax.broadcasted_iota(jnp.int32, (16, 32), 0)
    alive = (seq < count_ref[0]).astype(f32)
    live = mask_ref[...].astype(f32) * res_ref[...].astype(f32) * alive
    x = x_ref[...]
    diag = head_mask(32, 32, 1, 1)
    cols = [
        jnp.broadcast_to(jnp.sum(diag * live[k:k + 1, :], 1, keepdims=True), (32, 64))[None]
        for k in range(16)
    ]
    own_ref[...] = cat([x.astype(f32), cat(cols, 0)], 2).astype(bf16)
    rows_ref[0:16] = cat([x[:, :16], x[:, 16:]], 2)
    rows_ref[16] = cat([live, jnp.zeros((16, 96), f32)], 1).astype(bf16)

    scr[0] = ct_ref[...].astype(f32)
    for j in range(16):
        turned_ref[j] = scr[0, :, j, :].astype(bf16)

    xn, _ = norm_rows(pair_ref[...].astype(f32).reshape(512, 128))
    scr[1] = xn.reshape(32, 16, 128)
    w2 = cat([wb_ref[...], wb_ref[...]], 1)
    heads = head_mask(8, 256, 1, 32)
    rows = []
    for j in range(16):
        x2 = pair2(scr[1, :, j, :])
        tiled = cat([x2] * 8, 0)
        full = mm(w2, tiled, NT)
        rows.append(jnp.sum(full * heads, 0, keepdims=True))
    block = cat(rows, 0)
    for k in range(16):
        bias_ref[k] = block


def res_order(place_ref):
    return [jnp.bitwise_xor(place_ref[1], k) for k in range(8)]


def unpack(p):
    return cat([p[:, :, :64], p[:, :, 64:]], 1).reshape(256, 64)


def turn_kernel(ct_ref, turned_ref, out_ref):
    for k in range(8):
        out_ref[k, 0:512] = ct_ref[...].reshape(512, 128)
        out_ref[k, 512:1024] = turned_ref[...].reshape(512, 128)


def proj_kernel(*refs):
    g_refs, plane_refs = refs[0:8], refs[8:16]
    own_ref, win_ref, k2_ref, v2_ref, kt_ref, vt_ref, q_ref, gate_ref, live_ref = refs[16:25]
    wqg, wkvt, wkk, wvv = refs[25:]
    s = pl.program_id(0)

    @pl.when(s == 0)
    def _():
        w = win_ref[...].astype(f32)
        wt = w.T
        qg = cat([wt[0:64], wt[192:256]], 0)
        wqg[...] = cat([qg, qg], 1).astype(bf16)
        kv = wt[64:192]
        wkvt[...] = cat([kv, kv], 1).astype(bf16)
        for at, ref in ((64, wkk), (128, wvv)):
            one = w[:, at:at + 64]
            row = cat([one, one], 1)
            ref[...] = cat([row, row], 0).astype(bf16)
        live_ref[...] = cat([ref[0, :, 0:32] for ref in plane_refs], 1)

    lane = lax.broadcasted_iota(jnp.int32, (256, 128), 1)
    heads = head_mask(64, 256, 8, 32) * SCALE

    def two(x):
        hi = x.astype(bf16).astype(f32)
        return jnp.where(lane < 64, hi, x - hi).astype(bf16)

    every = range(GROUP)
    x2s = [
        pair2(norm_rows(unpack(cat([ref[u][None] for ref in g_refs], 0).astype(f32)))[0])
        for u in every
    ]
    xos = [pair2(norm_rows(own_ref[u].astype(f32)[:, :64])[0]) for u in every]
    ks = [mm(x2, wkk[...]) for x2 in x2s]
    vs = [mm(x2, wvv[...]) for x2 in x2s]
    kvts = [mm(wkvt[...], x2, NT) for x2 in x2s]
    qgs = [mm(wqg[...], cat([xo] * 8, 0), NT) for xo in xos]
    for u in every:
        k2_ref[u] = two(ks[u])
        v2_ref[u] = two(vs[u])
        hi, lo = split(kvts[u])
        kt_ref[u] = cat([hi[:64], lo[:64]], 0)
        vt_ref[u] = cat([hi[64:], lo[64:]], 0)
        qhi, qlo = split(qgs[u][:64] * heads)
        q_ref[u] = cat([qhi, qlo], 0)
        gate_ref[u] = jax.nn.sigmoid(qgs[u][64:])


def row_fwd_kernel(
    place_ref, k2_ref, vt_ref, q_ref, gate_ref, live_ref, own_ref, bias_ref, wo_ref,
    p_ref, o_ref, m1_ref, any_ref, c1_ref,
):
    s = pl.program_id(0)
    heads = head_mask(64, 256, 8, 32)
    wo = wo_ref[...]
    wo2 = cat([wo, wo], 0)
    seq = lax.broadcasted_iota(jnp.int32, (16, 128), 0)
    bias = cat([bias_ref[pl.ds(2 * at, 2)].reshape(32, 256) for at in res_order(place_ref)], 0)
    every = range(GROUP)
    alive, logit = [], []
    for u in every:
        pick = (seq == s * GROUP + u).astype(bf16)
        live = mm(live_ref[...], pick, TN)
        alive.append(live)
        k2 = k2_ref[u]
        qhi, qlo = q_ref[u, 0:64], q_ref[u, 64:128]
        logit.append(mm(k2, cat([qhi, qhi], 0)) + mm(k2[:, :64], qlo))
    outs = []
    for u in every:
        live = alive[u]
        logits = jnp.where(cat([live, live], 1) > 0, logit[u] + bias, NEG)
        e = jnp.exp(logits - jnp.max(logits, 0, keepdims=True))
        p = e * (1.0 / jnp.sum(e, 0, keepdims=True))
        p_ref[u] = p
        some = jnp.max(live, 0, keepdims=True)
        any_ref[u] = jnp.broadcast_to(cat([some, some], 1), (8, 256))
        phi, plo = split(p)
        vt = vt_ref[u]
        first = mm(vt, phi)
        outs.append((first[:64] + first[64:] + mm(vt[:64], plo)) * heads)
    for u in every:
        o_ref[u] = outs[u]
        ahi, alo = split(outs[u] * gate_ref[u])
        y = mm(cat([ahi, alo], 0), wo2, TN)
        own = own_ref[u].astype(f32)
        m1 = own[:, :64] + jnp.sum(y.reshape(8, 32, 64), 0)
        m1_ref[u] = m1
        c1_ref[:, 0, s * GROUP + u, :] = cat([m1[:16], m1[16:]], 1)
        lv = own[:, 64:]
        c1_ref[:, 1, s * GROUP + u, :] = cat([lv[:16], lv[16:]], 1)


def diag2(w):
    z = jnp.zeros_like(w)
    return cat([cat([w, z], 1), cat([z, w], 1)], 0)


def col_kernel(c1_ref, cw_ref, out_ref):
    x = c1_ref[:, 0].reshape(256, 128)
    live = c1_ref[:, 1].reshape(256, 128)
    halves = (head_mask(128, 128, 64, 64) * (1.0 / 64)).astype(bf16)
    center = x - mm3(x, halves)
    xn = center * lax.rsqrt(mm3(center * center, halves) + EPS)
    cw = cw_ref[...].astype(f32)
    wq = diag2(cw[:, 0:64]).astype(bf16)
    wk = diag2(cw[:, 64:128]).astype(bf16)
    wv = diag2(cw[:, 128:192]).astype(bf16)
    total = jnp.sum(live * xn, 0, keepdims=True)
    count = jnp.sum(live, 0, keepdims=True)
    mean = total / jnp.maximum(count, 1.0)
    colq = mm3(jnp.broadcast_to(mean, (8, 128)), wq)[0:1] * SCALE
    kt = mm2(xn, wk)
    vt = mm2(xn, wv)
    groups = head_mask(128, 128, 8, 8).astype(bf16)
    logits = jnp.where(live > 0, mm3(kt * colq, groups), NEG)
    peak = jnp.max(logits, 0, keepdims=True)
    e = jnp.exp(logits - peak)
    den = jnp.sum(e, 0, keepdims=True)
    w = e / den
    wv_ = w * vt
    attended = jnp.sum(wv_, 0, keepdims=True)
    khi, klo = split(kt)

    def by_key(z):
        zhi, zlo = split(z)
        full = mm(khi, zhi, TN) + mm(klo, zhi, TN) + mm(khi, zlo, TN)
        lane = lax.broadcasted_iota(jnp.int32, (8, 128), 1)
        return jnp.where(lane < 64, full[0:8], full[64:72])

    lt = live.T
    rows = [
        by_key(wv_), by_key(w), attended, peak, den, colq, count, count, count, count,
        lt[0:1, :128], lt[0:1, 128:], lt[64:65, :128], lt[64:65, 128:],
        count, count, count, count,
    ]
    block = cat(rows, 0)
    for k in range(16):
        out_ref[k] = block


def unpair(x):
    return cat([x[:, 0:64], x[:, 64:128]], 0)


def spread(v):
    return jnp.broadcast_to(v[None], (16, 32, 64)).reshape(512, 64)


def factor_kernel(m1_ref, c2_ref, own_ref, cw_ref, wv_ref, wt_ref, m2_ref, d_ref):
    m1 = m1_ref[...].reshape(512, 64)
    live = own_ref[...].reshape(512, 128)[:, 64:].astype(f32)
    attended = unpair(c2_ref[:, 16, :])
    xn, _ = norm_rows(m1)
    gate = jax.nn.sigmoid(mm2(xn, cw_ref[:, 192:256]))
    m2 = m1 + mm2(gate * spread(attended), wv_ref[...])
    m2_ref[...] = m2.reshape(16, 32, 64)
    xn2, _ = norm_rows(m2)
    lr = live * mm2(xn2, wt_ref[...])
    lr = lr.reshape(16, 32, 64)
    lr = cat([lr[:, :16], lr[:, 16:]], 2).astype(bf16)
    lt = [c2_ref[:, 24 + k, :].astype(bf16) for k in range(4)]
    for k in range(8):
        d_ref[k, 0:16] = lr
        for q in range(4):
            d_ref[k, 16 + q] = lt[q]


def masks_by_row(p):
    low = cat([p[:, 0], p[:, 1]], 2)
    high = cat([p[:, 2], p[:, 3]], 2)
    return cat([low, high], 1)


def outer_kernel(
    place_ref, da_ref, own_ref, cta_ref, ctb_ref, cta2_ref, ctb2_ref, w_ref, m2_ref, c2_ref, m1_ref,
    ownx_ref, adj_ref, cw_ref, wv_ref, wt_ref, g2_ref, dcg_ref, e1_ref,
    inv, turned, stage, res, lrs, wide, wf,
):
    step = pl.program_id(0)
    core = place_ref[0] % 2

    @pl.when(step == 0)
    def _():
        every = masks_by_row(da_ref[:, 16:20]).reshape(256, 256)
        mine = masks_by_row(own_ref[:, 16:20]).reshape(32, 256)
        value = 1.0 / jnp.maximum(mm(every, mine, NT), 1.0)
        for k in range(32):
            inv[k] = jnp.broadcast_to(value[:, k:k + 1], (256, 128))
        for s in range(16):
            piece = unpack(da_ref[:, s].astype(f32)).T
            for half in range(2):
                cols = piece[:, 128 * half:128 * half + 128]
                lrs[half, pl.ds(s, 32, stride=16), :] = cols[0:32]
                lrs[half, pl.ds(512 + s, 32, stride=16), :] = cols[32:64]
        for half in range(2):
            turned[0, :, 128 * half:128 * half + 128] = lrs[half, 512:1024].astype(bf16)
            turned[1, :, 128 * half:128 * half + 128] = lrs[half, 0:512].astype(bf16)
        wf[...] = w_ref[...].astype(f32)
        for k in range(32):
            first = wf[pl.ds(k, 32, stride=32), :].astype(bf16)
            second = w_ref[32 * k:32 * k + 32]
            for part in range(2):
                wide[0, :, 256 * k + 128 * part:256 * k + 128 * part + 128] = first
                wide[1, :, 256 * k + 128 * part:256 * k + 128 * part + 128] = second

    for side in range(2):
        for k in range(OWN_STEP):
            if side == 0:
                one = step * OWN_STEP + k
                x = cta_ref[:, 0, k].astype(f32)
                y = cta2_ref[:, 0, k].astype(f32)
                ct = cat([jnp.where(core == 0, x, y), jnp.where(core == 0, y, x)], 1)
            else:
                slot, at = k // (OWN_STEP // 2), k % (OWN_STEP // 2)
                one = (slot + core) % 2 * 16 + step * (OWN_STEP // 2) + at
                ct = (ctb_ref if slot == 0 else ctb2_ref)[:, 0, at].astype(f32)
            hi, lo = split(ct.reshape(256, 128) * inv[one])
            both = mm(turned[side], cat([hi, lo], 1))
            uhi, ulo = split(both[:, :128] + both[:, 128:])
            rows = pl.ds(pl.multiple_of(one * 16, 16), 16)
            for b in range(32):
                stage[side, rows, 256 * b:256 * b + 128] = uhi[16 * b:16 * b + 16]
                stage[side, rows, 256 * b + 128:256 * b + 256] = ulo[16 * b:16 * b + 16]

    @pl.when(step == 32 // OWN_STEP - 1)
    def _():
        grads = []
        for side in range(2):
            res[:, 0:32] = mm(stage[side], wide[side], NT)
            grads.append(cat([res[pl.ds(s, 32, stride=16), :] for s in range(16)], 0)[:, 0:32])
        lv = ownx_ref[...].reshape(512, 128)[:, 64:].astype(f32)
        dlr = cat(grads, 1) * lv
        m2 = m2_ref[...].reshape(512, 64)
        xn2, rstd2 = norm_rows(m2)
        adj = adj_ref[...].reshape(512, 64).astype(f32)
        g2 = adj + norm_back(xn2, rstd2, mm2(dlr, wt_ref[...], NT))
        g2_ref[...] = g2.reshape(16, 32, 64)
        xn, _ = norm_rows(m1_ref[...].reshape(512, 64))
        gate = jax.nn.sigmoid(mm2(xn, cw_ref[:, 192:256]))
        dmix = mm2(g2, wv_ref[...], NT)
        attended = spread(unpair(c2_ref[:, 16, :]))
        dcg_ref[...] = (dmix * attended * gate * (1.0 - gate)).reshape(16, 32, 64)
        da = jnp.sum((gate * dmix).reshape(16, 32, 64), 0)
        packed = cat([da[:16], da[16:]], 1)
        for k in range(16):
            e1_ref[k] = packed


def row_bwd_kernel(
    place_ref, e1_ref, c2_ref, m1_ref, own_ref, g2_ref, dcg_ref, cw_ref,
    p_ref, o_ref, v2_ref, gate_ref, any_ref, wo_ref,
    g1_ref, ds_ref, do_ref, dg_ref, bias_ref,
    g1s,
):
    s = pl.program_id(0)

    @pl.when(s == 0)
    def _():
        cw = cw_ref[...]
        groups = head_mask(64, 64, 8, 8).astype(bf16)
        da = jnp.sum(e1_ref[...], 0)
        da = unpair(da)
        attended = unpair(c2_ref[:, 16, :])
        peak = unpair(c2_ref[:, 17, :])
        den = unpair(c2_ref[:, 18, :])
        colq = unpair(c2_ref[:, 19, :])
        count = unpair(c2_ref[:, 20, :])
        delta = mm3(da * attended, groups)
        feature = lax.broadcasted_iota(jnp.int32, (32, 64), 1) % 8
        dq = jnp.zeros((32, 64), f32)
        for k in range(8):
            z = mm3(da * unpair(c2_ref[:, k, :]), groups) - delta * unpair(c2_ref[:, 8 + k, :])
            dq = dq + jnp.where(feature == k, z, 0.0)
        dtotal = mm2(dq * SCALE, cw[:, 0:64], NT) / jnp.maximum(count, 1.0)
        live = own_ref[...].reshape(512, 128)[:, 64:].astype(f32)
        xn, rstd = norm_rows(m1_ref[...].reshape(512, 64))
        kt = mm2(xn, cw[:, 64:128])
        vt = mm2(xn, cw[:, 128:192])
        qs = spread(colq)
        logits = jnp.where(live > 0, mm3(kt * qs, groups), NEG)
        weights = jnp.exp(logits - spread(peak)) / spread(den)
        das = spread(da)
        dl = weights * (mm2(vt * das, groups) - spread(delta)) * live
        dxn = (
            mm2(dcg_ref[...].reshape(512, 64), cw[:, 192:256], NT)
            + mm2(dl * qs, cw[:, 64:128], NT)
            + mm2(weights * das, cw[:, 128:192], NT)
            + live * spread(dtotal)
        )
        g1 = g2_ref[...].reshape(512, 64) + norm_back(xn, rstd, dxn)
        g1s[...] = g1.reshape(16, 32, 64)
        bias_ref[...] = jnp.zeros_like(bias_ref)

    heads = head_mask(64, 256, 8, 32)
    wo = wo_ref[...]
    wo2 = cat([wo, wo], 1)
    every = range(GROUP)
    douts = []
    for u in every:
        dm = g1s[s * GROUP + u]
        g1_ref[u] = dm
        douts.append(mm(wo2, cat([pair2(dm)] * 8, 0), NT))
    dos, deltas, dps = [], [], []
    for u in every:
        o = o_ref[u]
        gate = gate_ref[u]
        hi, lo = split(douts[u] * o * gate * (1.0 - gate))
        dg_ref[u] = cat([hi, lo], 0)
        do = douts[u] * gate * heads
        hi, lo = split(do)
        do_ref[u] = cat([hi, lo], 0)
        do_live = do * any_ref[u, 0:1, :]
        dos.append(do_live)
        deltas.append(jnp.sum(do_live * o, 0, keepdims=True))
    for u in every:
        v2 = v2_ref[u]
        lhi, llo = split(dos[u])
        dps.append(mm(v2, cat([lhi, lhi], 0)) + mm(v2[:, :64], llo))
    total = jnp.zeros((256, 256), f32)
    for u in every:
        ds = p_ref[u] * (dps[u] - deltas[u])
        total = total + ds
        shi, slo = split(ds)
        ds_ref[u, :, 0:256] = shi
        ds_ref[u, :, 256:512] = slo
    for k, at in enumerate(res_order(place_ref)):
        bias_ref[pl.ds(2 * at, 2)] += total[32 * k:32 * k + 32].reshape(2, 16, 256)


def row_inputs_kernel(
    place_ref, p_ref, ds_ref, do_ref, dg_ref, q_ref, kt_ref, win_ref, dxo_ref, f_ref, wback, wown
):
    @pl.when(pl.program_id(0) == 0)
    def _():
        wt = win_ref[...].astype(f32).T
        qg = cat([wt[0:64], wt[192:256]], 0)
        wback[...] = cat([wt[64:128], wt[64:128], wt[128:192], wt[128:192]], 0).astype(bf16)
        wown[...] = cat([qg, qg], 0).astype(bf16)

    heads = head_mask(64, 256, 8, 32) * SCALE
    zero = jnp.zeros((64, 256), bf16)
    every = range(GROUP)
    dqs, dks, dvs = [], [], []
    for u in every:
        shi, slo = ds_ref[u, :, 0:256], ds_ref[u, :, 256:512]
        kt = kt_ref[u]
        q = q_ref[u]
        first = mm(kt, shi)
        dqs.append((first[:64] + first[64:] + mm(kt[:64], slo)) * heads)
        dks.append(mm(shi, q, NT) + mm(slo, cat([q[:64], zero], 0), NT))
    for u in every:
        do = do_ref[u]
        phi, plo = split(p_ref[u])
        dvs.append(mm(phi, do, NT) + mm(plo, cat([do[:64], zero], 0), NT))
    dxs = [mm2(cat([dks[u], dvs[u]], 1), wback[...]).reshape(8, 32, 64) for u in every]
    dxos = []
    for u in every:
        dg = dg_ref[u]
        qhi, qlo = split(dqs[u])
        dxos.append(mm(cat([qhi, dg[:64], qlo, dg[64:]], 0), wown[...], TN))
    order = res_order(place_ref)
    for u in every:
        dense = cat([dxs[u][:, :16], dxs[u][:, 16:]], 2)
        for k, at in enumerate(order):
            f_ref[at, u] = dense[k]
        dxo_ref[u] = jnp.sum(dxos[u].reshape(8, 32, 64), 0)


def final_rows_kernel(f_ref, dxo_ref, g1_ref, own_ref, out_ref):
    total = jnp.sum(f_ref[...], 0)
    total = cat([total[:, :, :64], total[:, :, 64:]], 1).reshape(512, 64)
    total = total + dxo_ref[...].reshape(512, 64)
    xn, rstd = norm_rows(own_ref[...].reshape(512, 128)[:, :64].astype(f32))
    out = g1_ref[...].reshape(512, 64) + norm_back(xn, rstd, total)
    out_ref[...] = out.reshape(16, 32, 64)


def final_pair_kernel(b_ref, pair_ref, wb_ref, ct_ref, out_ref, scr):
    total = jnp.sum(b_ref[...], 0)
    w2 = cat([wb_ref[...], wb_ref[...]], 0)
    own = head_mask(8, 256, 1, 32)
    for j in range(16):
        wide = jnp.broadcast_to(total[j:j + 1, :], (8, 256)) * own
        hi, lo = split(wide)
        y = mm(cat([hi, lo], 0), w2, TN)
        scr[:, j, :] = jnp.sum(y.reshape(8, 32, 128), 0)
    xn, rstd = norm_rows(pair_ref[...].reshape(512, 128).astype(f32))
    out = norm_back(xn, rstd, scr[...].reshape(512, 128)) + ct_ref[...].reshape(512, 128).astype(f32)
    out_ref[...] = out.reshape(32, 16, 128)


def sds(shape, dtype=f32):
    return jax.ShapeDtypeStruct(shape, dtype)


def far(shape, dtype=f32):
    return pltpu.HBM(shape, dtype)


def full(shape):
    zeros = (0,) * len(shape)
    return pl.BlockSpec(shape, lambda s: zeros)


def row(shape):
    rest = (0,) * (len(shape) - 1)
    return pl.BlockSpec((GROUP,) + shape[1:], lambda s: (s,) + rest)


def whole_call(kernel, out_shape, *args, scratch=()):
    return pl.pallas_call(
        kernel, out_shape=out_shape, scratch_shapes=list(scratch), compiler_params=VMEM
    )(*args)


def project(rows, own, win):
    return pl.pallas_call(
        proj_kernel,
        grid=(16 // GROUP,),
        in_specs=[
            *[row((17, 16, 128)) for _ in range(8)],
            *[pl.BlockSpec((1, 16, 128), lambda s: (16, 0, 0)) for _ in range(8)],
            row((16, 32, 128)), full((64, 256)),
        ],
        out_specs=[
            row((16, 256, 128)), row((16, 256, 128)), row((16, 128, 256)), row((16, 128, 256)),
            row((16, 128, 256)), row((16, 64, 256)), full((16, 256)),
        ],
        out_shape=[
            sds((16, 256, 128), bf16), far((16, 256, 128), bf16), far((16, 128, 256), bf16),
            sds((16, 128, 256), bf16), sds((16, 128, 256), bf16), sds((16, 64, 256)),
            sds((16, 256), bf16),
        ],
        scratch_shapes=[
            pltpu.VMEM((128, 128), bf16), pltpu.VMEM((128, 128), bf16),
            pltpu.VMEM((128, 128), bf16), pltpu.VMEM((128, 128), bf16),
        ],
        compiler_params=VMEM,
    )(*rows, *rows, own, win)


def row_forward(place, k2, vt, q, gate, live, own, bias, wo):
    return pl.pallas_call(
        row_fwd_kernel,
        grid=(16 // GROUP,),
        in_specs=[
            SMEM, row((16, 256, 128)), row((16, 128, 256)), row((16, 128, 256)), row((16, 64, 256)),
            full((16, 256)), row((16, 32, 128)), full((16, 16, 256)), full((64, 64)),
        ],
        out_specs=[
            row((16, 256, 256)), row((16, 64, 256)), row((16, 32, 64)), row((16, 8, 256)),
            full((16, 2, 16, 128)),
        ],
        out_shape=[
            far((16, 256, 256)), far((16, 64, 256)), sds((16, 32, 64)), sds((16, 8, 256)),
            sds((16, 2, 16, 128)),
        ],
        compiler_params=VMEM,
    )(place, k2, vt, q, gate, live, own, bias, wo)


def outer_product(place, ct, ct2, factors, dblock, w, m2, c2, m1, own, adj, cw, wvo, wtf):
    half = OWN_STEP // 2
    one = pl.BlockSpec((8, 1, OWN_STEP, 16, 128), lambda s: (0, 0, s, 0, 0))
    two = pl.BlockSpec((8, 1, half, 32, 128), lambda s: (0, 1, s, 0, 0))
    return pl.pallas_call(
        outer_kernel,
        grid=(32 // OWN_STEP,),
        in_specs=[
            SMEM,
            full((8, 20, 16, 128)),
            pl.BlockSpec((1, 20, 16, 128), lambda s: (0, 0, 0, 0)),
            one, two, one, two,
            full((1024, 128)),
            full((16, 32, 64)), full((16, 32, 128)), full((16, 32, 64)), full((16, 32, 128)),
            full((16, 32, 64)), full((64, 256)), full((64, 64)), full((64, 64)),
        ],
        out_specs=[full((16, 32, 64)), full((16, 32, 64)), full((16, 16, 128))],
        out_shape=[sds((16, 32, 64)), sds((16, 32, 64)), sds((16, 16, 128))],
        scratch_shapes=[
            pltpu.VMEM((32, 256, 128), f32),
            pltpu.VMEM((2, 512, 256), bf16),
            pltpu.VMEM((2, 512, 8192), bf16),
            pltpu.VMEM((512, 128), f32),
            pltpu.VMEM((2, 1024, 128), f32),
            pltpu.VMEM((2, 32, 8192), bf16),
            pltpu.VMEM((1024, 128), f32),
        ],
        compiler_params=VMEM,
    )(
        place, factors, dblock, ct.reshape(8, 2, 32, 16, 128), ct.reshape(8, 2, 16, 32, 128),
        ct2.reshape(8, 2, 32, 16, 128), ct2.reshape(8, 2, 16, 32, 128), w, m2, c2, m1, own, adj,
        cw, wvo, wtf,
    )


def row_backward(place, e1, c2, m1, own, g2, dcg, cw, p, o, v2, gate, any_live, wo):
    return pl.pallas_call(
        row_bwd_kernel,
        grid=(16 // GROUP,),
        in_specs=[
            SMEM, full((16, 16, 128)), full((16, 32, 128)), full((16, 32, 64)), full((16, 32, 128)),
            full((16, 32, 64)), full((16, 32, 64)), full((64, 256)),
            row((16, 256, 256)), row((16, 64, 256)), row((16, 256, 128)), row((16, 64, 256)),
            row((16, 8, 256)), full((64, 64)),
        ],
        out_specs=[
            row((16, 32, 64)), row((16, 256, 512)), row((16, 128, 256)), row((16, 128, 256)),
            full((16, 16, 256)),
        ],
        out_shape=[
            sds((16, 32, 64)), far((16, 256, 512), bf16), sds((16, 128, 256), bf16),
            sds((16, 128, 256), bf16), sds((16, 16, 256)),
        ],
        scratch_shapes=[pltpu.VMEM((16, 32, 64), f32)],
        compiler_params=SMALL,
    )(place, e1, c2, m1, own, g2, dcg, cw, p, o, v2, gate, any_live, wo)


def row_inputs(place, p, ds, do, dg, q, kt, win):
    return pl.pallas_call(
        row_inputs_kernel,
        grid=(16 // GROUP,),
        in_specs=[
            SMEM, row((16, 256, 256)), row((16, 256, 512)), row((16, 128, 256)), row((16, 128, 256)),
            row((16, 128, 256)), row((16, 128, 256)), full((64, 256)),
        ],
        out_specs=[row((16, 32, 64)), pl.BlockSpec((8, GROUP, 16, 128), lambda s: (0, s, 0, 0))],
        out_shape=[sds((16, 32, 64)), sds((8, 16, 16, 128))],
        scratch_shapes=[pltpu.VMEM((256, 64), bf16), pltpu.VMEM((256, 64), bf16)],
        compiler_params=SMALL,
    )(place, p, ds, do, dg, q, kt, win)


def body(
    alignment_state,
    pairwise_state,
    alignment_mask,
    residue_entry_mask,
    sequence_live_count,
    horizontal_intake_coefs,
    pairwise_bias_weights,
    horizontal_readout_coefs,
    column_input_weights,
    vertical_readout_coefs,
    tensor_factor_coefs,
    outer_output_weights,
    adjoint_of_result_track,
    pairwise_cotangent,
):
    place = jnp.stack([lax.axis_index("depth"), lax.axis_index("res")]).astype(jnp.int32)
    hbm = pl.BlockSpec(memory_space=pltpu.HBM)
    heads_first = pairwise_bias_weights.T
    bias_block, row_block, own, turned = pl.pallas_call(
        prepare_kernel,
        in_specs=[hbm] * 6 + [SMEM],
        out_shape=[
            sds((16, 16, 256)), sds((17, 16, 128), bf16), sds((16, 32, 128), bf16),
            sds((16, 32, 128), bf16),
        ],
        scratch_shapes=[
            pltpu.VMEM((2, 32, 16, 128), f32), pltpu.VMEM((32, 16, 128), bf16),
            pltpu.VMEM((8, 128), bf16), pltpu.VMEM((32, 16, 128), bf16),
            pltpu.VMEM((16, 32, 64), bf16), pltpu.VMEM((16, 32), jnp.int32),
            pltpu.VMEM((1, 32), jnp.int32), pltpu.SemaphoreType.DMA((6,)),
        ],
        compiler_params=LARGE,
    )(
        pairwise_state, heads_first, pairwise_cotangent, alignment_state,
        alignment_mask, residue_entry_mask.reshape(1, 32), sequence_live_count,
    )
    rows = [row_block] + [
        lax.ppermute(row_block, "res", [(r, r ^ k) for r in range(8)]) for k in range(1, 8)
    ]
    cw = cat(
        [
            column_input_weights[:, :64],
            jnp.tile(column_input_weights[:, 64:72], (1, 8)),
            jnp.tile(column_input_weights[:, 72:80], (1, 8)),
            column_input_weights[:, 80:],
        ],
        1,
    )

    perm = [(d * 8 + r, (2 * r + d % 2) * 8 + d // 2) for d in range(16) for r in range(8)]
    turned = lax.ppermute(turned, ("depth", "res"), perm)
    both = whole_call(turn_kernel, sds((8, 1024, 128), bf16), pairwise_cotangent, turned)

    bias = lax.all_to_all(bias_block, "depth", 0, 0)
    bias, both, *rows = lax.optimization_barrier((bias, both, *rows))
    k2, v2, kt, vt, q, gate, live = project(rows, own, horizontal_intake_coefs)
    same_core = [[c + 2 * k for k in range(8)] for c in range(2)]
    ct = lax.all_to_all(both, "depth", 0, 0, axis_index_groups=same_core)
    p, o, m1, any_live, c1 = row_forward(
        place, k2, vt, q, gate, live, own, bias, horizontal_readout_coefs
    )
    c1, ct = lax.optimization_barrier((c1, ct))
    ct2 = lax.ppermute(ct, "depth", [(d, d ^ 1) for d in range(16)])
    c1 = lax.all_to_all(c1, "depth", 0, 0)
    c2 = whole_call(col_kernel, sds((16, 32, 128)), c1, cw)
    c2 = lax.all_to_all(c2, "depth", 0, 0)
    m2, dblock = whole_call(
        factor_kernel, [sds((16, 32, 64)), sds((8, 20, 16, 128), bf16)],
        m1, c2, own, cw, vertical_readout_coefs, tensor_factor_coefs,
    )
    factors = lax.all_to_all(dblock, "res", 0, 0)
    g2, dcg, e1 = outer_product(
        place, ct, ct2, factors, dblock, outer_output_weights, m2, c2, m1, own,
        adjoint_of_result_track, cw, vertical_readout_coefs, tensor_factor_coefs,
    )
    e1 = lax.all_to_all(e1, "depth", 0, 0)
    g1, ds, do, dg, bblock = row_backward(
        place, e1, c2, m1, own, g2, dcg, cw, p, o, v2, gate, any_live, horizontal_readout_coefs
    )
    bsum = lax.all_to_all(bblock, "depth", 0, 0)
    dxo, fblock = row_inputs(place, p, ds, do, dg, q, kt, horizontal_intake_coefs)
    fblock, bsum = lax.optimization_barrier((fblock, bsum))
    fsum = lax.all_to_all(fblock, "res", 0, 0)
    alignment_gradient = whole_call(final_rows_kernel, sds((16, 32, 64)), fsum, dxo, g1, own)
    pair_grad = whole_call(
        final_pair_kernel, sds((32, 16, 128)), bsum, pairwise_state, heads_first,
        pairwise_cotangent, scratch=[pltpu.VMEM((32, 16, 128), f32)],
    )
    return alignment_gradient, pair_grad


def solution(mesh):
    in_specs = (
        P("depth", "res", None),
        P("res", "depth", None),
        P("depth", "res"),
        P("res"),
        P("depth"),
        P(),
        P(),
        P(),
        P(),
        P(),
        P(),
        P(),
        P("depth", "res", None),
        P("res", "depth", None),
    )
    out_specs = (P("depth", "res", None), P("res", "depth", None))
    return jax.shard_map(body, mesh=mesh, in_specs=in_specs, out_specs=out_specs, check_vma=False)
```

```python
import jax
import jax.numpy as jnp
from jax import lax
from jax.experimental import pallas as pl
from jax.experimental.pallas import tpu as pltpu
from jax.sharding import PartitionSpec as P

f32 = jnp.float32
bf16 = jnp.bfloat16
EPS = 1e-05
NEG = -1000000000.0
SCALE = 8 ** (-0.5)
NN = (((1,), (0,)), ((), ()))
NT = (((1,), (1,)), ((), ()))
TN = (((0,), (0,)), ((), ()))
GROUP = 8
SMEM = pl.BlockSpec(memory_space=pltpu.SMEM)
OWN_STEP = 8
def limit(mib):
    return pltpu.CompilerParams(vmem_limit_bytes=mib * 1024 * 1024)


VMEM = limit(50)
LARGE = limit(60)
SMALL = limit(50)


def mm(a, b, dims=NN):
    return lax.dot_general(a, b, dims, preferred_element_type=f32)


def split(x):
    hi = x.astype(bf16)
    lo = (x - hi.astype(f32)).astype(bf16)
    return hi, lo


def split3(x):
    hi = x.astype(bf16)
    rest = x - hi.astype(f32)
    mid = rest.astype(bf16)
    lo = (rest - mid.astype(f32)).astype(bf16)
    return hi, mid, lo


def cat(parts, axis):
    return jnp.concatenate(parts, axis=axis)


def mm2(x, w, dims=NN):
    hi, lo = split(x)
    return mm(hi, w, dims) + mm(lo, w, dims)


def mm3(x, w):
    hi, mid, lo = split3(x)
    return mm(hi, w) + mm(mid, w) + mm(lo, w)


def norm_rows(x):
    center = x - jnp.mean(x, -1, keepdims=True)
    rstd = lax.rsqrt(jnp.mean(center * center, -1, keepdims=True) + EPS)
    return center * rstd, rstd


def norm_back(normed, rstd, grad):
    return rstd * (
        grad
        - jnp.mean(grad, -1, keepdims=True)
        - normed * jnp.mean(grad * normed, -1, keepdims=True)
    )


def pair2(x):
    hi, lo = split(x)
    return cat([hi, lo], 1)


def head_mask(rows, cols, row_div, col_div):
    a = lax.broadcasted_iota(jnp.int32, (rows, cols), 0) // row_div
    b = lax.broadcasted_iota(jnp.int32, (rows, cols), 1) // col_div
    return (a == b).astype(f32)


def prepare_kernel(
    pair_hbm, wb_hbm, ct_hbm, x_hbm, mask_hbm, res_hbm, count_ref,
    bias_ref, rows_ref, own_ref, turned_ref,
    scr, pair_ref, wb_ref, ct_ref, x_ref, mask_ref, res_ref, sems,
):
    moves = [
        pltpu.make_async_copy(src, dst, sems.at[k])
        for k, (src, dst) in enumerate(
            (
                (x_hbm, x_ref), (mask_hbm, mask_ref), (res_hbm, res_ref), (ct_hbm, ct_ref),
                (pair_hbm, pair_ref), (wb_hbm, wb_ref),
            )
        )
    ]
    for move in moves:
        move.start()
    for move in moves:
        move.wait()
    seq = lax.broadcasted_iota(jnp.int32, (16, 32), 0)
    alive = (seq < count_ref[0]).astype(f32)
    live = mask_ref[...].astype(f32) * res_ref[...].astype(f32) * alive
    x = x_ref[...]
    diag = head_mask(32, 32, 1, 1)
    cols = [
        jnp.broadcast_to(jnp.sum(diag * live[k:k + 1, :], 1, keepdims=True), (32, 64))[None]
        for k in range(16)
    ]
    own_ref[...] = cat([x.astype(f32), cat(cols, 0)], 2).astype(bf16)
    rows_ref[0:16] = cat([x[:, :16], x[:, 16:]], 2)
    rows_ref[16] = cat([live, jnp.zeros((16, 96), f32)], 1).astype(bf16)

    scr[0] = ct_ref[...].astype(f32)
    for j in range(16):
        turned_ref[j] = scr[0, :, j, :].astype(bf16)

    xn, _ = norm_rows(pair_ref[...].astype(f32).reshape(512, 128))
    scr[1] = xn.reshape(32, 16, 128)
    w2 = cat([wb_ref[...], wb_ref[...]], 1)
    heads = head_mask(8, 256, 1, 32)
    rows = []
    for j in range(16):
        x2 = pair2(scr[1, :, j, :])
        tiled = cat([x2] * 8, 0)
        full = mm(w2, tiled, NT)
        rows.append(jnp.sum(full * heads, 0, keepdims=True))
    block = cat(rows, 0)
    for k in range(16):
        bias_ref[k] = block


def res_order(place_ref):
    return [jnp.bitwise_xor(place_ref[1], k) for k in range(8)]


def unpack(p):
    return cat([p[:, :, :64], p[:, :, 64:]], 1).reshape(256, 64)


def turn_kernel(ct_ref, turned_ref, out_ref):
    for k in range(8):
        out_ref[k, 0:512] = ct_ref[...].reshape(512, 128)
        out_ref[k, 512:1024] = turned_ref[...].reshape(512, 128)


def proj_kernel(*refs):
    g_refs, plane_refs = refs[0:8], refs[8:16]
    own_ref, win_ref, k2_ref, v2_ref, kt_ref, vt_ref, q_ref, gate_ref, live_ref = refs[16:25]
    wqg, wkvt, wkk, wvv = refs[25:]
    s = pl.program_id(0)

    @pl.when(s == 0)
    def _():
        w = win_ref[...].astype(f32)
        wt = w.T
        qg = cat([wt[0:64], wt[192:256]], 0)
        wqg[...] = cat([qg, qg], 1).astype(bf16)
        kv = wt[64:192]
        wkvt[...] = cat([kv, kv], 1).astype(bf16)
        for at, ref in ((64, wkk), (128, wvv)):
            one = w[:, at:at + 64]
            row = cat([one, one], 1)
            ref[...] = cat([row, row], 0).astype(bf16)
        live_ref[...] = cat([ref[0, :, 0:32] for ref in plane_refs], 1)

    lane = lax.broadcasted_iota(jnp.int32, (256, 128), 1)
    heads = head_mask(64, 256, 8, 32) * SCALE

    def two(x):
        hi = x.astype(bf16).astype(f32)
        return jnp.where(lane < 64, hi, x - hi).astype(bf16)

    every = range(GROUP)
    x2s = [
        pair2(norm_rows(unpack(cat([ref[u][None] for ref in g_refs], 0).astype(f32)))[0])
        for u in every
    ]
    xos = [pair2(norm_rows(own_ref[u].astype(f32)[:, :64])[0]) for u in every]
    ks = [mm(x2, wkk[...]) for x2 in x2s]
    vs = [mm(x2, wvv[...]) for x2 in x2s]
    kvts = [mm(wkvt[...], x2, NT) for x2 in x2s]
    qgs = [mm(wqg[...], cat([xo] * 8, 0), NT) for xo in xos]
    for u in every:
        k2_ref[u] = two(ks[u])
        v2_ref[u] = two(vs[u])
        hi, lo = split(kvts[u])
        kt_ref[u] = cat([hi[:64], lo[:64]], 0)
        vt_ref[u] = cat([hi[64:], lo[64:]], 0)
        qhi, qlo = split(qgs[u][:64] * heads)
        q_ref[u] = cat([qhi, qlo], 0)
        gate_ref[u] = jax.nn.sigmoid(qgs[u][64:])


def row_fwd_kernel(
    place_ref, k2_ref, vt_ref, q_ref, gate_ref, live_ref, own_ref, bias_ref, wo_ref,
    p_ref, o_ref, m1_ref, any_ref, c1_ref,
):
    s = pl.program_id(0)
    heads = head_mask(64, 256, 8, 32)
    wo = wo_ref[...]
    wo2 = cat([wo, wo], 0)
    seq = lax.broadcasted_iota(jnp.int32, (16, 128), 0)
    bias = cat([bias_ref[pl.ds(2 * at, 2)].reshape(32, 256) for at in res_order(place_ref)], 0)
    every = range(GROUP)
    alive, logit = [], []
    for u in every:
        pick = (seq == s * GROUP + u).astype(bf16)
        live = mm(live_ref[...], pick, TN)
        alive.append(live)
        k2 = k2_ref[u]
        qhi, qlo = q_ref[u, 0:64], q_ref[u, 64:128]
        logit.append(mm(k2, cat([qhi, qhi], 0)) + mm(k2[:, :64], qlo))
    outs = []
    for u in every:
        live = alive[u]
        logits = jnp.where(cat([live, live], 1) > 0, logit[u] + bias, NEG)
        e = jnp.exp(logits - jnp.max(logits, 0, keepdims=True))
        p = e * (1.0 / jnp.sum(e, 0, keepdims=True))
        p_ref[u] = p
        some = jnp.max(live, 0, keepdims=True)
        any_ref[u] = jnp.broadcast_to(cat([some, some], 1), (8, 256))
        phi, plo = split(p)
        vt = vt_ref[u]
        first = mm(vt, phi)
        outs.append((first[:64] + first[64:] + mm(vt[:64], plo)) * heads)
    for u in every:
        o_ref[u] = outs[u]
        ahi, alo = split(outs[u] * gate_ref[u])
        y = mm(cat([ahi, alo], 0), wo2, TN)
        own = own_ref[u].astype(f32)
        m1 = own[:, :64] + jnp.sum(y.reshape(8, 32, 64), 0)
        m1_ref[u] = m1
        c1_ref[:, 0, s * GROUP + u, :] = cat([m1[:16], m1[16:]], 1)
        lv = own[:, 64:]
        c1_ref[:, 1, s * GROUP + u, :] = cat([lv[:16], lv[16:]], 1)


def diag2(w):
    z = jnp.zeros_like(w)
    return cat([cat([w, z], 1), cat([z, w], 1)], 0)


def col_kernel(c1_ref, cw_ref, out_ref):
    x = c1_ref[:, 0].reshape(256, 128)
    live = c1_ref[:, 1].reshape(256, 128)
    halves = (head_mask(128, 128, 64, 64) * (1.0 / 64)).astype(bf16)
    center = x - mm3(x, halves)
    xn = center * lax.rsqrt(mm3(center * center, halves) + EPS)
    cw = cw_ref[...].astype(f32)
    wq = diag2(cw[:, 0:64]).astype(bf16)
    wk = diag2(cw[:, 64:128]).astype(bf16)
    wv = diag2(cw[:, 128:192]).astype(bf16)
    total = jnp.sum(live * xn, 0, keepdims=True)
    count = jnp.sum(live, 0, keepdims=True)
    mean = total / jnp.maximum(count, 1.0)
    colq = mm3(jnp.broadcast_to(mean, (8, 128)), wq)[0:1] * SCALE
    kt = mm2(xn, wk)
    vt = mm2(xn, wv)
    groups = head_mask(128, 128, 8, 8).astype(bf16)
    logits = jnp.where(live > 0, mm3(kt * colq, groups), NEG)
    peak = jnp.max(logits, 0, keepdims=True)
    e = jnp.exp(logits - peak)
    den = jnp.sum(e, 0, keepdims=True)
    w = e / den
    wv_ = w * vt
    attended = jnp.sum(wv_, 0, keepdims=True)
    khi, klo = split(kt)

    def by_key(z):
        zhi, zlo = split(z)
        full = mm(khi, zhi, TN) + mm(klo, zhi, TN) + mm(khi, zlo, TN)
        lane = lax.broadcasted_iota(jnp.int32, (8, 128), 1)
        return jnp.where(lane < 64, full[0:8], full[64:72])

    lt = live.T
    rows = [
        by_key(wv_), by_key(w), attended, peak, den, colq, count, count, count, count,
        lt[0:1, :128], lt[0:1, 128:], lt[64:65, :128], lt[64:65, 128:],
        count, count, count, count,
    ]
    block = cat(rows, 0)
    for k in range(16):
        out_ref[k] = block


def unpair(x):
    return cat([x[:, 0:64], x[:, 64:128]], 0)


def spread(v):
    return jnp.broadcast_to(v[None], (16, 32, 64)).reshape(512, 64)


def factor_kernel(m1_ref, c2_ref, own_ref, cw_ref, wv_ref, wt_ref, m2_ref, d_ref):
    m1 = m1_ref[...].reshape(512, 64)
    live = own_ref[...].reshape(512, 128)[:, 64:].astype(f32)
    attended = unpair(c2_ref[:, 16, :])
    xn, _ = norm_rows(m1)
    gate = jax.nn.sigmoid(mm2(xn, cw_ref[:, 192:256]))
    m2 = m1 + mm2(gate * spread(attended), wv_ref[...])
    m2_ref[...] = m2.reshape(16, 32, 64)
    xn2, _ = norm_rows(m2)
    lr = live * mm2(xn2, wt_ref[...])
    lr = lr.reshape(16, 32, 64)
    lr = cat([lr[:, :16], lr[:, 16:]], 2).astype(bf16)
    lt = [c2_ref[:, 24 + k, :].astype(bf16) for k in range(4)]
    for k in range(8):
        d_ref[k, 0:16] = lr
        for q in range(4):
            d_ref[k, 16 + q] = lt[q]


def masks_by_row(p):
    low = cat([p[:, 0], p[:, 1]], 2)
    high = cat([p[:, 2], p[:, 3]], 2)
    return cat([low, high], 1)


def outer_kernel(
    place_ref, da_ref, own_ref, cta_ref, ctb_ref, cta2_ref, ctb2_ref, w_ref, m2_ref, c2_ref, m1_ref,
    ownx_ref, adj_ref, cw_ref, wv_ref, wt_ref, g2_ref, dcg_ref, e1_ref,
    inv, turned, stage, res, lrs, wide, wf,
):
    step = pl.program_id(0)
    core = place_ref[0] % 2

    @pl.when(step == 0)
    def _():
        every = masks_by_row(da_ref[:, 16:20]).reshape(256, 256)
        mine = masks_by_row(own_ref[:, 16:20]).reshape(32, 256)
        value = 1.0 / jnp.maximum(mm(every, mine, NT), 1.0)
        for k in range(32):
            inv[k] = jnp.broadcast_to(value[:, k:k + 1], (256, 128))
        for s in range(16):
            piece = unpack(da_ref[:, s].astype(f32)).T
            for half in range(2):
                cols = piece[:, 128 * half:128 * half + 128]
                lrs[half, pl.ds(s, 32, stride=16), :] = cols[0:32]
                lrs[half, pl.ds(512 + s, 32, stride=16), :] = cols[32:64]
        for half in range(2):
            turned[0, :, 128 * half:128 * half + 128] = lrs[half, 512:1024].astype(bf16)
            turned[1, :, 128 * half:128 * half + 128] = lrs[half, 0:512].astype(bf16)
        wf[...] = w_ref[...].astype(f32)
        for k in range(32):
            first = wf[pl.ds(k, 32, stride=32), :].astype(bf16)
            second = w_ref[32 * k:32 * k + 32]
            for part in range(2):
                wide[0, :, 256 * k + 128 * part:256 * k + 128 * part + 128] = first
                wide[1, :, 256 * k + 128 * part:256 * k + 128 * part + 128] = second

    for side in range(2):
        for k in range(OWN_STEP):
            if side == 0:
                one = step * OWN_STEP + k
                x = cta_ref[:, 0, k].astype(f32)
                y = cta2_ref[:, 0, k].astype(f32)
                ct = cat([jnp.where(core == 0, x, y), jnp.where(core == 0, y, x)], 1)
            else:
                slot, at = k // (OWN_STEP // 2), k % (OWN_STEP // 2)
                one = (slot + core) % 2 * 16 + step * (OWN_STEP // 2) + at
                ct = (ctb_ref if slot == 0 else ctb2_ref)[:, 0, at].astype(f32)
            hi, lo = split(ct.reshape(256, 128) * inv[one])
            both = mm(turned[side], cat([hi, lo], 1))
            uhi, ulo = split(both[:, :128] + both[:, 128:])
            rows = pl.ds(pl.multiple_of(one * 16, 16), 16)
            for b in range(32):
                stage[side, rows, 256 * b:256 * b + 128] = uhi[16 * b:16 * b + 16]
                stage[side, rows, 256 * b + 128:256 * b + 256] = ulo[16 * b:16 * b + 16]

    @pl.when(step == 32 // OWN_STEP - 1)
    def _():
        grads = []
        for side in range(2):
            res[:, 0:32] = mm(stage[side], wide[side], NT)
            grads.append(cat([res[pl.ds(s, 32, stride=16), :] for s in range(16)], 0)[:, 0:32])
        lv = ownx_ref[...].reshape(512, 128)[:, 64:].astype(f32)
        dlr = cat(grads, 1) * lv
        m2 = m2_ref[...].reshape(512, 64)
        xn2, rstd2 = norm_rows(m2)
        adj = adj_ref[...].reshape(512, 64).astype(f32)
        g2 = adj + norm_back(xn2, rstd2, mm2(dlr, wt_ref[...], NT))
        g2_ref[...] = g2.reshape(16, 32, 64)
        xn, _ = norm_rows(m1_ref[...].reshape(512, 64))
        gate = jax.nn.sigmoid(mm2(xn, cw_ref[:, 192:256]))
        dmix = mm2(g2, wv_ref[...], NT)
        attended = spread(unpair(c2_ref[:, 16, :]))
        dcg_ref[...] = (dmix * attended * gate * (1.0 - gate)).reshape(16, 32, 64)
        da = jnp.sum((gate * dmix).reshape(16, 32, 64), 0)
        packed = cat([da[:16], da[16:]], 1)
        for k in range(16):
            e1_ref[k] = packed


def row_bwd_kernel(
    place_ref, e1_ref, c2_ref, m1_ref, own_ref, g2_ref, dcg_ref, cw_ref,
    p_ref, o_ref, v2_ref, gate_ref, any_ref, wo_ref,
    g1_ref, ds_ref, do_ref, dg_ref, bias_ref,
    g1s,
):
    s = pl.program_id(0)

    @pl.when(s == 0)
    def _():
        cw = cw_ref[...]
        groups = head_mask(64, 64, 8, 8).astype(bf16)
        da = jnp.sum(e1_ref[...], 0)
        da = unpair(da)
        attended = unpair(c2_ref[:, 16, :])
        peak = unpair(c2_ref[:, 17, :])
        den = unpair(c2_ref[:, 18, :])
        colq = unpair(c2_ref[:, 19, :])
        count = unpair(c2_ref[:, 20, :])
        delta = mm3(da * attended, groups)
        feature = lax.broadcasted_iota(jnp.int32, (32, 64), 1) % 8
        dq = jnp.zeros((32, 64), f32)
        for k in range(8):
            z = mm3(da * unpair(c2_ref[:, k, :]), groups) - delta * unpair(c2_ref[:, 8 + k, :])
            dq = dq + jnp.where(feature == k, z, 0.0)
        dtotal = mm2(dq * SCALE, cw[:, 0:64], NT) / jnp.maximum(count, 1.0)
        live = own_ref[...].reshape(512, 128)[:, 64:].astype(f32)
        xn, rstd = norm_rows(m1_ref[...].reshape(512, 64))
        kt = mm2(xn, cw[:, 64:128])
        vt = mm2(xn, cw[:, 128:192])
        qs = spread(colq)
        logits = jnp.where(live > 0, mm3(kt * qs, groups), NEG)
        weights = jnp.exp(logits - spread(peak)) / spread(den)
        das = spread(da)
        dl = weights * (mm2(vt * das, groups) - spread(delta)) * live
        dxn = (
            mm2(dcg_ref[...].reshape(512, 64), cw[:, 192:256], NT)
            + mm2(dl * qs, cw[:, 64:128], NT)
            + mm2(weights * das, cw[:, 128:192], NT)
            + live * spread(dtotal)
        )
        g1 = g2_ref[...].reshape(512, 64) + norm_back(xn, rstd, dxn)
        g1s[...] = g1.reshape(16, 32, 64)
        bias_ref[...] = jnp.zeros_like(bias_ref)

    heads = head_mask(64, 256, 8, 32)
    wo = wo_ref[...]
    wo2 = cat([wo, wo], 1)
    every = range(GROUP)
    douts = []
    for u in every:
        dm = g1s[s * GROUP + u]
        g1_ref[u] = dm
        douts.append(mm(wo2, cat([pair2(dm)] * 8, 0), NT))
    dos, deltas, dps = [], [], []
    for u in every:
        o = o_ref[u]
        gate = gate_ref[u]
        hi, lo = split(douts[u] * o * gate * (1.0 - gate))
        dg_ref[u] = cat([hi, lo], 0)
        do = douts[u] * gate * heads
        hi, lo = split(do)
        do_ref[u] = cat([hi, lo], 0)
        do_live = do * any_ref[u, 0:1, :]
        dos.append(do_live)
        deltas.append(jnp.sum(do_live * o, 0, keepdims=True))
    for u in every:
        v2 = v2_ref[u]
        lhi, llo = split(dos[u])
        dps.append(mm(v2, cat([lhi, lhi], 0)) + mm(v2[:, :64], llo))
    total = jnp.zeros((256, 256), f32)
    for u in every:
        ds = p_ref[u] * (dps[u] - deltas[u])
        total = total + ds
        ds_ref[u] = ds
    for k, at in enumerate(res_order(place_ref)):
        bias_ref[pl.ds(2 * at, 2)] += total[32 * k:32 * k + 32].reshape(2, 16, 256)


def row_inputs_kernel(
    place_ref, p_ref, ds_ref, do_ref, dg_ref, q_ref, kt_ref, win_ref, dxo_ref, f_ref, wback, wown
):
    @pl.when(pl.program_id(0) == 0)
    def _():
        wt = win_ref[...].astype(f32).T
        qg = cat([wt[0:64], wt[192:256]], 0)
        wback[...] = cat([wt[64:128], wt[64:128], wt[128:192], wt[128:192]], 0).astype(bf16)
        wown[...] = cat([qg, qg], 0).astype(bf16)

    heads = head_mask(64, 256, 8, 32) * SCALE
    zero = jnp.zeros((64, 256), bf16)
    every = range(GROUP)
    dqs, dks, dvs = [], [], []
    for u in every:
        shi, slo = split(ds_ref[u])
        kt = kt_ref[u]
        q = q_ref[u]
        first = mm(kt, shi)
        dqs.append((first[:64] + first[64:] + mm(kt[:64], slo)) * heads)
        dks.append(mm(shi, q, NT) + mm(slo, cat([q[:64], zero], 0), NT))
    for u in every:
        do = do_ref[u]
        phi, plo = split(p_ref[u])
        dvs.append(mm(phi, do, NT) + mm(plo, cat([do[:64], zero], 0), NT))
    dxs = [mm2(cat([dks[u], dvs[u]], 1), wback[...]).reshape(8, 32, 64) for u in every]
    dxos = []
    for u in every:
        dg = dg_ref[u]
        qhi, qlo = split(dqs[u])
        dxos.append(mm(cat([qhi, dg[:64], qlo, dg[64:]], 0), wown[...], TN))
    order = res_order(place_ref)
    for u in every:
        dense = cat([dxs[u][:, :16], dxs[u][:, 16:]], 2)
        for k, at in enumerate(order):
            f_ref[at, u] = dense[k]
        dxo_ref[u] = jnp.sum(dxos[u].reshape(8, 32, 64), 0)


def final_rows_kernel(f_ref, dxo_ref, g1_ref, own_ref, out_ref):
    total = jnp.sum(f_ref[...], 0)
    total = cat([total[:, :, :64], total[:, :, 64:]], 1).reshape(512, 64)
    total = total + dxo_ref[...].reshape(512, 64)
    xn, rstd = norm_rows(own_ref[...].reshape(512, 128)[:, :64].astype(f32))
    out = g1_ref[...].reshape(512, 64) + norm_back(xn, rstd, total)
    out_ref[...] = out.reshape(16, 32, 64)


def final_pair_kernel(b_ref, pair_ref, wb_ref, ct_ref, out_ref, scr):
    total = jnp.sum(b_ref[...], 0)
    w2 = cat([wb_ref[...], wb_ref[...]], 0)
    own = head_mask(8, 256, 1, 32)
    for j in range(16):
        wide = jnp.broadcast_to(total[j:j + 1, :], (8, 256)) * own
        hi, lo = split(wide)
        y = mm(cat([hi, lo], 0), w2, TN)
        scr[:, j, :] = jnp.sum(y.reshape(8, 32, 128), 0)
    xn, rstd = norm_rows(pair_ref[...].reshape(512, 128).astype(f32))
    out = norm_back(xn, rstd, scr[...].reshape(512, 128)) + ct_ref[...].reshape(512, 128).astype(f32)
    out_ref[...] = out.reshape(32, 16, 128)


def sds(shape, dtype=f32):
    return jax.ShapeDtypeStruct(shape, dtype)


def far(shape, dtype=f32):
    return pltpu.HBM(shape, dtype)


def full(shape):
    zeros = (0,) * len(shape)
    return pl.BlockSpec(shape, lambda s: zeros)


def row(shape):
    rest = (0,) * (len(shape) - 1)
    return pl.BlockSpec((GROUP,) + shape[1:], lambda s: (s,) + rest)


def whole_call(kernel, out_shape, *args, scratch=()):
    return pl.pallas_call(
        kernel, out_shape=out_shape, scratch_shapes=list(scratch), compiler_params=VMEM
    )(*args)


def project(rows, own, win):
    return pl.pallas_call(
        proj_kernel,
        grid=(16 // GROUP,),
        in_specs=[
            *[row((17, 16, 128)) for _ in range(8)],
            *[pl.BlockSpec((1, 16, 128), lambda s: (16, 0, 0)) for _ in range(8)],
            row((16, 32, 128)), full((64, 256)),
        ],
        out_specs=[
            row((16, 256, 128)), row((16, 256, 128)), row((16, 128, 256)), row((16, 128, 256)),
            row((16, 128, 256)), row((16, 64, 256)), full((16, 256)),
        ],
        out_shape=[
            sds((16, 256, 128), bf16), far((16, 256, 128), bf16), far((16, 128, 256), bf16),
            sds((16, 128, 256), bf16), sds((16, 128, 256), bf16), sds((16, 64, 256)),
            sds((16, 256), bf16),
        ],
        scratch_shapes=[
            pltpu.VMEM((128, 128), bf16), pltpu.VMEM((128, 128), bf16),
            pltpu.VMEM((128, 128), bf16), pltpu.VMEM((128, 128), bf16),
        ],
        compiler_params=VMEM,
    )(*rows, *rows, own, win)


def row_forward(place, k2, vt, q, gate, live, own, bias, wo):
    return pl.pallas_call(
        row_fwd_kernel,
        grid=(16 // GROUP,),
        in_specs=[
            SMEM, row((16, 256, 128)), row((16, 128, 256)), row((16, 128, 256)), row((16, 64, 256)),
            full((16, 256)), row((16, 32, 128)), full((16, 16, 256)), full((64, 64)),
        ],
        out_specs=[
            row((16, 256, 256)), row((16, 64, 256)), row((16, 32, 64)), row((16, 8, 256)),
            full((16, 2, 16, 128)),
        ],
        out_shape=[
            far((16, 256, 256)), far((16, 64, 256)), sds((16, 32, 64)), sds((16, 8, 256)),
            sds((16, 2, 16, 128)),
        ],
        compiler_params=VMEM,
    )(place, k2, vt, q, gate, live, own, bias, wo)


def outer_product(place, ct, ct2, factors, dblock, w, m2, c2, m1, own, adj, cw, wvo, wtf):
    half = OWN_STEP // 2
    one = pl.BlockSpec((8, 1, OWN_STEP, 16, 128), lambda s: (0, 0, s, 0, 0))
    two = pl.BlockSpec((8, 1, half, 32, 128), lambda s: (0, 1, s, 0, 0))
    return pl.pallas_call(
        outer_kernel,
        grid=(32 // OWN_STEP,),
        in_specs=[
            SMEM,
            full((8, 20, 16, 128)),
            pl.BlockSpec((1, 20, 16, 128), lambda s: (0, 0, 0, 0)),
            one, two, one, two,
            full((1024, 128)),
            full((16, 32, 64)), full((16, 32, 128)), full((16, 32, 64)), full((16, 32, 128)),
            full((16, 32, 64)), full((64, 256)), full((64, 64)), full((64, 64)),
        ],
        out_specs=[full((16, 32, 64)), full((16, 32, 64)), full((16, 16, 128))],
        out_shape=[sds((16, 32, 64)), sds((16, 32, 64)), sds((16, 16, 128))],
        scratch_shapes=[
            pltpu.VMEM((32, 256, 128), f32),
            pltpu.VMEM((2, 512, 256), bf16),
            pltpu.VMEM((2, 512, 8192), bf16),
            pltpu.VMEM((512, 128), f32),
            pltpu.VMEM((2, 1024, 128), f32),
            pltpu.VMEM((2, 32, 8192), bf16),
            pltpu.VMEM((1024, 128), f32),
        ],
        compiler_params=VMEM,
    )(
        place, factors, dblock, ct.reshape(8, 2, 32, 16, 128), ct.reshape(8, 2, 16, 32, 128),
        ct2.reshape(8, 2, 32, 16, 128), ct2.reshape(8, 2, 16, 32, 128), w, m2, c2, m1, own, adj,
        cw, wvo, wtf,
    )


def row_backward(place, e1, c2, m1, own, g2, dcg, cw, p, o, v2, gate, any_live, wo):
    return pl.pallas_call(
        row_bwd_kernel,
        grid=(16 // GROUP,),
        in_specs=[
            SMEM, full((16, 16, 128)), full((16, 32, 128)), full((16, 32, 64)), full((16, 32, 128)),
            full((16, 32, 64)), full((16, 32, 64)), full((64, 256)),
            row((16, 256, 256)), row((16, 64, 256)), row((16, 256, 128)), row((16, 64, 256)),
            row((16, 8, 256)), full((64, 64)),
        ],
        out_specs=[
            row((16, 32, 64)), row((16, 256, 256)), row((16, 128, 256)), row((16, 128, 256)),
            full((16, 16, 256)),
        ],
        out_shape=[
            sds((16, 32, 64)), far((16, 256, 256)), sds((16, 128, 256), bf16),
            sds((16, 128, 256), bf16), sds((16, 16, 256)),
        ],
        scratch_shapes=[pltpu.VMEM((16, 32, 64), f32)],
        compiler_params=SMALL,
    )(place, e1, c2, m1, own, g2, dcg, cw, p, o, v2, gate, any_live, wo)


def row_inputs(place, p, ds, do, dg, q, kt, win):
    return pl.pallas_call(
        row_inputs_kernel,
        grid=(16 // GROUP,),
        in_specs=[
            SMEM, row((16, 256, 256)), row((16, 256, 256)), row((16, 128, 256)), row((16, 128, 256)),
            row((16, 128, 256)), row((16, 128, 256)), full((64, 256)),
        ],
        out_specs=[row((16, 32, 64)), pl.BlockSpec((8, GROUP, 16, 128), lambda s: (0, s, 0, 0))],
        out_shape=[sds((16, 32, 64)), sds((8, 16, 16, 128))],
        scratch_shapes=[pltpu.VMEM((256, 64), bf16), pltpu.VMEM((256, 64), bf16)],
        compiler_params=SMALL,
    )(place, p, ds, do, dg, q, kt, win)


def body(
    alignment_state,
    pairwise_state,
    alignment_mask,
    residue_entry_mask,
    sequence_live_count,
    horizontal_intake_coefs,
    pairwise_bias_weights,
    horizontal_readout_coefs,
    column_input_weights,
    vertical_readout_coefs,
    tensor_factor_coefs,
    outer_output_weights,
    adjoint_of_result_track,
    pairwise_cotangent,
):
    place = jnp.stack([lax.axis_index("depth"), lax.axis_index("res")]).astype(jnp.int32)
    hbm = pl.BlockSpec(memory_space=pltpu.HBM)
    heads_first = pairwise_bias_weights.T
    bias_block, row_block, own, turned = pl.pallas_call(
        prepare_kernel,
        in_specs=[hbm] * 6 + [SMEM],
        out_shape=[
            sds((16, 16, 256)), sds((17, 16, 128), bf16), sds((16, 32, 128), bf16),
            sds((16, 32, 128), bf16),
        ],
        scratch_shapes=[
            pltpu.VMEM((2, 32, 16, 128), f32), pltpu.VMEM((32, 16, 128), bf16),
            pltpu.VMEM((8, 128), bf16), pltpu.VMEM((32, 16, 128), bf16),
            pltpu.VMEM((16, 32, 64), bf16), pltpu.VMEM((16, 32), jnp.int32),
            pltpu.VMEM((1, 32), jnp.int32), pltpu.SemaphoreType.DMA((6,)),
        ],
        compiler_params=LARGE,
    )(
        pairwise_state, heads_first, pairwise_cotangent, alignment_state,
        alignment_mask, residue_entry_mask.reshape(1, 32), sequence_live_count,
    )
    rows = [row_block] + [
        lax.ppermute(row_block, "res", [(r, r ^ k) for r in range(8)]) for k in range(1, 8)
    ]
    cw = cat(
        [
            column_input_weights[:, :64],
            jnp.tile(column_input_weights[:, 64:72], (1, 8)),
            jnp.tile(column_input_weights[:, 72:80], (1, 8)),
            column_input_weights[:, 80:],
        ],
        1,
    )

    perm = [(d * 8 + r, (2 * r + d % 2) * 8 + d // 2) for d in range(16) for r in range(8)]
    turned = lax.ppermute(turned, ("depth", "res"), perm)
    both = whole_call(turn_kernel, sds((8, 1024, 128), bf16), pairwise_cotangent, turned)

    bias = lax.all_to_all(bias_block, "depth", 0, 0)
    bias, both, *rows = lax.optimization_barrier((bias, both, *rows))
    k2, v2, kt, vt, q, gate, live = project(rows, own, horizontal_intake_coefs)
    same_core = [[c + 2 * k for k in range(8)] for c in range(2)]
    ct = lax.all_to_all(both, "depth", 0, 0, axis_index_groups=same_core)
    p, o, m1, any_live, c1 = row_forward(
        place, k2, vt, q, gate, live, own, bias, horizontal_readout_coefs
    )
    c1, ct = lax.optimization_barrier((c1, ct))
    ct2 = lax.ppermute(ct, "depth", [(d, d ^ 1) for d in range(16)])
    c1 = lax.all_to_all(c1, "depth", 0, 0)
    c2 = whole_call(col_kernel, sds((16, 32, 128)), c1, cw)
    c2 = lax.all_to_all(c2, "depth", 0, 0)
    m2, dblock = whole_call(
        factor_kernel, [sds((16, 32, 64)), sds((8, 20, 16, 128), bf16)],
        m1, c2, own, cw, vertical_readout_coefs, tensor_factor_coefs,
    )
    factors = lax.all_to_all(dblock, "res", 0, 0)
    g2, dcg, e1 = outer_product(
        place, ct, ct2, factors, dblock, outer_output_weights, m2, c2, m1, own,
        adjoint_of_result_track, cw, vertical_readout_coefs, tensor_factor_coefs,
    )
    e1 = lax.all_to_all(e1, "depth", 0, 0)
    g1, ds, do, dg, bblock = row_backward(
        place, e1, c2, m1, own, g2, dcg, cw, p, o, v2, gate, any_live, horizontal_readout_coefs
    )
    bsum = lax.all_to_all(bblock, "depth", 0, 0)
    dxo, fblock = row_inputs(place, p, ds, do, dg, q, kt, horizontal_intake_coefs)
    fblock, bsum = lax.optimization_barrier((fblock, bsum))
    fsum = lax.all_to_all(fblock, "res", 0, 0)
    alignment_gradient = whole_call(final_rows_kernel, sds((16, 32, 64)), fsum, dxo, g1, own)
    pair_grad = whole_call(
        final_pair_kernel, sds((32, 16, 128)), bsum, pairwise_state, heads_first,
        pairwise_cotangent, scratch=[pltpu.VMEM((32, 16, 128), f32)],
    )
    return alignment_gradient, pair_grad


def solution(mesh):
    in_specs = (
        P("depth", "res", None),
        P("res", "depth", None),
        P("depth", "res"),
        P("res"),
        P("depth"),
        P(),
        P(),
        P(),
        P(),
        P(),
        P(),
        P(),
        P("depth", "res", None),
        P("res", "depth", None),
    )
    out_specs = (P("depth", "res", None), P("res", "depth", None))
    return jax.shard_map(body, mesh=mesh, in_specs=in_specs, out_specs=out_specs, check_vma=False)
```
